32 devices in a mesh: wide: 8 (over z, core), narrow: 4 (over y, x).
Axes of the slice: x: 2, y: 2, z: 4, core: 2. Of those that a mesh axis runs over, the one named last changes fastest.
Arguments:
- tokens: bfloat16 [32, 12, 84, 768], P(('wide', 'narrow')), may hold values from -6 to 6
- condition: float32 [32, 768], P(('wide', 'narrow')), may hold values from -6 to 6
- timesteps: int32 [32], P(('wide', 'narrow')), may hold values from 0 to 999, as said below
- loss_codes: int32 [32], P(('wide', 'narrow')), may hold values from 0 to 3
- out_grad: bfloat16 [32, 12, 84, 768], P(('wide', 'narrow')), may hold values from -6 to 6
- mod_weight: bfloat16 [768, 4608], P(('wide', 'narrow')), may hold values from -0.21875 to 0.21875
- mod_bias: bfloat16 [4608], P(('wide', 'narrow')), may hold values from -3 to 3
- qkv_weight: bfloat16 [768, 2304], P(('wide', 'narrow')), may hold values from -0.21875 to 0.21875
- qv_bias: bfloat16 [1536], P(('wide', 'narrow')), may hold values from -3 to 3
- proj_weight: bfloat16 [768, 768], P(('wide', 'narrow')), may hold values from -0.625 to 0.625
- proj_bias: bfloat16 [768], P(('wide', 'narrow')), may hold values from -3 to 3
- up_weight: bfloat16 [768, 3072], P(('wide', 'narrow')), may hold values from -0.21875 to 0.21875
- up_bias: bfloat16 [3072], P(('wide', 'narrow')), may hold values from -3 to 3
- down_weight: bfloat16 [3072, 768], P(('wide', 'narrow')), may hold values from -0.109375 to 0.109375
- down_bias: bfloat16 [768], P(('wide', 'narrow')), may hold values from -3 to 3
Outputs:
- block_output: bfloat16 [32, 12, 84, 768], P(('wide', 'narrow'))
- tokens_grad: bfloat16 [32, 12, 84, 768], P(('wide', 'narrow'))
- condition_grad: float32 [32, 768], P(('wide', 'narrow'))
- mod_weight_grad: float32 [768, 4608], P(('wide', 'narrow'))
- mod_bias_grad: float32 [4608], P(('wide', 'narrow'))
- qkv_weight_grad: float32 [768, 2304], P(('wide', 'narrow'))
- qv_bias_grad: float32 [1536], P(('wide', 'narrow'))
- proj_weight_grad: float32 [768, 768], P(('wide', 'narrow'))
- proj_bias_grad: float32 [768], P(('wide', 'narrow'))
- up_weight_grad: float32 [768, 3072], P(('wide', 'narrow'))
- up_bias_grad: float32 [3072], P(('wide', 'narrow'))
- down_weight_grad: float32 [3072, 768], P(('wide', 'narrow'))
- down_bias_grad: float32 [768], P(('wide', 'narrow'))
The draws below stay inside these ranges and needn't reach their ends.
Inputs may be any that keep to these rules, and one draw needn't show every extreme that they name: timesteps lean toward high noise.
All inputs are finite; a program needn't handle non-finite values.
Results may differ from the reference program's by a relative error of at most 0.017.
The reference program's roundings to bfloat16 on the way count: a program that leaves them out, or rounds other values in their place, can miss the bound.
Values may be sent and summed in bfloat16 or wider, within the bound.
A program may use at most 256 MiB of HBM per device.

```python
import math
import jax
import jax.numpy as jnp
from jax import lax

D = 768
HEAD_DIM = 64
FF = 3072
FRAMES = 12
PATCHES = 84
TSTEPS = 1000
CLIPS = 32


def draw_timesteps(key, part):
    key = jax.random.fold_in(key, 11)
    first_key, second_key = jax.random.split(key)
    first_draw = jax.random.randint(first_key, (CLIPS,), 0, TSTEPS)
    second_draw = jax.random.randint(second_key, (CLIPS,), 0, TSTEPS)
    return jnp.maximum(first_draw, second_draw).astype(jnp.int32)


def place_ends(entries, key, low, high):
    place = [jax.random.randint(jax.random.fold_in(key, axis), (), 0, length) for axis, length in enumerate(entries.shape)]
    widest = entries.shape.index(max(entries.shape))
    next_to = place[:widest] + [(place[widest] + 1) % entries.shape[widest]] + place[widest + 1:]
    return entries.at[tuple(place)].set(low).at[tuple(next_to)].set(high)


def steps_of(rng, dims, cuts, low, largest):
    def one(axis_at, parts):
        draws = jax.random.uniform(jax.random.fold_in(jax.random.fold_in(rng, 6), axis_at), (parts,), jnp.float32, low / len(cuts), largest / len(cuts))
        return jnp.repeat(jnp.exp(draws), dims[axis_at] // parts).reshape((-1,) + (1,) * (len(dims) - axis_at - 1))

    loudness = one(*cuts[0])
    for cut in cuts[1:]:
        loudness = loudness * one(*cut)
    return loudness


def scatter_about(rng, shape, scale, most, cuts=(), held_as=jnp.bfloat16):
    values = scale * jax.random.normal(rng, shape, jnp.float32)
    if cuts:
        values = values * steps_of(rng, shape, cuts, -0.22, 0.18)
    return jnp.clip(values, -most, most).astype(held_as)


def setup_inputs(seed: int = 0) -> dict:
    seeds = jax.random.split(jax.random.key(seed), 16)
    return {
        "tokens": scatter_about(seeds[0], (CLIPS, FRAMES, PATCHES, D), 1.0, 6.0, ((0, 32),)),
        "condition": scatter_about(seeds[1], (CLIPS, D), 1.0, 6.0, ((0, 32),), jnp.float32),
        "timesteps": draw_timesteps(jax.random.fold_in(seeds[15], 71), 0),
        "loss_codes": place_ends(jax.random.randint(seeds[3], (CLIPS,), 0, 4), jax.random.fold_in(seeds[3], 1), 0, 3).astype(jnp.int32),
        "out_grad": scatter_about(seeds[4], (CLIPS, FRAMES, PATCHES, D), 1.0, 6.0, ((0, 32),)),
        "mod_weight": scatter_about(seeds[5], (D, 6 * D), D ** -0.5, 0.21875, ((0, 32),)),
        "mod_bias": scatter_about(seeds[6], (6 * D,), 0.5, 3.0, ((0, 32),)),
        "qkv_weight": scatter_about(seeds[7], (D, 3 * D), D ** -0.5, 0.21875, ((0, 32),)),
        "qv_bias": scatter_about(seeds[8], (2 * D,), 0.5, 3.0, ((0, 32),)),
        "proj_weight": scatter_about(seeds[9], (D, D), (D // 8) ** -0.5, 0.625, ((0, 32),)),
        "proj_bias": scatter_about(seeds[10], (D,), 0.5, 3.0, ((0, 32),)),
        "up_weight": scatter_about(seeds[11], (D, FF), D ** -0.5, 0.21875, ((0, 32),)),
        "up_bias": scatter_about(seeds[12], (FF,), 0.5, 3.0, ((0, 32),)),
        "down_weight": scatter_about(seeds[13], (FF, D), FF ** -0.5, 0.109375, ((0, 32),)),
        "down_bias": scatter_about(seeds[14], (D,), 0.5, 3.0, ((0, 32),)),
    }


@jax.custom_vjp
def low(v):
    return lax.optimization_barrier(v.astype(jnp.bfloat16)).astype(jnp.float32)

@jax.custom_vjp
def low_back(v):
    return v

def low_keep(v):
    return (low(v), None)

def low_pass(kept, grad):
    return (grad,)

def back_keep(v):
    return (v, None)

def back_low(kept, grad):
    return (low(grad),)
low.defvjp(low_keep, low_pass)
low_back.defvjp(back_keep, back_low)
highest = lax.Precision.HIGHEST

def matmul(left_side, right_side):
    return jnp.dot(left_side, right_side, precision=highest, preferred_element_type=jnp.float32)

def rounded(inputs):
    return low(low_back(inputs))

def layernorm(inputs):
    center = inputs - lax.optimization_barrier(jnp.mean(inputs, axis=-1, keepdims=True))
    spread = lax.optimization_barrier(jnp.mean(center * center, axis=-1, keepdims=True))
    return center * lax.rsqrt(spread + 1e-06)

def modulate(inputs, shift_part, scale_part):
    return layernorm(inputs) * (1.0 + scale_part) + shift_part

def softmax_last(scores):
    return jax.nn.softmax(scores, axis=-1)

def time_embed(noise_steps, model_width):
    half_width = model_width // 2
    frequency = jnp.exp(-math.log(10000.0) * jnp.arange(half_width, dtype=jnp.float32) / half_width)
    angles = noise_steps.astype(jnp.float32)[:, None] * frequency[None, :]
    return jnp.concatenate([jnp.cos(angles), jnp.sin(angles)], axis=-1)

def clip_forward(clip_tokens, conditioning, params):
    mod_full, modb_full, qkv_full, qvb_full, proj_full, projb_full, up_full, upb_full, down_full, downb_full = params
    frames, patches, model_width = clip_tokens.shape
    head_count = model_width // HEAD_DIM
    gated = low(jax.nn.silu(conditioning))
    modulation = low_back(matmul(gated[None, :], mod_full)[0] + modb_full)
    shift_first, scale_first, gate_first, shift_second, scale_second, gate_second = jnp.split(modulation, 6)
    token_rows = clip_tokens.reshape(frames * patches, model_width)
    normed = low(modulate(token_rows, shift_first, scale_first))
    projected = matmul(normed, qkv_full)
    shape_four = (frames, patches, head_count, HEAD_DIM)
    queries = rounded(projected[:, :model_width] + qvb_full[:model_width]).reshape(shape_four)
    keys_all = rounded(projected[:, model_width:2 * model_width]).reshape(shape_four)
    values_all = rounded(projected[:, 2 * model_width:] + qvb_full[model_width:]).reshape(shape_four)
    scores = low_back(jnp.einsum('fphd,gphd->phfg', queries, keys_all, precision=highest) * HEAD_DIM ** (-0.5))
    softened = low(softmax_last(scores))
    attended = rounded(jnp.einsum('phfg,gphd->fphd', softened, values_all, precision=highest).reshape(frames * patches, model_width))
    branch_first = low_back(matmul(attended, proj_full) + projb_full)
    middle = token_rows + gate_first * branch_first
    normed_second = low(modulate(middle, shift_second, scale_second))
    hidden = low_back(matmul(normed_second, up_full) + upb_full)
    activated = low(jax.nn.gelu(hidden, approximate=True))
    branch_second = low_back(matmul(activated, down_full) + downb_full)
    result = middle + gate_second * branch_second
    return result.reshape(frames, patches, model_width)

def reference(tokens, condition, timesteps, loss_codes, out_grad, mod_weight, mod_bias, qkv_weight, qv_bias, proj_weight, proj_bias, up_weight, up_bias, down_weight, down_bias):
    params = tuple((array.astype(jnp.float32) for array in (mod_weight, mod_bias, qkv_weight, qv_bias, proj_weight, proj_bias, up_weight, up_bias, down_weight, down_bias)))
    conditioning = condition.astype(jnp.float32) + time_embed(timesteps, D)
    clip_weight = (loss_codes.astype(jnp.float32) + 1.0) * 0.25
    cotangent = out_grad.astype(jnp.float32) * clip_weight[:, None, None, None]

    def one_clip(totals, clip_item):
        clip_tokens, clip_cond, clip_cot = clip_item
        result, pullback = jax.vjp(clip_forward, clip_tokens, clip_cond, params)
        grad_tokens, grad_cond, grad_params = pullback(clip_cot)
        totals = jax.tree.map(jnp.add, totals, grad_params)
        return (totals, (result.astype(jnp.bfloat16), grad_tokens.astype(jnp.bfloat16), grad_cond))
    zeros = jax.tree.map(jnp.zeros_like, params)
    totals, (outputs, tokens_grad, condition_grad) = lax.scan(one_clip, zeros, (tokens.astype(jnp.float32), conditioning, cotangent))
    return (outputs, tokens_grad, condition_grad, totals[0], totals[1], totals[2], totals[3], totals[4], totals[5], totals[6], totals[7], totals[8], totals[9])
```

```python
import math

import jax
import jax.numpy as jnp
from jax import lax
from jax.experimental import pallas as pl
from jax.experimental.pallas import tpu as pltpu
from jax.sharding import PartitionSpec as P

HEAD_DIM = 64
VMEM_LIMIT = 63 * 2**20


BF = jnp.bfloat16
F32 = jnp.float32
MESH = pl.DeviceIdType.MESH
ANY = pl.BlockSpec(memory_space=pl.ANY)
VMEM = pl.BlockSpec(memory_space=pltpu.VMEM)
BLOCKS = 12
SHARD = 48 * BLOCKS
SMALL = SHARD + 16
HALF = 384
GROUP = 96


def mm(a, b):
    return jnp.dot(a, b, preferred_element_type=F32)


def mm_nt(a, b):
    return lax.dot_general(a, b, (((1,), (1,)), ((), ())), preferred_element_type=F32)


def mm_tn(a, b):
    return lax.dot_general(a, b, (((0,), (0,)), ((), ())), preferred_element_type=F32)


class Place:
    def __init__(self):
        wide = lax.axis_index("wide")
        narrow = lax.axis_index("narrow")
        self.z, self.c = wide // 2, wide % 2
        self.y, self.x = narrow // 2, narrow % 2
        self.me = wide * 4 + narrow

    def dev(self, z=None, c=None, y=None, x=None):
        z = self.z if z is None else z
        c = self.c if c is None else c
        y = self.y if y is None else y
        x = self.x if x is None else x
        return (z * 2 + c, y * 2 + x)

    def peers(self):
        column = [self.dev(z=(self.z + i) % 4) for i in (1, 2, 3)]
        plane = [self.dev(x=1 - self.x), self.dev(y=1 - self.y), self.dev(y=1 - self.y, x=1 - self.x)]
        return column, plane, self.dev(c=1 - self.c)

    def greet(self):
        bar = pltpu.get_barrier_semaphore()
        column, plane, sibling = self.peers()
        for target in column + plane + [sibling]:
            pl.semaphore_signal(bar, inc=1, device_id=target, device_id_type=MESH)
        pl.semaphore_wait(bar, 7)


def when(cond, act):
    pl.when(cond)(act)


class Gather:
    def __init__(self, place, buf, ssem, rsem, k, rows):
        self.p, self.buf, self.ssem, self.rsem, self.k, self.rows = place, buf, ssem, rsem, k, rows

    def copy(self, i, idx, dev):
        ref = self.buf.at[idx + (self.rows, slice(None))]
        return pltpu.make_async_remote_copy(
            ref, ref, self.ssem.at[self.k, i], self.rsem.at[self.k, i], device_id=dev, device_id_type=MESH
        )

    def up(self, h, op):
        p = self.p
        if op == "recv":
            when(p.z >= h, lambda: self.copy(h - 1, (p.z - h, p.c, p.y, p.x), p.dev(x=1 - p.x)).wait_recv())
            return
        cp = lambda: self.copy(h - 1, (p.z - (h - 1), p.c, p.y, p.x), p.dev(z=p.z + 1))
        when((p.z <= 2) & (p.z >= h - 1), (lambda: cp().start()) if op == "start" else (lambda: cp().wait_send()))

    def down(self, h, op):
        p = self.p
        if op == "recv":
            when(p.z + h <= 3, lambda: self.copy(h + 2, (p.z + h, p.c, p.y, p.x), p.dev(x=1 - p.x)).wait_recv())
            return
        cp = lambda: self.copy(h + 2, (p.z + (h - 1), p.c, p.y, p.x), p.dev(z=p.z - 1))
        when((p.z >= 1) & (p.z + (h - 1) <= 3), (lambda: cp().start()) if op == "start" else (lambda: cp().wait_send()))

    def plane(self):
        p = self.p
        low, high, every = pl.ds(0, 2), pl.ds(2, 2), slice(None)
        return (
            ((low, p.c, p.y, p.x), p.dev(x=1 - p.x), (low, p.c, p.y, 1 - p.x)),
            ((high, p.c, p.y, p.x), p.dev(y=1 - p.y), (high, p.c, 1 - p.y, p.x)),
            ((low, p.c, p.y, every), p.dev(y=1 - p.y), (low, p.c, 1 - p.y, every)),
            ((high, p.c, every, p.x), p.dev(x=1 - p.x), (high, p.c, every, 1 - p.x)),
            ((every, p.c, every, every), p.dev(c=1 - p.c), (every, 1 - p.c, every, every)),
        )

    def step(self, s):
        if 1 <= s <= 3:
            self.up(s, "recv")
            if s < 3:
                self.up(s + 1, "start")
            self.down(s, "recv")
            if s < 3:
                self.down(s + 1, "start")
        if s == 0:
            self.up(1, "start")
            self.down(1, "start")
        table = self.plane()
        starts = {3: (0, 1), 4: (2, 3), 5: (4,)}.get(s, ())
        recvs = {4: (0, 1), 5: (2, 3), 6: (4,)}.get(s, ())
        for i in recvs:
            self.copy(6 + i, table[i][2], table[i][1]).wait_recv()
        for i in starts:
            self.copy(6 + i, table[i][0], table[i][1]).start()

    def finish(self):
        for h in (1, 2, 3):
            self.up(h, "sent")
            self.down(h, "sent")
        for i, row in enumerate(self.plane()):
            self.copy(6 + i, row[0], row[1]).wait_send()


class Reduce:
    def __init__(self, place, buf, land, ssem, rsem, k, rows, final):
        self.p, self.buf, self.land, self.ssem, self.rsem, self.k, self.rows = place, buf, land, ssem, rsem, k, rows
        self.final = final

    def copy(self, i, idx, land, lidx, dev):
        tail = (self.rows, slice(None))
        return pltpu.make_async_remote_copy(
            self.buf.at[idx + tail], land.at[lidx + tail], self.ssem.at[self.k, i], self.rsem.at[self.k, i],
            device_id=dev, device_id_type=MESH,
        )

    def table(self):
        p = self.p
        low, high, every = pl.ds(0, 2), pl.ds(2, 2), slice(None)
        core, a2, b2, a1, b1, zd, zu = self.land
        return (
            ((every, 1 - p.c, every, every), core, (every, every, every), p.dev(c=1 - p.c)),
            ((low, p.c, 1 - p.y, every), a2, (every, every), p.dev(y=1 - p.y)),
            ((high, p.c, every, 1 - p.x), b2, (every, every), p.dev(x=1 - p.x)),
            ((low, p.c, p.y, 1 - p.x), a1, (every,), p.dev(x=1 - p.x)),
            ((high, p.c, 1 - p.y, p.x), b1, (every,), p.dev(y=1 - p.y)),
        )

    def add(self, idx, land, lidx):
        tail = (self.rows, slice(None))
        self.buf[idx + tail] = self.buf[idx + tail] + land[lidx + tail]

    def down(self, t, op):
        p, zd = self.p, self.land[5]
        if op == "recv":
            def take():
                self.copy(4 + t, (p.z - 3 + t, p.c, p.y, p.x), zd, (t - 1,), p.dev(x=1 - p.x)).wait_recv()
                if t < 3:
                    self.add((p.z - 3 + t, p.c, p.y, p.x), zd, (t - 1,))
            when((p.z <= 2) & (p.z - 3 + t >= 0), take)
            return
        cp = lambda: self.copy(4 + t, (p.z - 4 + t, p.c, p.y, p.x), zd, (t - 1,), p.dev(z=p.z - 1))
        when((p.z >= 1) & (p.z - 4 + t >= 0), (lambda: cp().start()) if op == "start" else (lambda: cp().wait_send()))

    def up(self, t, op):
        p, zu = self.p, self.land[6]
        if op == "recv":
            def take():
                self.copy(7 + t, (p.z + 3 - t, p.c, p.y, p.x), zu, (t - 1,), p.dev(x=1 - p.x)).wait_recv()
                if t < 3:
                    self.add((p.z + 3 - t, p.c, p.y, p.x), zu, (t - 1,))
            when((p.z >= 1) & (p.z + 3 - t <= 3), take)
            return
        cp = lambda: self.copy(7 + t, (p.z + 4 - t, p.c, p.y, p.x), zu, (t - 1,), p.dev(z=p.z + 1))
        when((p.z <= 2) & (p.z + 4 - t <= 3), (lambda: cp().start()) if op == "start" else (lambda: cp().wait_send()))

    def step(self, s):
        p = self.p
        core, a2, b2, a1, b1, zd, zu = self.land
        table = self.table()
        starts = {0: (0,), 1: (1, 2), 2: (3, 4)}.get(s, ())
        recvs = {1: (0,), 2: (1, 2), 3: (3, 4)}.get(s, ())
        for i in recvs:
            row = table[i]
            self.copy(i, row[0], row[1], row[2], row[3]).wait_recv()
        if s == 1:
            @pl.loop(0, 16)
            def _(i):
                zi, yi, xi = i // 4, (i // 2) % 2, i % 2
                self.add((zi, p.c, yi, xi), core, (zi, yi, xi))
        if s == 2:
            @pl.loop(0, 4)
            def _(i):
                self.add((i // 2, p.c, p.y, i % 2), a2, (i // 2, i % 2))
                self.add((2 + i // 2, p.c, i % 2, p.x), b2, (i // 2, i % 2))
        if s == 3:
            @pl.loop(0, 2)
            def _(i):
                self.add((i, p.c, p.y, p.x), a1, (i,))
                self.add((2 + i, p.c, p.y, p.x), b1, (i,))
        for i in starts:
            row = table[i]
            self.copy(i, row[0], row[1], row[2], row[3]).start()
        if s == 3:
            self.down(1, "start")
            self.up(1, "start")
        if s in (4, 5):
            t = s - 3
            self.down(t, "recv")
            self.down(t + 1, "start")
            self.up(t, "recv")
            self.up(t + 1, "start")
        if s == 6:
            self.down(3, "recv")
            self.up(3, "recv")
            tail = (self.rows, slice(None))
            own = self.buf[(p.z, p.c, p.y, p.x) + tail].astype(F32)
            from_above = zd[(2,) + tail].astype(F32)
            from_below = zu[(2,) + tail].astype(F32)
            self.final(
                jnp.where(p.z < 3, own + from_above, own) + jnp.where(p.z > 0, from_below, jnp.zeros_like(own))
            )

    def finish(self):
        for t in (1, 2, 3):
            self.down(t, "sent")
            self.up(t, "sent")
        for i, row in enumerate(self.table()):
            self.copy(i, row[0], row[1], row[2], row[3]).wait_send()


class SmallGather:
    def __init__(self, place, buf, ssem, rsem, k, rows):
        self.p, self.buf, self.ssem, self.rsem, self.k, self.rows = place, buf, ssem, rsem, k, rows

    def copy(self, i, idx, dev):
        ref = self.buf.at[idx + (self.rows, slice(None))]
        return pltpu.make_async_remote_copy(
            ref, ref, self.ssem.at[self.k, i], self.rsem.at[self.k, i], device_id=dev, device_id_type=MESH
        )

    def table(self):
        p = self.p
        column, plane, sibling = p.peers()
        every = slice(None)
        first = [(i, (p.z, p.c, p.y, p.x), column[i], ((p.z + 3 - i) % 4, p.c, p.y, p.x)) for i in range(3)]
        far = [(p.y, 1 - p.x), (1 - p.y, p.x), (1 - p.y, 1 - p.x)]
        second = [(3 + i, (every, p.c, p.y, p.x), plane[i], (every, p.c) + far[i]) for i in range(3)]
        third = [(6, (every, p.c, every, every), sibling, (every, 1 - p.c, every, every))]
        return first, second, third

    def step(self, s):
        hops = self.table()
        if s > 0:
            for i, _, dev, came in hops[s - 1]:
                self.copy(i, came, dev).wait_recv()
        if s < 3:
            for i, idx, dev, _ in hops[s]:
                self.copy(i, idx, dev).start()

    def finish(self):
        for hop in self.table():
            for i, idx, dev, _ in hop:
                self.copy(i, idx, dev).wait_send()


class SmallReduce:
    def __init__(self, place, buf, land, ssem, rsem, k, final):
        self.p, self.buf, self.land, self.ssem, self.rsem, self.k = place, buf, land, ssem, rsem, k
        self.final = final

    def copy(self, i, idx, dst, dev):
        return pltpu.make_async_remote_copy(
            self.buf.at[idx], dst, self.ssem.at[self.k, i], self.rsem.at[self.k, i], device_id=dev, device_id_type=MESH
        )

    def table(self):
        p = self.p
        column, plane, sibling = p.peers()
        every = slice(None)
        core, flat, line = self.land
        far = [(p.y, 1 - p.x), (1 - p.y, p.x), (1 - p.y, 1 - p.x)]
        first = [(0, (every, 1 - p.c, every, every), core, sibling)]
        second = [(1 + i, (every, p.c) + far[i], flat.at[i], plane[i]) for i in range(3)]
        third = [(4 + i, ((p.z + 1 + i) % 4, p.c, p.y, p.x), line.at[i], column[i]) for i in range(3)]
        return first, second, third

    def step(self, s):
        p = self.p
        core, flat, line = self.land
        hops = self.table()
        if s > 0:
            for i, idx, dst, dev in hops[s - 1]:
                self.copy(i, idx, dst, dev).wait_recv()
        if s == 1:
            self.buf[:, p.c, :, :, :, :] += core[...]
        if s == 2:
            self.buf[:, p.c, p.y, p.x, :, :] += flat[0] + flat[1] + flat[2]
        if s < 3:
            for i, idx, dst, dev in hops[s]:
                self.copy(i, idx, dst, dev).start()
        else:
            self.final(self.buf[p.z, p.c, p.y, p.x, :, :] + line[0] + line[1] + line[2])

    def finish(self):
        for hop in self.table():
            for i, idx, dst, dev in hop:
                self.copy(i, idx, dst, dev).wait_send()


def small_landing(rows, cols):
    return [
        pltpu.VMEM((4, 2, 2, rows, cols), F32), pltpu.VMEM((3, 4, rows, cols), F32), pltpu.VMEM((3, rows, cols), F32)
    ]


def landing(rows, cols, dtype):
    return [
        pltpu.VMEM((4, 2, 2, rows, cols), dtype),
        pltpu.VMEM((2, 2, rows, cols), dtype),
        pltpu.VMEM((2, 2, rows, cols), dtype),
        pltpu.VMEM((2, rows, cols), dtype),
        pltpu.VMEM((2, rows, cols), dtype),
        pltpu.VMEM((3, rows, cols), dtype),
        pltpu.VMEM((3, rows, cols), dtype),
    ]


def pack48(block):
    wide = block.astype(F32)
    return jnp.concatenate([wide[:, :HALF], wide[:, HALF:]], axis=0).astype(BF)


def iota(shape, dim):
    return lax.broadcasted_iota(jnp.int32, shape, dim)


def onehot(cond):
    return jnp.where(cond, 1.0, 0.0).astype(BF)


def ln_hat(v):
    center = v - jnp.mean(v, axis=-1, keepdims=True)
    spread = jnp.mean(center * center, axis=-1, keepdims=True)
    return center * lax.rsqrt(spread + 1e-06)


def fold(v):
    total = v[0:8]
    for i in range(1, v.shape[0] // 8):
        total = total + v[8 * i:8 * i + 8]
    return total


def pick_row(flat, r):
    return mm(onehot(iota((32, 512), 1) == iota((32, 512), 0) * 16 + r), flat)


def spread_bias(rows, n, start, width):
    k = rows.shape[1]
    lane = iota((k, width), 0)
    col = iota((k, width), 1) + start
    grid = mm(rows.astype(BF), onehot((col % n == lane) & (lane < n)))
    dev = iota((32, width), 0)
    mine = (iota((32, width), 1) + start) // n == dev
    return jnp.sum(jnp.where(mine, grid, 0.0), axis=0, keepdims=True)


def softmax_pair(qs, k, bias):
    scores = mm_nt(qs, k) * 0.125 + bias
    top = jnp.max(scores, axis=-1, keepdims=True)
    e = jnp.exp(scores - top)
    return e / jnp.sum(e, axis=-1, keepdims=True)


def group_start(g, tokens):
    return pl.multiple_of(jnp.minimum(g * GROUP, tokens - GROUP), 16)


def fill_mask(mask_ref, frames):
    shape = mask_ref.shape
    row = iota(shape, 0) % GROUP
    mask_ref[...] = jnp.where(row // frames == iota(shape, 1) // frames, 0.0, -1e30)


F_SEQ = (
    0, "XH", 10, 20, 1, 11, 21, 30, 2, 12, 22, 40, 3, "PM", 90, 13, 31, 23, 41, 60, 91, 32, 50, 42, 61, 14, 80, 92,
    24, 51, 15, 62, 33, 93, "MV", 16, 43, 25, 52, "LN", 81, "R0", 34, ("QK", 0,), 26, 70, 44, "R1", ("QK", 1,), 82,
    35, 71, 53, 36, "R2", ("QK", 2,), 45, 63, 72, ("AT", 0, 1), ("AT", 1, 2), 54, ("AT", 2, 3), 46, ("AT", 3, 4),
    ("AT", 4, 5), ("AT", 5, 6), ("AT", 6, 7), ("AT", 7, 8), ("AT", 8, 9), 64, ("AT", 9, 10), ("AT", 10, 11), "R3", 55,
    "PR", "L2", 56, 73, "GB", "R4", ("UP", 0,), 65, 83, ("UP", 1,), 74, ("UP", 2,), 66, "R5", ("UP", 3,), ("UP", 4,),
    84, ("UP", 5,), ("DG", 0,), 75, ("DG", 1,), ("DG", 2,), ("DG", 3,), ("DG", 4,), 76, ("DG", 5,), ("DG", 6,), 85,
    ("DG", 7,), "R6", "DN0", 86, "R7", "DN1",
)


F_ROWS = ((0, 48), (48, 48), (96, 48), (144, 48), (192, 96), (288, 96), (384, 96), (480, 96))


def f_kernel(
    x_hbm, og_hbm, cw_ref, small_ref, mw_ref, qw_ref, pw_ref, uw_ref, dw_ref,
    bo_hbm, n1_hbm, qkv_hbm, att_hbm, br_hbm, mid_hbm, n2_hbm, dg_hbm, gp_hbm, gb_hbm,
    wq_hbm, wp_hbm, wu_hbm, wd_hbm, mod_out, gmy_out, mwp_out,
    gbuf, pm, pbuf, l0, l1, l2, dbuf,
    wq, wp, wu, wd, x_v, og_v, n_v, qkv, att, br, mid, act, gpt, bo, gb, amask, bq, bp, bu, bd, acc,
    gs, gr, ps, pr, lsem, gpsem, dsem,
):
    p = Place()
    tokens, width = x_v.shape
    rows_of = [slice(SHARD, SMALL)] + [slice(a, a + n) for a, n in F_ROWS]
    gath = [
        (Gather if k else SmallGather)(p, gbuf, gs, gr, k, pl.ds(r.start, r.stop - r.start)) for k, r in enumerate(rows_of)
    ]
    loads = [pltpu.make_async_copy(x_hbm, x_v, lsem.at[0]), pltpu.make_async_copy(og_hbm, og_v, lsem.at[1])]
    for cp in loads:
        cp.start()
    outs = []
    saved = []

    def save(src, dst):
        cp = pltpu.make_async_copy(src, dst, lsem.at[2 + len(saved)])
        cp.start()
        outs.append(cp)
        saved.append(cp)
        return cp

    own = (p.z, p.c, p.y, p.x)
    gbuf[own + (slice(SHARD, SMALL), slice(None))] = small_ref[...]
    for b in range(3):
        gbuf[own + (slice(48 * b, 48 * b + 48), slice(None))] = pack48(qw_ref[:, width * b:width * b + width])
    gbuf[own + (slice(144, 192), slice(None))] = pack48(pw_ref[...])
    for b in range(4):
        gbuf[own + (slice(192 + 48 * b, 240 + 48 * b), slice(None))] = pack48(uw_ref[:, width * b:width * b + width])
    gbuf[own + (slice(384, 480), slice(None))] = dw_ref[:, :HALF]
    gbuf[own + (slice(480, 576), slice(None))] = dw_ref[:, HALF:]
    p.greet()

    def final_mod(total):
        for m in range(6):
            for j in range(6):
                mod_out[m:m + 1, 128 * j:128 * j + 128] = total[6 * m + j:6 * m + j + 1, :]

    red = SmallReduce(p, pbuf, (l0, l1, l2), ps, pr, 0, final_mod)

    def small_work():
        fill_mask(amask, 12)
        flat = gbuf[:, :, :, :, SHARD:SMALL, :].reshape(512, HALF)
        gated = jnp.concatenate([pick_row(flat, 0), pick_row(flat, 1)], axis=1).astype(BF)
        sel = onehot((iota((width, 128), 0) == p.me * 24 + iota((width, 128), 1)) & (iota((width, 128), 1) < 24))
        gmy = mm(gated, sel).astype(BF)
        gmy_out[...] = gmy
        pad = jnp.zeros((8, width), F32)
        for m in range(6):
            cols = slice(width * m, width * m + width)
            part = jnp.concatenate([mw_ref[:, cols].astype(F32), pad], axis=0).astype(BF)
            mwp_out[:, cols] = part
            prod = mm(gmy[:, :32], part)
            for j in range(6):
                pm[32 * (6 * m + j):32 * (6 * m + j) + 32, :] = prod[:, 128 * j:128 * j + 128]

        @pl.loop(0, 32)
        def _(d):
            for j in range(36):
                pbuf[d // 8, (d // 4) % 2, (d // 2) % 2, d % 2, j:j + 1, :] = pm[pl.ds(32 * j + d, 1), :]
            pbuf[d // 8, (d // 4) % 2, (d // 2) % 2, d % 2, 36:40, :] = jnp.zeros((4, 128), F32)

    def biases():
        flat = gbuf[:, :, :, :, SHARD:SMALL, :].reshape(512, HALF)
        qv, prj, up, dn, md = (pick_row(flat, r) for r in (2, 3, 4, 5, 6))
        bq[:, 0:width] = spread_bias(qv[:, :128], 48, 0, width)
        bq[:, width:2 * width] = jnp.zeros((1, width), F32)
        bq[:, 2 * width:] = spread_bias(qv[:, :128], 48, width, width)
        bp[...] = spread_bias(prj[:, :128], 24, 0, width)
        bd[...] = spread_bias(dn[:, :128], 24, 0, width)
        for m in range(4):
            bu[:, width * m:width * m + width] = spread_bias(up[:, :128], 96, width * m, width)
        for m in range(6):
            mod_out[m:m + 1, :] += spread_bias(md[:, :256], 144, width * m, width)

    def unpack(b, dst, col):
        @pl.loop(0, 16)
        def _(i):
            src = (i // 4, (i // 2) % 2, i % 2)
            one = gbuf[src + (0, slice(48 * b, 48 * b + 48), slice(None))].astype(F32)
            two = gbuf[src + (1, slice(48 * b, 48 * b + 48), slice(None))].astype(F32)
            at = pl.ds(pl.multiple_of(i * 48, 16), 48)
            dst[at, col:col + HALF] = jnp.concatenate([one[:24], two[:24]], axis=0).astype(BF)
            dst[at, col + HALF:col + 2 * HALF] = jnp.concatenate([one[24:], two[24:]], axis=0).astype(BF)

    def unpack_down(h):
        @pl.loop(0, 32)
        def _(d):
            wd[pl.ds(pl.multiple_of(d * 96, 16), 96), HALF * h:HALF * h + HALF] = gbuf[
                d // 8, (d // 4) % 2, (d // 2) % 2, d % 2, 384 + 96 * h:480 + 96 * h, :
            ]

    def rows_loop(body):
        @pl.loop(0, tokens // 48, unroll=3)
        def _(i):
            body(pl.ds(pl.multiple_of(i * 48, 16), 48))

    def first_hat(at):
        mid[at, :] = ln_hat(x_v[at, :].astype(F32))

    def first_norm(at):
        n_v[at, :] = (mid[at, :] * (1.0 + mod_out[1:2, :]) + mod_out[0:1, :]).astype(BF)

    def second_norm(at):
        n_v[at, :] = (ln_hat(mid[at, :]) * (1.0 + mod_out[4:5, :]) + mod_out[3:4, :]).astype(BF)

    def qkv_block(i):
        cols = slice(width * i, width * i + width)
        qkv[:, cols] = (mm(n_v[...], wq[:, cols]) + bq[:, cols]).astype(BF)

    def attention(first, last):
        low_lane = iota((GROUP, 128), 1) < 64

        @pl.loop(first, last)
        def _(g):
            rows = pl.ds(group_start(g, tokens), GROUP)
            for h in range(width // 128):
                q = qkv[rows, 128 * h:128 * h + 128]
                k = qkv[rows, width + 128 * h:width + 128 * h + 128]
                v = qkv[rows, 2 * width + 128 * h:2 * width + 128 * h + 128]
                zero = jnp.zeros_like(q)
                qs = jnp.concatenate([jnp.where(low_lane, q, zero), jnp.where(low_lane, zero, q)], axis=0)
                probs = softmax_pair(qs, k, amask[...]).astype(BF)
                both = mm(probs, v)
                att[rows, 128 * h:128 * h + 128] = jnp.where(low_lane, both[:GROUP], both[GROUP:]).astype(BF)

    def proj():
        branch = mm(att[...], wp[...]) + bp[...]
        br[...] = branch.astype(BF)
        mid[...] = x_v[...].astype(F32) + mod_out[2:3, :] * branch

    def second_cot(at):
        low = (og_v[at, :].astype(F32) * cw_ref[:, 0:1] * mod_out[5:6, :]).astype(BF)
        gb[at, :] = low
        acc[...] += fold(low.astype(F32))

    def dg_copy(j):
        return pltpu.make_async_copy(dbuf.at[j % 2], dg_hbm.at[j // 2, j % 2], dsem.at[j % 2])

    def down_grad(j):
        if j >= 2:
            dg_copy(j - 2).wait()
        grad = mm_tn(act[:, HALF * j:HALF * j + HALF], gb[...])
        for dd in range(4):
            part = grad[96 * dd:96 * dd + 96].astype(BF)
            dbuf[j % 2, dd // 2, dd % 2, 0:96, :] = part[:, :HALF]
            dbuf[j % 2, dd // 2, dd % 2, 96:192, :] = part[:, HALF:]
        dg_copy(j).start()

    def gp_copy(j):
        return pltpu.make_async_copy(gpt.at[j % 2], gp_hbm.at[:, pl.ds(512 * j, 512)], gpsem.at[j % 2])

    def up_tile(j):
        cols = slice(512 * j, 512 * j + 512)
        if j >= 2:
            gp_copy(j - 2).wait()

        @pl.loop(0, 3)
        def _(m):
            at = pl.ds(pl.multiple_of(m * 336, 16), 336)
            hid = mm(n_v[at, :], wu[:, cols]) + bu[:, cols]
            sq = hid * hid
            slope_in = 0.7978845608 + (0.7978845608 * 0.044715) * sq
            half = 0.5 + 0.5 * jnp.tanh(hid * slope_in)
            act[at, cols] = (hid * half).astype(BF)
            rate = 2.0 * 0.7978845608 + (6.0 * 0.7978845608 * 0.044715) * sq
            gpt[j % 2, at, :] = (half + (hid * rate) * (half - half * half)).astype(BF)
        gp_copy(j).start()

    def down_half(h):
        cw = cw_ref[:, 0:1]
        cols = slice(HALF * h, HALF * h + HALF)

        def body(i, gg):
            at = pl.ds(pl.multiple_of(i * 336, 16), 336)
            branch = mm(act[at, :], wd[:, cols]) + bd[:, cols]
            gate = mod_out[5:6, cols]
            bo[at, cols] = (mid[at, cols] + gate * branch).astype(BF)
            cot = og_v[at, cols].astype(F32) * cw
            return gg + jnp.sum(cot * branch, axis=0, keepdims=True)

        mod_out[6:7, cols] = lax.fori_loop(0, tokens // 336, body, jnp.zeros((1, HALF), F32))

    n1_out = []

    def do(tag, *span):
        if isinstance(tag, int):
            item = red if tag >= 90 else gath[tag // 10]
            item.step(tag % 10)
        elif tag == "PM":
            small_work()
        elif tag == "XH":
            loads[0].wait()
            rows_loop(first_hat)
        elif tag == "MV":
            mod_out[6:8, :] = jnp.zeros((2, width), F32)
            acc[...] = jnp.zeros_like(acc)
            biases()
        elif tag in ("R0", "R1", "R2", "R3"):
            b = int(tag[1])
            if b < 3:
                unpack(b, wq, width * b)
            else:
                unpack(b, wp, 0)
                save(wp, wp_hbm)
            if b == 2:
                save(wq, wq_hbm)
        elif tag == "LN":
            rows_loop(first_norm)
            n1_out.append(save(n_v, n1_hbm))
        elif tag == "QK":
            qkv_block(*span)
            if span == (2,):
                save(qkv, qkv_hbm)
        elif tag == "AT":
            attention(*span)
            if span[1] == 11:
                save(att, att_hbm)
        elif tag == "PR":
            proj()
            save(br, br_hbm)
            save(mid, mid_hbm)
            n1_out[0].wait()
            outs.remove(n1_out[0])
        elif tag == "L2":
            rows_loop(second_norm)
            save(n_v, n2_hbm)
        elif tag in ("R4", "R5"):
            b = 4 if tag == "R4" else 6
            unpack(b, wu, width * (b - 4))
            unpack(b + 1, wu, width * (b - 3))
            if tag == "R5":
                save(wu, wu_hbm)
        elif tag == "UP":
            up_tile(*span)
        elif tag == "GB":
            loads[1].wait()
            rows_loop(second_cot)
            mod_out[7:8, :] = jnp.sum(acc[...], axis=0, keepdims=True)
            save(gb, gb_hbm)
        elif tag == "DG":
            down_grad(*span)
        elif tag in ("R6", "R7"):
            unpack_down(int(tag[1]) - 6)
            if tag == "R7":
                save(wd, wd_hbm)
        elif tag == "DN0":
            down_half(0)
        elif tag == "DN1":
            down_half(1)
            save(bo, bo_hbm)

    for tag in F_SEQ:
        do(*(tag if isinstance(tag, tuple) else (tag,)))
    for j in (4, 5):
        gp_copy(j).wait()
    for j in (6, 7):
        dg_copy(j).wait()
    for cp in outs:
        cp.wait()
    for g in gath:
        g.finish()
    red.finish()


def forward(xt, ogt, cw, small, mod_w, qkv_w, proj_w, up_w, down_w):
    t, d = xt.shape
    hid = up_w.shape[1]
    s = jax.ShapeDtypeStruct
    outs = [
        s((t, d), BF), s((t, d), BF), s((t, 3 * d), BF), s((t, d), BF), s((t, d), BF), s((t, d), F32), s((t, d), BF),
        s((4, 2, 2, 2, 192, HALF), BF), s((t, hid), BF), s((t, d), BF),
        s((d, 3 * d), BF), s((d, d), BF), s((d, hid), BF), s((hid, d), BF),
        s((8, d), F32), s((32, 128), BF), s((32, 6 * d), BF),
    ]
    v = pltpu.VMEM
    scratch = [
        v((4, 2, 2, 2, SMALL, HALF), BF), v((6 * d // 128 * 32, 128), F32), v((4, 2, 2, 2, 40, 128), F32), *small_landing(40, 128), v((2, 2, 2, 192, HALF), BF),
        v((d, 3 * d), BF), v((d, d), BF), v((d, hid), BF), v((hid, d), BF),
        v((t, d), BF), v((t, d), BF), v((t, d), BF), v((t, 3 * d), BF), v((t, d), BF), v((t, d), BF), v((t, d), F32),
        v((t, hid), BF), v((2, t, 512), BF), v((t, d), BF), v((t, d), BF), v((2 * GROUP, GROUP), F32),
        v((1, 3 * d), F32), v((1, d), F32), v((1, hid), F32), v((1, d), F32), v((8, d), F32),
        pltpu.SemaphoreType.DMA((9, 11)), pltpu.SemaphoreType.DMA((9, 11)),
        pltpu.SemaphoreType.DMA((1, 11)), pltpu.SemaphoreType.DMA((1, 11)),
        pltpu.SemaphoreType.DMA((24,)), pltpu.SemaphoreType.DMA((2,)), pltpu.SemaphoreType.DMA((2,)),
    ]
    return pl.pallas_call(
        f_kernel,
        out_shape=outs,
        in_specs=[ANY, ANY] + [VMEM] * 7,
        out_specs=[ANY] * 14 + [VMEM] * 3,
        scratch_shapes=scratch,
        compiler_params=pltpu.CompilerParams(collective_id=0, has_side_effects=True, vmem_limit_bytes=VMEM_LIMIT),
        cost_estimate=pl.CostEstimate(flops=15 * 10**9, bytes_accessed=70 * 10**6, transcendentals=4 * 10**6),
        name="forward",
    )(xt, ogt, cw, small, mod_w, qkv_w, proj_w, up_w, down_w)


B_SEQ = (
    "LD", 0, "ST", 10, ("A", 0,), ("A", 1,), ("A", 2,), 1, ("A", 3,), ("A", 4,), ("A", 5,), 11, "U0", "U1", 20, "U2",
    2, "U3", 30, ("N0", 0,), 21, ("N0", 1,), ("N0", 2,), "L2", 3, 12, 31, "PG", 40, 4, "PA", ("AB", 0, 1), 5, 13, 22,
    ("AB", 1, 2), ("AB", 2, 3), 6, 14, 41, ("AB", 3, 4), 32, ("AB", 4, 5), 15, 23, ("AB", 5, 6), 42, ("AB", 6, 7), 16,
    24, ("AB", 7, 8), 33, 43, ("AB", 8, 9), 25, ("AB", 9, 10), 34, 44, ("AB", 10, 11), 26, "Q0", 35, 45, 50, "Q1", 60,
    "Q2", 36, 46, 51, 61, 70, ("N1", 0,), ("N1", 1,), 71, ("N1", 2,), "L1", 52, 62, "MB", 90, "BI", "BB", 91, 80, 53,
    72, 63, 81, 54, 92, 64, 55, 73, 93, "GM", 100, 82, 56, 65, 74, 101, 83, 66, 75, 102, 76, 103, "CO",
)
CHUNKS = ((384, 96), (480, 96), (192, 96), (288, 96), (144, 48), (0, 48), (48, 48), (96, 48))


def ln_parts(v):
    center = v - jnp.mean(v, axis=-1, keepdims=True)
    spread = jnp.mean(center * center, axis=-1, keepdims=True)
    inv = lax.rsqrt(spread + 1e-06)
    return center * inv, inv


def ln_back(g, hat, inv, scale):
    dh = g * (1.0 + scale)
    return inv * (dh - jnp.mean(dh, axis=-1, keepdims=True) - hat * jnp.mean(dh * hat, axis=-1, keepdims=True))


def split_bias(vec, n):
    width = vec.shape[1]
    mine = iota((32, width), 1) // n == iota((32, width), 0)
    lane = iota((width, 128), 1)
    ones = jnp.where((iota((width, 128), 0) % n == lane) & (lane < n), 1.0, 0.0)
    return jnp.dot(jnp.where(mine, vec, 0.0), ones, precision=lax.Precision.HIGHEST, preferred_element_type=F32)


def b_kernel(
    x_hbm, og_hbm, cw_ref, mod_ref, gmy_ref, mwp_ref,
    n1_hbm, qkv_hbm, att_hbm, br_hbm, mid_hbm, n2_hbm, dg_hbm, gp_hbm, gb_hbm, wq_hbm, wp_hbm, wu_hbm, wd_hbm,
    tg_hbm, gq_out, gp_out, gu_out, gd_out, bias_out, gmw_out, gmb_out, cg_out,
    gbuf, k0, k1, k2, k3, k4, k5, k6, sbuf, t0, t1, t2, mbuf, cbuf, stage,
    wa, wu, gh, gb, nb, mid, gn, br, amask, vec, accs,
    rs, rr, ts, tr, gs, gr, lsem,
):
    p = Place()
    tokens, width = gb.shape
    cw = cw_ref[:, 0:1]
    pending = {}

    def load(name, i, src, dst):
        pending[name] = pltpu.make_async_copy(src, dst, lsem.at[i])
        pending[name].start()

    def put48(dst_out, b, total):
        dst_out[:, width * b:width * b + HALF] = total[:24]
        dst_out[:, width * b + HALF:width * b + width] = total[24:48]

    def finals(k):
        def go(total):
            if k < 2:
                gd_out[:, HALF * k:HALF * k + HALF] = total
            elif k < 4:
                put48(gu_out, 2 * (k - 2), total[:48])
                put48(gu_out, 2 * (k - 2) + 1, total[48:])
            elif k == 4:
                put48(gp_out, 0, total)
            else:
                put48(gq_out, k - 5, total)
        return go

    land = (k0, k1, k2, k3, k4, k5, k6)
    reds = [Reduce(p, gbuf, land, rs, rr, k, pl.ds(a, n), finals(k)) for k, (a, n) in enumerate(CHUNKS)]

    def bias_final(total):
        bias_out[...] = total

    bred = SmallReduce(p, sbuf, (t0, t1, t2), ts, tr, 0, bias_final)
    mgath = SmallGather(p, mbuf, gs, gr, 0, pl.ds(0, 16))
    cgath = SmallGather(p, cbuf, gs, gr, 1, pl.ds(0, 32))

    def weight_grad(left_ref, right, b):
        @pl.loop(0, 2)
        def _(m):
            at = pl.ds(pl.multiple_of(m * HALF, HALF), HALF)
            grad = mm_tn(left_ref[:, at], right[...])
            for dd in range(16):
                gbuf[2 * m + dd // 8, dd // 4 % 2, dd // 2 % 2, dd % 2, 48 * b:48 * b + 48, :] = pack48(
                    grad[24 * dd:24 * dd + 24]
                )

    def act_grad(j):
        cols = slice(512 * j, 512 * j + 512)
        low = (mm_nt(gb[...], wa[cols, :]) * gh[:, cols].astype(F32)).astype(BF)
        gh[:, cols] = low
        vec[0:1, cols] = jnp.sum(low.astype(F32), axis=0, keepdims=True)

    def norm2_back():
        scale, gate = mod_ref[4:5, :], mod_ref[2:3, :]
        accs[...] = jnp.zeros_like(accs)

        @pl.loop(0, tokens // 48, unroll=3)
        def _(i):
            at = pl.ds(pl.multiple_of(i * 48, 16), 48)
            g = gn[at, :]
            hat, inv = ln_parts(mid[at, :])
            gm = gb[at, :].astype(F32) * cw + ln_back(g, hat, inv, scale)
            gn[at, :] = gm
            low = (gm * gate).astype(BF)
            gh[at, 3 * width:4 * width] = low
            accs[0:8, :] += fold(g)
            accs[8:16, :] += fold(g * hat)
            accs[16:24, :] += fold(gm * br[at, :].astype(F32))
            accs[24:32, :] += fold(low.astype(F32))

        for i, row in enumerate((3, 4, 2)):
            vec[1 + row:2 + row, 0:width] = jnp.sum(accs[8 * i:8 * i + 8, :], axis=0, keepdims=True)
        vec[8:9, 0:width] = jnp.sum(accs[24:32, :], axis=0, keepdims=True)

    def norm1_back():
        scale = mod_ref[1:2, :]
        accs[...] = jnp.zeros_like(accs)

        @pl.loop(0, tokens // 48, unroll=3)
        def _(i):
            at = pl.ds(pl.multiple_of(i * 48, 16), 48)
            g = mid[at, :]
            hat, inv = ln_parts(br[at, :].astype(F32))
            nb[at, :] = (gn[at, :] + ln_back(g, hat, inv, scale)).astype(BF)
            accs[0:8, :] += fold(g)
            accs[8:16, :] += fold(g * hat)

        for i in range(2):
            vec[1 + i:2 + i, 0:width] = jnp.sum(accs[8 * i:8 * i + 8, :], axis=0, keepdims=True)

    def attention_back(first, last):
        low_lane = iota((GROUP, 128), 1) < 64

        @pl.loop(first, last)
        def _(g):
            start = group_start(g, tokens)
            rows = pl.ds(start, GROUP)
            for h in range(width // 128):
                q, k, v = (gh[rows, width * i + 128 * h:width * i + 128 * h + 128] for i in range(3))
                ga = gb[rows, 128 * h:128 * h + 128]
                zero = jnp.zeros_like(q)
                qs = jnp.concatenate([jnp.where(low_lane, q, zero), jnp.where(low_lane, zero, q)], axis=0)
                gas = jnp.concatenate([jnp.where(low_lane, ga, zero), jnp.where(low_lane, zero, ga)], axis=0)
                probs = softmax_pair(qs, k, amask[...])
                gprobs = mm_nt(gas, v)
                gv = mm_tn(probs.astype(BF), gas)
                inner = jnp.sum(probs * gprobs, axis=-1, keepdims=True)
                gsc = (probs * (gprobs - inner)).astype(BF)
                both = mm(gsc, k)
                gq = jnp.where(low_lane, both[:GROUP], both[GROUP:]) * 0.125
                gk = mm_tn(gsc, qs) * 0.125
                for i, g_part in enumerate((gq, gk, gv)):
                    at = pl.ds(pl.multiple_of(start + i * tokens, 16), GROUP)
                    wu[at, 128 * h:128 * h + 128] = g_part.astype(BF)

    def qkv_bias():
        accs[...] = jnp.zeros_like(accs)

        @pl.loop(0, tokens // 48, unroll=3)
        def _(i):
            at = pl.ds(pl.multiple_of(i * 48, 16), 48)
            accs[0:8, :] += fold(wu[at, :].astype(F32))
            accs[8:16, :] += fold(wu[pl.ds(pl.multiple_of(2 * tokens + i * 48, 16), 48), :].astype(F32))

        for i in range(2):
            vec[9:10, width * i:width * i + width] = jnp.sum(accs[8 * i:8 * i + 8, :], axis=0, keepdims=True)

    def bias_blocks():
        stage[0:32, :] = split_bias(vec[9:10, 0:2 * width], 48)
        stage[32:64, :] = split_bias(vec[8:9, 0:width], 24)
        stage[64:96, :] = split_bias(vec[0:1, :], 96)
        stage[96:128, :] = split_bias(vec[7:8, 0:width], 24)

        @pl.loop(0, 32)
        def _(d):
            at = (d // 8, (d // 4) % 2, (d // 2) % 2, d % 2)
            for r in range(4):
                sbuf[at + (slice(r, r + 1), slice(None))] = stage[pl.ds(32 * r + d, 1), :]
            sbuf[at + (slice(4, 8), slice(None))] = jnp.zeros((4, 128), F32)

    def mod_block():
        rows = []
        for m in range(6):
            row = vec[1 + m:2 + m, 0:width]
            rows += [row[:, :HALF], row[:, HALF:]]
        rows.append(jnp.zeros((4, HALF), F32))
        mbuf[p.z, p.c, p.y, p.x, :, :] = jnp.concatenate(rows, axis=0).astype(BF)

    def mod_grads():
        flat = mbuf[...].reshape(512, HALF)
        gmy = gmy_ref[:, 0:32]
        cond = jnp.zeros((32, 32), F32)
        for i in range(12):
            cols = slice(HALF * i, HALF * i + HALF)
            every = pick_row(flat, i)
            low = every.astype(BF)
            gmw_out[:, cols] = mm_tn(gmy, low)[:24]
            gmb_out[:, cols] = jnp.sum(every, axis=0, keepdims=True)
            cond = cond + mm_nt(low, mwp_ref[:, cols])
        mine = (p.z, p.c, p.y, p.x)
        cbuf[mine + (slice(None), slice(None))] = jnp.zeros((32, 128), F32)
        cbuf[mine + (slice(None), slice(0, 32))] = cond

    def cond_out():
        @pl.loop(0, 32)
        def _(d):
            cg_out[pl.ds(d, 1), :] = cbuf[d // 8, (d // 4) % 2, (d // 2) % 2, d % 2, pl.ds(p.me, 1), :]

    def do(tag, *span):
        if isinstance(tag, int):
            (reds + [bred, mgath, cgath])[tag // 10].step(tag % 10)
        elif tag == "MB":
            mod_block()
        elif tag == "BB":
            bias_blocks()
        elif tag == "LD":
            rows = pl.ds(384, 192)
            load("far", 16, dg_hbm.at[:, 1 - p.c], gbuf.at[:, 1 - p.c, :, :, rows, :])
            load("near", 17, dg_hbm.at[:, p.c], gbuf.at[:, p.c, :, :, rows, :])
            load("gb", 0, gb_hbm, gb)
            load("wd", 1, wd_hbm, wa)
            load("gp", 2, gp_hbm, gh)
            load("n2", 3, n2_hbm, nb)
            for i in range(4):
                load("u%d" % i, 12 + i, wu_hbm.at[:, pl.ds(width * i, width)], wu.at[pl.ds(width * i, width), :])
            load("mid", 5, mid_hbm, mid)
            load("br", 6, br_hbm, br)
            p.greet()
            pending["far"].wait()
        elif tag == "ST":
            vec[...] = jnp.zeros_like(vec)
            vec[6:7, 0:width] = mod_ref[6:7, :]
            vec[7:8, 0:width] = mod_ref[7:8, :]
            fill_mask(amask, 12)
            pending["near"].wait()
        elif tag == "A":
            if span == (0,):
                pending["gb"].wait()
                pending["wd"].wait()
                pending["gp"].wait()
            act_grad(*span)
            if span == (5,):
                load("og", 0, og_hbm, gb)
                for i in range(3):
                    load("w%d" % i, 7 + i, wq_hbm.at[:, pl.ds(width * i, width)], wa.at[pl.ds(width * i, width), :])
                load("wp", 10, wp_hbm, wa.at[pl.ds(3 * width, width), :])
        elif tag[0] == "U":
            i = int(tag[1])
            if i == 0:
                pending["n2"].wait()
            weight_grad(nb, gh.at[:, pl.ds(width * i, width)], 4 + i)
            if i == 3:
                load("att", 3, att_hbm, nb)
        elif tag == "N0":
            j = span[0]
            if j == 0:
                for i in range(4):
                    pending["u%d" % i].wait()
            total = mm_nt(gh[:, 0:width], wu[256 * j:256 * j + 256, :])
            for i in (1, 2, 3):
                total = total + mm_nt(
                    gh[:, width * i:width * i + width], wu[width * i + 256 * j:width * i + 256 * j + 256, :]
                )
            gn[:, 256 * j:256 * j + 256] = total
            if j == 2:
                load("qkv", 2, qkv_hbm, gh.at[:, pl.ds(0, 3 * width)])
        elif tag == "L2":
            for name in ("mid", "br", "og"):
                pending[name].wait()
            norm2_back()
            load("x", 6, x_hbm, br)
        elif tag == "PG":
            pending["att"].wait()
            weight_grad(nb, gh.at[:, pl.ds(3 * width, width)], 3)
            load("n1", 3, n1_hbm, nb)
        elif tag == "PA":
            for name in ("w0", "w1", "w2", "wp"):
                pending[name].wait()
            gb[...] = mm_nt(gh[:, 3 * width:4 * width], wa[3 * width:4 * width, :]).astype(BF)
        elif tag == "AB":
            if span[0] == 0:
                pending["qkv"].wait()
            attention_back(*span)
        elif tag in ("Q0", "Q1", "Q2"):
            if tag == "Q0":
                pending["n1"].wait()
            i = int(tag[1])
            weight_grad(nb, wu.at[pl.ds(tokens * i, tokens), :], i)
        elif tag == "N1":
            j = span[0]
            total = mm_nt(wu[0:tokens, :], wa[256 * j:256 * j + 256, :])
            for i in (1, 2):
                total = total + mm_nt(
                    wu[tokens * i:tokens * i + tokens, :], wa[width * i + 256 * j:width * i + 256 * j + 256, :]
                )
            mid[:, 256 * j:256 * j + 256] = total
        elif tag == "L1":
            pending["x"].wait()
            norm1_back()
            load("tg", 11, nb, tg_hbm)
        elif tag == "BI":
            qkv_bias()
        elif tag == "GM":
            mod_grads()
        elif tag == "CO":
            cond_out()

    for tag in B_SEQ:
        do(*(tag if isinstance(tag, tuple) else (tag,)))
    pending["tg"].wait()
    for item in reds + [bred, mgath, cgath]:
        item.finish()


def backward(xt, ogt, cw, mod, gmy, mwp, n1, qkv, att, br, mid, n2, dg, gp, gb, wq, wp, wu, wd):
    t, d = xt.shape
    hid = gp.shape[1]
    s = jax.ShapeDtypeStruct
    outs = [
        s((t, d), BF), s((24, 3 * d), F32), s((24, d), F32), s((24, hid), F32), s((96, d), F32), s((8, 128), F32),
        s((24, 6 * d), F32), s((1, 6 * d), F32), s((32, 128), F32),
    ]
    v = pltpu.VMEM
    dma = pltpu.SemaphoreType.DMA
    scratch = [
        v((4, 2, 2, 2, SHARD, HALF), BF), *landing(SHARD, HALF, BF),
        v((4, 2, 2, 2, 8, 128), F32), *small_landing(8, 128),
        v((4, 2, 2, 2, 16, HALF), BF), v((4, 2, 2, 2, 32, 128), F32), v((128, 128), F32),
        v((hid, d), BF), v((hid, d), BF), v((t, hid), BF), v((t, d), BF), v((t, d), BF),
        v((t, d), F32), v((t, d), F32), v((t, d), BF), v((2 * GROUP, GROUP), F32), v((16, hid), F32), v((32, d), F32),
        dma((8, 11)), dma((8, 11)), dma((1, 11)), dma((1, 11)), dma((2, 11)), dma((2, 11)), dma((18,)),
    ]
    return pl.pallas_call(
        b_kernel,
        out_shape=outs,
        in_specs=[ANY, ANY] + [VMEM] * 4 + [ANY] * 13,
        out_specs=[ANY] + [VMEM] * 8,
        scratch_shapes=scratch,
        compiler_params=pltpu.CompilerParams(collective_id=1, has_side_effects=True, vmem_limit_bytes=VMEM_LIMIT),
        cost_estimate=pl.CostEstimate(flops=29 * 10**9, bytes_accessed=70 * 10**6, transcendentals=10**6),
        name="backward",
    )(xt, ogt, cw, mod, gmy, mwp, n1, qkv, att, br, mid, n2, dg, gp, gb, wq, wp, wu, wd)


def time_embed(noise_steps, model_width):
    half_width = model_width // 2
    frequency = jnp.exp(-math.log(10000.0) * jnp.arange(half_width, dtype=jnp.float32) / half_width)
    angles = noise_steps.astype(jnp.float32)[:, None] * frequency[None, :]
    return jnp.concatenate([jnp.cos(angles), jnp.sin(angles)], axis=-1)


def fast_local(
    tokens, condition, timesteps, loss_codes, out_grad, mod_weight, mod_bias, qkv_weight, qv_bias,
    proj_weight, proj_bias, up_weight, up_bias, down_weight, down_bias,
):
    axes = ("wide", "narrow")
    _, frames, patches, width = tokens.shape
    count = frames * patches
    cond = condition[0] + time_embed(timesteps, width)[0]
    silu_value, silu_back = jax.vjp(jax.nn.silu, cond)
    gated = silu_value.astype(BF)
    rows = [gated[:HALF], gated[HALF:], qv_bias, proj_bias, up_bias, down_bias, mod_bias]
    small = jnp.stack([jnp.pad(r, (0, HALF - r.shape[0])) for r in rows] + [jnp.zeros((HALF,), BF)] * 9)
    turn = lambda a: a[0].transpose(1, 0, 2).reshape(count, width)
    back = lambda a: a.reshape(patches, frames, width).transpose(1, 0, 2)[None]
    xt, ogt = turn(tokens), turn(out_grad)
    cw = jnp.broadcast_to((loss_codes.astype(F32)[:, None] + 1.0) * 0.25, (1, 128))
    bo, n1, qkv, att, br, mid, n2, dg, gp, gb, wq, wp, wu, wd, mod, gmy, mwp = forward(
        xt, ogt, cw, small, mod_weight, qkv_weight, proj_weight, up_weight, down_weight
    )
    tg, g_qkv, g_proj, g_up, g_down, bias, g_mod, gb_mod, cg = backward(
        xt, ogt, cw, mod, gmy, mwp, n1, qkv, att, br, mid, n2, dg, gp, gb, wq, wp, wu, wd
    )
    me = lax.axis_index(axes)
    own_mod = lax.dynamic_slice(gb_mod[0], (me * mod_bias.shape[0],), mod_bias.shape)
    cond_grad = silu_back(cg[:, :24].reshape(width))[0][None]
    return (
        back(bo), back(tg), cond_grad, g_mod, own_mod,
        g_qkv, bias[0, :48], g_proj, bias[1, :24], g_up, bias[2, :96], g_down, bias[3, :24],
    )


def layernorm(inputs):
    center = inputs - jnp.mean(inputs, axis=-1, keepdims=True)
    spread = jnp.mean(center * center, axis=-1, keepdims=True)
    return center * lax.rsqrt(spread + 1e-06)


def modulate(inputs, shift_part, scale_part):
    return layernorm(inputs) * (1.0 + scale_part) + shift_part


def softmax_last(scores):
    return jax.nn.softmax(scores, axis=-1)


def gelu_tanh(inputs):
    return jax.nn.gelu(inputs, approximate=True)


def product(left_side, right_side):
    return jnp.dot(left_side, right_side, preferred_element_type=jnp.float32)


def column_sum(inputs):
    return jnp.sum(inputs.astype(jnp.float32), axis=0)


def local(
    tokens,
    condition,
    timesteps,
    loss_codes,
    out_grad,
    mod_weight,
    mod_bias,
    qkv_weight,
    qv_bias,
    proj_weight,
    proj_bias,
    up_weight,
    up_bias,
    down_weight,
    down_bias,
):
    gathered = (
        lax.all_gather(mod_weight, ("wide", "narrow"), axis=0, tiled=True),
        lax.all_gather(mod_bias, ("wide", "narrow"), axis=0, tiled=True),
        lax.all_gather(qkv_weight, ("wide", "narrow"), axis=0, tiled=True),
        lax.all_gather(qv_bias, ("wide", "narrow"), axis=0, tiled=True),
        lax.all_gather(proj_weight, ("wide", "narrow"), axis=0, tiled=True),
        lax.all_gather(proj_bias, ("wide", "narrow"), axis=0, tiled=True),
        lax.all_gather(up_weight, ("wide", "narrow"), axis=0, tiled=True),
        lax.all_gather(up_bias, ("wide", "narrow"), axis=0, tiled=True),
        lax.all_gather(down_weight, ("wide", "narrow"), axis=0, tiled=True),
        lax.all_gather(down_bias, ("wide", "narrow"), axis=0, tiled=True),
    )
    (
        mod_full,
        modb_full,
        qkv_full,
        qvb_full,
        proj_full,
        projb_full,
        up_full,
        upb_full,
        down_full,
        downb_full,
    ) = gathered
    frames = tokens.shape[1]
    patches = tokens.shape[2]
    model_width = tokens.shape[3]
    head_count = model_width // HEAD_DIM
    scale_factor = HEAD_DIM ** (-0.5)
    shape_four = (frames, patches, head_count, HEAD_DIM)
    conditioning = condition[0] + time_embed(timesteps, model_width)[0]
    silu_value, silu_back = jax.vjp(jax.nn.silu, conditioning)
    gated = silu_value.astype(jnp.bfloat16)
    modulation = product(gated[None, :], mod_full)[0] + modb_full.astype(jnp.float32)
    shift_first, scale_first, gate_first, shift_second, scale_second, gate_second = jnp.split(
        modulation, 6
    )
    token_rows = tokens[0].reshape(frames * patches, model_width).astype(jnp.float32)
    normed_value, first_norm_back = jax.vjp(modulate, token_rows, shift_first, scale_first)
    normed = normed_value.astype(jnp.bfloat16)
    projected = product(normed, qkv_full)
    queries = (
        (projected[:, :model_width] + qvb_full[:model_width].astype(jnp.float32))
        .astype(jnp.bfloat16)
        .reshape(shape_four)
    )
    keys_all = projected[:, model_width : 2 * model_width].astype(jnp.bfloat16).reshape(shape_four)
    values_all = (
        (projected[:, 2 * model_width :] + qvb_full[model_width:].astype(jnp.float32))
        .astype(jnp.bfloat16)
        .reshape(shape_four)
    )
    scores = (
        jnp.einsum("fphd,gphd->phfg", queries, keys_all, preferred_element_type=jnp.float32)
        * scale_factor
    )
    soft_value, softmax_back = jax.vjp(softmax_last, scores)
    softened = soft_value.astype(jnp.bfloat16)
    attended_four = jnp.einsum(
        "phfg,gphd->fphd", softened, values_all, preferred_element_type=jnp.float32
    )
    attended = attended_four.reshape(frames * patches, model_width).astype(jnp.bfloat16)
    branch_first = product(attended, proj_full) + projb_full.astype(jnp.float32)
    middle = token_rows + gate_first * branch_first
    second_value, second_norm_back = jax.vjp(modulate, middle, shift_second, scale_second)
    normed_second = second_value.astype(jnp.bfloat16)
    hidden = product(normed_second, up_full) + upb_full.astype(jnp.float32)
    gelu_value, gelu_back = jax.vjp(gelu_tanh, hidden)
    activated = gelu_value.astype(jnp.bfloat16)
    branch_second = product(activated, down_full) + downb_full.astype(jnp.float32)
    result = middle + gate_second * branch_second
    block_output = result.astype(jnp.bfloat16).reshape(tokens.shape)
    mod_back, qkv_back, proj_back, up_back, down_back = (
        lax.all_gather(mod_weight, ("wide", "narrow"), axis=0, tiled=True),
        lax.all_gather(qkv_weight, ("wide", "narrow"), axis=0, tiled=True),
        lax.all_gather(proj_weight, ("wide", "narrow"), axis=0, tiled=True),
        lax.all_gather(up_weight, ("wide", "narrow"), axis=0, tiled=True),
        lax.all_gather(down_weight, ("wide", "narrow"), axis=0, tiled=True),
    )
    clip_weight = (loss_codes[0].astype(jnp.float32) + 1.0) * 0.25
    cotangent = out_grad[0].reshape(frames * patches, model_width).astype(jnp.float32) * clip_weight
    grad_gate_second = jnp.sum(cotangent * branch_second, axis=0)
    grad_branch_second = (cotangent * gate_second).astype(jnp.bfloat16)
    grad_down = jnp.einsum(
        "rk,rd->kd", activated, grad_branch_second, preferred_element_type=jnp.float32
    )
    grad_down_bias = column_sum(grad_branch_second)
    grad_activated = jnp.einsum(
        "rd,kd->rk", grad_branch_second, down_back, preferred_element_type=jnp.float32
    )
    grad_hidden = gelu_back(grad_activated)[0].astype(jnp.bfloat16)
    grad_up = jnp.einsum(
        "rd,rk->dk", normed_second, grad_hidden, preferred_element_type=jnp.float32
    )
    grad_up_bias = column_sum(grad_hidden)
    grad_normed_second = jnp.einsum(
        "rk,dk->rd", grad_hidden, up_back, preferred_element_type=jnp.float32
    )
    middle_part, grad_shift_second, grad_scale_second = second_norm_back(grad_normed_second)
    grad_middle = cotangent + middle_part
    grad_gate_first = jnp.sum(grad_middle * branch_first, axis=0)
    grad_branch_first = (grad_middle * gate_first).astype(jnp.bfloat16)
    grad_proj = jnp.einsum(
        "re,rd->ed", attended, grad_branch_first, preferred_element_type=jnp.float32
    )
    grad_proj_bias = column_sum(grad_branch_first)
    grad_attended = (
        jnp.einsum("rd,ed->re", grad_branch_first, proj_back, preferred_element_type=jnp.float32)
        .astype(jnp.bfloat16)
        .reshape(shape_four)
    )
    grad_softened = jnp.einsum(
        "fphd,gphd->phfg", grad_attended, values_all, preferred_element_type=jnp.float32
    )
    grad_values = jnp.einsum(
        "phfg,fphd->gphd", softened, grad_attended, preferred_element_type=jnp.float32
    ).astype(jnp.bfloat16)
    grad_scores = softmax_back(grad_softened)[0].astype(jnp.bfloat16)
    grad_queries = (
        jnp.einsum("phfg,gphd->fphd", grad_scores, keys_all, preferred_element_type=jnp.float32)
        * scale_factor
    ).astype(jnp.bfloat16)
    grad_keys = (
        jnp.einsum("phfg,fphd->gphd", grad_scores, queries, preferred_element_type=jnp.float32)
        * scale_factor
    ).astype(jnp.bfloat16)
    flat_shape = (frames * patches, model_width)
    grad_projected = jnp.concatenate(
        [
            grad_queries.reshape(flat_shape),
            grad_keys.reshape(flat_shape),
            grad_values.reshape(flat_shape),
        ],
        axis=1,
    )
    grad_qkv = jnp.einsum("rd,rk->dk", normed, grad_projected, preferred_element_type=jnp.float32)
    grad_qv_bias = jnp.concatenate(
        [column_sum(grad_queries.reshape(flat_shape)), column_sum(grad_values.reshape(flat_shape))]
    )
    grad_normed = jnp.einsum(
        "rk,dk->rd", grad_projected, qkv_back, preferred_element_type=jnp.float32
    )
    token_part, grad_shift_first, grad_scale_first = first_norm_back(grad_normed)
    tokens_grad = (grad_middle + token_part).astype(jnp.bfloat16).reshape(tokens.shape)
    grad_modulation = jnp.concatenate(
        [
            grad_shift_first,
            grad_scale_first,
            grad_gate_first,
            grad_shift_second,
            grad_scale_second,
            grad_gate_second,
        ]
    ).astype(jnp.bfloat16)
    grad_gated = jnp.einsum(
        "ij,j->i", mod_back, grad_modulation, preferred_element_type=jnp.float32
    )
    condition_grad = silu_back(grad_gated)[0][None, :]
    remaining = (
        grad_qkv,
        grad_qv_bias,
        grad_proj,
        grad_proj_bias,
        grad_up,
        grad_up_bias,
        grad_down,
        grad_down_bias,
    )
    grad_mod = jnp.einsum("i,j->ij", gated, grad_modulation, preferred_element_type=jnp.float32)
    grad_mod_bias = grad_modulation.astype(jnp.float32)
    gradients = (grad_mod, grad_mod_bias) + remaining
    owned = lax.psum_scatter(gradients, ("wide", "narrow"), scatter_dimension=0, tiled=True)
    owned_mod = owned[0]
    owned_mod_bias = owned[1]
    rest_owned = owned[2:]
    return (
        block_output,
        tokens_grad,
        condition_grad,
        owned_mod,
        owned_mod_bias,
        rest_owned[0],
        rest_owned[1],
        rest_owned[2],
        rest_owned[3],
        rest_owned[4],
        rest_owned[5],
        rest_owned[6],
        rest_owned[7],
    )


def solution(mesh):
    axes = ("wide", "narrow")
    four, two, one = P(axes, None, None, None), P(axes, None), P(axes)
    in_specs = (four, two, one, one, four, two, one, two, one, two, one, two, one, two, one)
    out_specs = (four, four, two, two, one, two, one, two, one, two, one, two, one)
    body = fast_local if (mesh.shape["wide"], mesh.shape["narrow"]) == (8, 4) else local
    return jax.shard_map(body, mesh=mesh, in_specs=in_specs, out_specs=out_specs, check_vma=False)
```

```python
import math

import jax
import jax.numpy as jnp
from jax import lax
from jax.experimental import pallas as pl
from jax.experimental.pallas import tpu as pltpu
from jax.sharding import PartitionSpec as P

HEAD_DIM = 64
VMEM_LIMIT = 63 * 2**20


BF = jnp.bfloat16
F32 = jnp.float32
MESH = pl.DeviceIdType.MESH
ANY = pl.BlockSpec(memory_space=pl.ANY)
VMEM = pl.BlockSpec(memory_space=pltpu.VMEM)
BLOCKS = 12
SHARD = 48 * BLOCKS
SMALL = SHARD + 16
HALF = 384
GROUP = 96


def mm(a, b):
    return jnp.dot(a, b, preferred_element_type=F32)


def mm_nt(a, b):
    return lax.dot_general(a, b, (((1,), (1,)), ((), ())), preferred_element_type=F32)


def mm_tn(a, b):
    return lax.dot_general(a, b, (((0,), (0,)), ((), ())), preferred_element_type=F32)


class Place:
    def __init__(self):
        wide = lax.axis_index("wide")
        narrow = lax.axis_index("narrow")
        self.z, self.c = wide // 2, wide % 2
        self.y, self.x = narrow // 2, narrow % 2
        self.me = wide * 4 + narrow

    def dev(self, z=None, c=None, y=None, x=None):
        z = self.z if z is None else z
        c = self.c if c is None else c
        y = self.y if y is None else y
        x = self.x if x is None else x
        return (z * 2 + c, y * 2 + x)

    def peers(self):
        column = [self.dev(z=(self.z + i) % 4) for i in (1, 2, 3)]
        plane = [self.dev(x=1 - self.x), self.dev(y=1 - self.y), self.dev(y=1 - self.y, x=1 - self.x)]
        return column, plane, self.dev(c=1 - self.c)

    def greet(self):
        bar = pltpu.get_barrier_semaphore()
        column, plane, sibling = self.peers()
        for target in column + plane + [sibling]:
            pl.semaphore_signal(bar, inc=1, device_id=target, device_id_type=MESH)
        pl.semaphore_wait(bar, 7)


def when(cond, act):
    pl.when(cond)(act)


class Gather:
    def __init__(self, place, buf, ssem, rsem, k, rows):
        self.p, self.buf, self.ssem, self.rsem, self.k, self.rows = place, buf, ssem, rsem, k, rows

    def copy(self, i, idx, dev):
        ref = self.buf.at[idx + (self.rows, slice(None))]
        return pltpu.make_async_remote_copy(
            ref, ref, self.ssem.at[self.k, i], self.rsem.at[self.k, i], device_id=dev, device_id_type=MESH
        )

    def up(self, h, op):
        p = self.p
        if op == "recv":
            when(p.z >= h, lambda: self.copy(h - 1, (p.z - h, p.c, p.y, p.x), p.dev(x=1 - p.x)).wait_recv())
            return
        cp = lambda: self.copy(h - 1, (p.z - (h - 1), p.c, p.y, p.x), p.dev(z=p.z + 1))
        when((p.z <= 2) & (p.z >= h - 1), (lambda: cp().start()) if op == "start" else (lambda: cp().wait_send()))

    def down(self, h, op):
        p = self.p
        if op == "recv":
            when(p.z + h <= 3, lambda: self.copy(h + 2, (p.z + h, p.c, p.y, p.x), p.dev(x=1 - p.x)).wait_recv())
            return
        cp = lambda: self.copy(h + 2, (p.z + (h - 1), p.c, p.y, p.x), p.dev(z=p.z - 1))
        when((p.z >= 1) & (p.z + (h - 1) <= 3), (lambda: cp().start()) if op == "start" else (lambda: cp().wait_send()))

    def plane(self):
        p = self.p
        low, high, every = pl.ds(0, 2), pl.ds(2, 2), slice(None)
        return (
            ((low, p.c, p.y, p.x), p.dev(x=1 - p.x), (low, p.c, p.y, 1 - p.x)),
            ((high, p.c, p.y, p.x), p.dev(y=1 - p.y), (high, p.c, 1 - p.y, p.x)),
            ((low, p.c, p.y, every), p.dev(y=1 - p.y), (low, p.c, 1 - p.y, every)),
            ((high, p.c, every, p.x), p.dev(x=1 - p.x), (high, p.c, every, 1 - p.x)),
            ((every, p.c, every, every), p.dev(c=1 - p.c), (every, 1 - p.c, every, every)),
        )

    def step(self, s):
        if 1 <= s <= 3:
            self.up(s, "recv")
            if s < 3:
                self.up(s + 1, "start")
            self.down(s, "recv")
            if s < 3:
                self.down(s + 1, "start")
        if s == 0:
            self.up(1, "start")
            self.down(1, "start")
        table = self.plane()
        starts = {3: (0, 1), 4: (2, 3), 5: (4,)}.get(s, ())
        recvs = {4: (0, 1), 5: (2, 3), 6: (4,)}.get(s, ())
        for i in recvs:
            self.copy(6 + i, table[i][2], table[i][1]).wait_recv()
        for i in starts:
            self.copy(6 + i, table[i][0], table[i][1]).start()

    def finish(self):
        for h in (1, 2, 3):
            self.up(h, "sent")
            self.down(h, "sent")
        for i, row in enumerate(self.plane()):
            self.copy(6 + i, row[0], row[1]).wait_send()


class Reduce:
    def __init__(self, place, buf, land, ssem, rsem, k, rows, final):
        self.p, self.buf, self.land, self.ssem, self.rsem, self.k, self.rows = place, buf, land, ssem, rsem, k, rows
        self.final = final

    def copy(self, i, idx, land, lidx, dev):
        tail = (self.rows, slice(None))
        return pltpu.make_async_remote_copy(
            self.buf.at[idx + tail], land.at[lidx + tail], self.ssem.at[self.k, i], self.rsem.at[self.k, i],
            device_id=dev, device_id_type=MESH,
        )

    def table(self):
        p = self.p
        low, high, every = pl.ds(0, 2), pl.ds(2, 2), slice(None)
        core, a2, b2, a1, b1, zd, zu = self.land
        return (
            ((every, 1 - p.c, every, every), core, (every, every, every), p.dev(c=1 - p.c)),
            ((low, p.c, 1 - p.y, every), a2, (every, every), p.dev(y=1 - p.y)),
            ((high, p.c, every, 1 - p.x), b2, (every, every), p.dev(x=1 - p.x)),
            ((low, p.c, p.y, 1 - p.x), a1, (every,), p.dev(x=1 - p.x)),
            ((high, p.c, 1 - p.y, p.x), b1, (every,), p.dev(y=1 - p.y)),
        )

    def add(self, idx, land, lidx):
        tail = (self.rows, slice(None))
        self.buf[idx + tail] = self.buf[idx + tail] + land[lidx + tail]

    def down(self, t, op):
        p, zd = self.p, self.land[5]
        if op == "recv":
            def take():
                self.copy(4 + t, (p.z - 3 + t, p.c, p.y, p.x), zd, (t - 1,), p.dev(x=1 - p.x)).wait_recv()
                if t < 3:
                    self.add((p.z - 3 + t, p.c, p.y, p.x), zd, (t - 1,))
            when((p.z <= 2) & (p.z - 3 + t >= 0), take)
            return
        cp = lambda: self.copy(4 + t, (p.z - 4 + t, p.c, p.y, p.x), zd, (t - 1,), p.dev(z=p.z - 1))
        when((p.z >= 1) & (p.z - 4 + t >= 0), (lambda: cp().start()) if op == "start" else (lambda: cp().wait_send()))

    def up(self, t, op):
        p, zu = self.p, self.land[6]
        if op == "recv":
            def take():
                self.copy(7 + t, (p.z + 3 - t, p.c, p.y, p.x), zu, (t - 1,), p.dev(x=1 - p.x)).wait_recv()
                if t < 3:
                    self.add((p.z + 3 - t, p.c, p.y, p.x), zu, (t - 1,))
            when((p.z >= 1) & (p.z + 3 - t <= 3), take)
            return
        cp = lambda: self.copy(7 + t, (p.z + 4 - t, p.c, p.y, p.x), zu, (t - 1,), p.dev(z=p.z + 1))
        when((p.z <= 2) & (p.z + 4 - t <= 3), (lambda: cp().start()) if op == "start" else (lambda: cp().wait_send()))

    def step(self, s):
        p = self.p
        core, a2, b2, a1, b1, zd, zu = self.land
        table = self.table()
        starts = {0: (0,), 1: (1, 2), 2: (3, 4)}.get(s, ())
        recvs = {1: (0,), 2: (1, 2), 3: (3, 4)}.get(s, ())
        for i in recvs:
            row = table[i]
            self.copy(i, row[0], row[1], row[2], row[3]).wait_recv()
        if s == 1:
            @pl.loop(0, 16)
            def _(i):
                zi, yi, xi = i // 4, (i // 2) % 2, i % 2
                self.add((zi, p.c, yi, xi), core, (zi, yi, xi))
        if s == 2:
            @pl.loop(0, 4)
            def _(i):
                self.add((i // 2, p.c, p.y, i % 2), a2, (i // 2, i % 2))
                self.add((2 + i // 2, p.c, i % 2, p.x), b2, (i // 2, i % 2))
        if s == 3:
            @pl.loop(0, 2)
            def _(i):
                self.add((i, p.c, p.y, p.x), a1, (i,))
                self.add((2 + i, p.c, p.y, p.x), b1, (i,))
        for i in starts:
            row = table[i]
            self.copy(i, row[0], row[1], row[2], row[3]).start()
        if s == 3:
            self.down(1, "start")
            self.up(1, "start")
        if s in (4, 5):
            t = s - 3
            self.down(t, "recv")
            self.down(t + 1, "start")
            self.up(t, "recv")
            self.up(t + 1, "start")
        if s == 6:
            self.down(3, "recv")
            self.up(3, "recv")
            tail = (self.rows, slice(None))
            own = self.buf[(p.z, p.c, p.y, p.x) + tail].astype(F32)
            from_above = zd[(2,) + tail].astype(F32)
            from_below = zu[(2,) + tail].astype(F32)
            self.final(
                jnp.where(p.z < 3, own + from_above, own) + jnp.where(p.z > 0, from_below, jnp.zeros_like(own))
            )

    def finish(self):
        for t in (1, 2, 3):
            self.down(t, "sent")
            self.up(t, "sent")
        for i, row in enumerate(self.table()):
            self.copy(i, row[0], row[1], row[2], row[3]).wait_send()


class SmallGather:
    def __init__(self, place, buf, ssem, rsem, k, rows):
        self.p, self.buf, self.ssem, self.rsem, self.k, self.rows = place, buf, ssem, rsem, k, rows

    def copy(self, i, idx, dev):
        ref = self.buf.at[idx + (self.rows, slice(None))]
        return pltpu.make_async_remote_copy(
            ref, ref, self.ssem.at[self.k, i], self.rsem.at[self.k, i], device_id=dev, device_id_type=MESH
        )

    def table(self):
        p = self.p
        column, plane, sibling = p.peers()
        every = slice(None)
        first = [(i, (p.z, p.c, p.y, p.x), column[i], ((p.z + 3 - i) % 4, p.c, p.y, p.x)) for i in range(3)]
        far = [(p.y, 1 - p.x), (1 - p.y, p.x), (1 - p.y, 1 - p.x)]
        second = [(3 + i, (every, p.c, p.y, p.x), plane[i], (every, p.c) + far[i]) for i in range(3)]
        third = [(6, (every, p.c, every, every), sibling, (every, 1 - p.c, every, every))]
        return first, second, third

    def step(self, s):
        hops = self.table()
        if s > 0:
            for i, _, dev, came in hops[s - 1]:
                self.copy(i, came, dev).wait_recv()
        if s < 3:
            for i, idx, dev, _ in hops[s]:
                self.copy(i, idx, dev).start()

    def finish(self):
        for hop in self.table():
            for i, idx, dev, _ in hop:
                self.copy(i, idx, dev).wait_send()


class SmallReduce:
    def __init__(self, place, buf, land, ssem, rsem, k, final):
        self.p, self.buf, self.land, self.ssem, self.rsem, self.k = place, buf, land, ssem, rsem, k
        self.final = final

    def copy(self, i, idx, dst, dev):
        return pltpu.make_async_remote_copy(
            self.buf.at[idx], dst, self.ssem.at[self.k, i], self.rsem.at[self.k, i], device_id=dev, device_id_type=MESH
        )

    def table(self):
        p = self.p
        column, plane, sibling = p.peers()
        every = slice(None)
        core, flat, line = self.land
        far = [(p.y, 1 - p.x), (1 - p.y, p.x), (1 - p.y, 1 - p.x)]
        first = [(0, (every, 1 - p.c, every, every), core, sibling)]
        second = [(1 + i, (every, p.c) + far[i], flat.at[i], plane[i]) for i in range(3)]
        third = [(4 + i, ((p.z + 1 + i) % 4, p.c, p.y, p.x), line.at[i], column[i]) for i in range(3)]
        return first, second, third

    def step(self, s):
        p = self.p
        core, flat, line = self.land
        hops = self.table()
        if s > 0:
            for i, idx, dst, dev in hops[s - 1]:
                self.copy(i, idx, dst, dev).wait_recv()
        if s == 1:
            self.buf[:, p.c, :, :, :, :] += core[...]
        if s == 2:
            self.buf[:, p.c, p.y, p.x, :, :] += flat[0] + flat[1] + flat[2]
        if s < 3:
            for i, idx, dst, dev in hops[s]:
                self.copy(i, idx, dst, dev).start()
        else:
            self.final(self.buf[p.z, p.c, p.y, p.x, :, :] + line[0] + line[1] + line[2])

    def finish(self):
        for hop in self.table():
            for i, idx, dst, dev in hop:
                self.copy(i, idx, dst, dev).wait_send()


def small_landing(rows, cols):
    return [
        pltpu.VMEM((4, 2, 2, rows, cols), F32), pltpu.VMEM((3, 4, rows, cols), F32), pltpu.VMEM((3, rows, cols), F32)
    ]


def landing(rows, cols, dtype):
    return [
        pltpu.VMEM((4, 2, 2, rows, cols), dtype),
        pltpu.VMEM((2, 2, rows, cols), dtype),
        pltpu.VMEM((2, 2, rows, cols), dtype),
        pltpu.VMEM((2, rows, cols), dtype),
        pltpu.VMEM((2, rows, cols), dtype),
        pltpu.VMEM((3, rows, cols), dtype),
        pltpu.VMEM((3, rows, cols), dtype),
    ]


def pack48(block):
    wide = block.astype(F32)
    return jnp.concatenate([wide[:, :HALF], wide[:, HALF:]], axis=0).astype(BF)


def iota(shape, dim):
    return lax.broadcasted_iota(jnp.int32, shape, dim)


def onehot(cond):
    return jnp.where(cond, 1.0, 0.0).astype(BF)


def ln_hat(v):
    center = v - jnp.mean(v, axis=-1, keepdims=True)
    spread = jnp.mean(center * center, axis=-1, keepdims=True)
    return center * lax.rsqrt(spread + 1e-06)


def fold(v):
    total = v[0:8]
    for i in range(1, v.shape[0] // 8):
        total = total + v[8 * i:8 * i + 8]
    return total


def turn(src, step, put):
    frames, patches, width = src.shape
    count = frames * patches
    for h in range(width // 128):
        base = count * (h % 2)
        cols = slice(128 * h, 128 * h + 128)
        for f in range(frames):
            step[pl.ds(base + f, patches, stride=frames), :] = src[f, :, cols].astype(F32)
        put(cols, step[base:base + count, :])


def turn_back(src, step, dst):
    frames, patches, width = dst.shape
    count = frames * patches
    for h in range(width // 128):
        base = count * (h % 2)
        cols = slice(128 * h, 128 * h + 128)
        step[base:base + count, :] = src[:, cols]
        for f in range(frames):
            dst[f, :, cols] = step[pl.ds(base + f, patches, stride=frames), :].astype(BF)


def pick_row(flat, r):
    return mm(onehot(iota((32, 512), 1) == iota((32, 512), 0) * 16 + r), flat)


def spread_bias(rows, n, start, width):
    k = rows.shape[1]
    lane = iota((k, width), 0)
    col = iota((k, width), 1) + start
    grid = mm(rows.astype(BF), onehot((col % n == lane) & (lane < n)))
    dev = iota((32, width), 0)
    mine = (iota((32, width), 1) + start) // n == dev
    return jnp.sum(jnp.where(mine, grid, 0.0), axis=0, keepdims=True)


def softmax_pair(qs, k, bias):
    scores = mm_nt(qs, k) * 0.125 + bias
    top = jnp.max(scores, axis=-1, keepdims=True)
    e = jnp.exp(scores - top)
    return e / jnp.sum(e, axis=-1, keepdims=True)


def group_start(g, tokens):
    return pl.multiple_of(jnp.minimum(g * GROUP, tokens - GROUP), 16)


def fill_mask(mask_ref, frames):
    shape = mask_ref.shape
    row = iota(shape, 0) % GROUP
    mask_ref[...] = jnp.where(row // frames == iota(shape, 1) // frames, 0.0, -1e30)


F_SEQ = (
    10, 30, 0, 20, "IO", 11, 31, 1, 21, 12, 40, 32, 22, 50, 2, 13, 60, 41, 33, 80, 3, 23, "PM", 90, 14, 51, 61, 42,
    91, 70, 24, 15, 34, 52, "XH", 43, 92, 62, 81, 16, "R0", 71, 53, 25, 93, "MV", "LN", 35, "GB", 26, 82, 44, "R1",
    ("QK", 0,), 36, 72, "R2", 63, ("QK", 1,), 54, ("QK", 2,), 45, ("AT", 0, 1), ("AT", 1, 2), ("AT", 2, 3), 64, 73,
    ("AT", 3, 4), ("AT", 4, 5), 83, ("AT", 5, 6), 46, "R3", ("AT", 6, 7), ("AT", 7, 8), ("AT", 8, 9), ("AT", 9, 10),
    55, ("AT", 10, 11), "PR", "L2", 56, "R4", ("UP", 0,), 65, ("UP", 1,), 74, ("UP", 2,), 66, "R5", 84, ("UP", 3,),
    ("UP", 4,), ("UP", 5,), ("DG", 0,), 75, ("DG", 1,), ("DG", 2,), ("DG", 3,), ("DG", 4,), ("DG", 5,), 76,
    ("DG", 6,), 85, "R6", "DN0", ("DG", 7,), 86, "R7", "DN1",
)


F_ROWS = ((0, 48), (48, 48), (96, 48), (144, 48), (192, 96), (288, 96), (384, 96), (480, 96))


def f_kernel(
    x_hbm, og_hbm, code_ref, gated_ref, qv_ref, pb_ref, ub_ref, db_ref, mb_ref, mw_ref, qw_ref, pw_ref, uw_ref, dw_ref,
    bo_hbm, xt_hbm, ogt_hbm, n1_hbm, qkv_hbm, att_hbm, br_hbm, mid_hbm, n2_hbm, dg_hbm, gp_hbm, gb_hbm,
    wq_hbm, wp_hbm, wu_hbm, wd_hbm, mod_out, gmy_out, mwp_out,
    gbuf, pm, pbuf, l0, l1, l2, dbuf,
    wq, wp, wu, wd, x_v, og_v, n_v, qkv, att, br, mid, act, gpt, raw, gb, amask, bq, bp, bu, bd, acc, step, sm,
    gs, gr, ps, pr, lsem, gpsem, dsem,
):
    p = Place()
    tokens, width = x_v.shape
    rows_of = [slice(SHARD, SMALL)] + [slice(a, a + n) for a, n in F_ROWS]
    gath = [
        (Gather if k else SmallGather)(p, gbuf, gs, gr, k, pl.ds(r.start, r.stop - r.start)) for k, r in enumerate(rows_of)
    ]
    loads = [pltpu.make_async_copy(h.at[0], raw.at[i], lsem.at[i]) for i, h in enumerate((x_hbm, og_hbm))]
    for cp in loads:
        cp.start()
    outs = []
    saved = []

    def save(src, dst):
        cp = pltpu.make_async_copy(src, dst, lsem.at[2 + len(saved)])
        cp.start()
        outs.append(cp)
        saved.append(cp)
        return cp

    def finish(cp):
        cp.wait()
        outs[:] = [o for o in outs if o is not cp]

    own = (p.z, p.c, p.y, p.x)
    weight = (code_ref[0].astype(F32) + 1.0) * 0.25
    sm[...] = jnp.zeros_like(sm)
    sm[0:1, :] = gated_ref[:, :HALF].astype(F32)
    sm[1:2, :] = gated_ref[:, HALF:].astype(F32)
    for i, ref in enumerate((qv_ref, pb_ref, ub_ref, db_ref, mb_ref)):
        sm[2 + i:3 + i, 0:ref.shape[1]] = ref[...].astype(F32)
    gbuf[own + (slice(SHARD, SMALL), slice(None))] = sm[...].astype(BF)
    for b in range(3):
        gbuf[own + (slice(48 * b, 48 * b + 48), slice(None))] = pack48(qw_ref[:, width * b:width * b + width])
    gbuf[own + (slice(144, 192), slice(None))] = pack48(pw_ref[...])
    for b in range(4):
        gbuf[own + (slice(192 + 48 * b, 240 + 48 * b), slice(None))] = pack48(uw_ref[:, width * b:width * b + width])
    gbuf[own + (slice(384, 480), slice(None))] = dw_ref[:, :HALF]
    gbuf[own + (slice(480, 576), slice(None))] = dw_ref[:, HALF:]
    p.greet()

    frames = x_hbm.shape[1]

    def final_mod(total):
        for m in range(6):
            for j in range(6):
                mod_out[m:m + 1, 128 * j:128 * j + 128] = total[6 * m + j:6 * m + j + 1, :]

    red = SmallReduce(p, pbuf, (l0, l1, l2), ps, pr, 0, final_mod)

    def small_work():
        fill_mask(amask, frames)
        flat = gbuf[:, :, :, :, SHARD:SMALL, :].reshape(512, HALF)
        gated = jnp.concatenate([pick_row(flat, 0), pick_row(flat, 1)], axis=1).astype(BF)
        sel = onehot((iota((width, 128), 0) == p.me * 24 + iota((width, 128), 1)) & (iota((width, 128), 1) < 24))
        gmy = mm(gated, sel).astype(BF)
        gmy_out[...] = gmy
        pad = jnp.zeros((8, width), F32)
        for m in range(6):
            cols = slice(width * m, width * m + width)
            part = jnp.concatenate([mw_ref[:, cols].astype(F32), pad], axis=0).astype(BF)
            mwp_out[:, cols] = part
            prod = mm(gmy[:, :32], part)
            for j in range(6):
                pm[32 * (6 * m + j):32 * (6 * m + j) + 32, :] = prod[:, 128 * j:128 * j + 128]

        @pl.loop(0, 32)
        def _(d):
            for j in range(36):
                pbuf[d // 8, (d // 4) % 2, (d // 2) % 2, d % 2, j:j + 1, :] = pm[pl.ds(32 * j + d, 1), :]
            pbuf[d // 8, (d // 4) % 2, (d // 2) % 2, d % 2, 36:40, :] = jnp.zeros((4, 128), F32)

    def biases():
        flat = gbuf[:, :, :, :, SHARD:SMALL, :].reshape(512, HALF)
        qv, prj, up, dn, md = (pick_row(flat, r) for r in (2, 3, 4, 5, 6))
        bq[:, 0:width] = spread_bias(qv[:, :128], 48, 0, width)
        bq[:, width:2 * width] = jnp.zeros((1, width), F32)
        bq[:, 2 * width:] = spread_bias(qv[:, :128], 48, width, width)
        bp[...] = spread_bias(prj[:, :128], 24, 0, width)
        bd[...] = spread_bias(dn[:, :128], 24, 0, width)
        for m in range(4):
            bu[:, width * m:width * m + width] = spread_bias(up[:, :128], 96, width * m, width)
        for m in range(6):
            mod_out[m:m + 1, :] += spread_bias(md[:, :256], 144, width * m, width)

    def unpack(b, dst, col):
        @pl.loop(0, 16)
        def _(i):
            src = (i // 4, (i // 2) % 2, i % 2)
            one = gbuf[src + (0, slice(48 * b, 48 * b + 48), slice(None))].astype(F32)
            two = gbuf[src + (1, slice(48 * b, 48 * b + 48), slice(None))].astype(F32)
            at = pl.ds(pl.multiple_of(i * 48, 16), 48)
            dst[at, col:col + HALF] = jnp.concatenate([one[:24], two[:24]], axis=0).astype(BF)
            dst[at, col + HALF:col + 2 * HALF] = jnp.concatenate([one[24:], two[24:]], axis=0).astype(BF)

    def unpack_down(h):
        @pl.loop(0, 32)
        def _(d):
            wd[pl.ds(pl.multiple_of(d * 96, 16), 96), HALF * h:HALF * h + HALF] = gbuf[
                d // 8, (d // 4) % 2, (d // 2) % 2, d % 2, 384 + 96 * h:480 + 96 * h, :
            ]

    def rows_loop(body):
        @pl.loop(0, tokens // 48, unroll=3)
        def _(i):
            body(pl.ds(pl.multiple_of(i * 48, 16), 48))

    def put_x(cols, value):
        mid[:, cols] = value
        x_v[:, cols] = value.astype(BF)

    def put_og(cols, value):
        og_v[:, cols] = value.astype(BF)

    def first_hat(at):
        mid[at, :] = ln_hat(mid[at, :])

    def first_norm(at):
        n_v[at, :] = (mid[at, :] * (1.0 + mod_out[1:2, :]) + mod_out[0:1, :]).astype(BF)

    def second_norm(at):
        n_v[at, :] = (ln_hat(mid[at, :]) * (1.0 + mod_out[4:5, :]) + mod_out[3:4, :]).astype(BF)

    def qkv_block(i):
        cols = slice(width * i, width * i + width)
        qkv[:, cols] = (mm(n_v[...], wq[:, cols]) + bq[:, cols]).astype(BF)

    def attention(first, last):
        low_lane = iota((GROUP, 128), 1) < 64

        @pl.loop(first, last)
        def _(g):
            rows = pl.ds(group_start(g, tokens), GROUP)
            for h in range(width // 128):
                q = qkv[rows, 128 * h:128 * h + 128]
                k = qkv[rows, width + 128 * h:width + 128 * h + 128]
                v = qkv[rows, 2 * width + 128 * h:2 * width + 128 * h + 128]
                zero = jnp.zeros_like(q)
                qs = jnp.concatenate([jnp.where(low_lane, q, zero), jnp.where(low_lane, zero, q)], axis=0)
                probs = softmax_pair(qs, k, amask[...]).astype(BF)
                both = mm(probs, v)
                att[rows, 128 * h:128 * h + 128] = jnp.where(low_lane, both[:GROUP], both[GROUP:]).astype(BF)

    def proj():
        branch = mm(att[...], wp[...]) + bp[...]
        br[...] = branch.astype(BF)
        mid[...] = x_v[...].astype(F32) + mod_out[2:3, :] * branch

    def second_cot(at):
        low = (og_v[at, :].astype(F32) * weight * mod_out[5:6, :]).astype(BF)
        gb[at, :] = low
        acc[...] += fold(low.astype(F32))

    def dg_copy(j):
        return pltpu.make_async_copy(dbuf.at[j % 2], dg_hbm.at[j // 2, j % 2], dsem.at[j % 2])

    def down_grad(j):
        if j >= 2:
            dg_copy(j - 2).wait()
        grad = mm_tn(act[:, HALF * j:HALF * j + HALF], gb[...])
        for dd in range(4):
            part = grad[96 * dd:96 * dd + 96].astype(BF)
            dbuf[j % 2, dd // 2, dd % 2, 0:96, :] = part[:, :HALF]
            dbuf[j % 2, dd // 2, dd % 2, 96:192, :] = part[:, HALF:]
        dg_copy(j).start()

    def gp_copy(j):
        return pltpu.make_async_copy(gpt.at[j % 2], gp_hbm.at[:, pl.ds(512 * j, 512)], gpsem.at[j % 2])

    def up_tile(j):
        cols = slice(512 * j, 512 * j + 512)
        if j >= 2:
            gp_copy(j - 2).wait()

        @pl.loop(0, 3)
        def _(m):
            at = pl.ds(pl.multiple_of(m * 336, 16), 336)
            hid = mm(n_v[at, :], wu[:, cols]) + bu[:, cols]
            sq = hid * hid
            slope_in = 0.7978845608 + (0.7978845608 * 0.044715) * sq
            half = 0.5 + 0.5 * jnp.tanh(hid * slope_in)
            act[at, cols] = (hid * half).astype(BF)
            rate = 2.0 * 0.7978845608 + (6.0 * 0.7978845608 * 0.044715) * sq
            gpt[j % 2, at, :] = (half + (hid * rate) * (half - half * half)).astype(BF)
        gp_copy(j).start()

    def down_half(h):
        cols = slice(HALF * h, HALF * h + HALF)

        def body(i, gg):
            at = pl.ds(pl.multiple_of(i * 336, 16), 336)
            branch = mm(act[at, :], wd[:, cols]) + bd[:, cols]
            gate = mod_out[5:6, cols]
            mid[at, cols] += gate * branch
            cot = og_v[at, cols].astype(F32) * weight
            return gg + jnp.sum(cot * branch, axis=0, keepdims=True)

        mod_out[6:7, cols] = lax.fori_loop(0, tokens // 336, body, jnp.zeros((1, HALF), F32))

    n1_out = []

    def do(tag, *span):
        if isinstance(tag, int):
            item = red if tag >= 90 else gath[tag // 10]
            item.step(tag % 10)
        elif tag == "PM":
            small_work()
        elif tag == "IO":
            loads[1].wait()
            turn(raw.at[1], step, put_og)
            save(og_v, ogt_hbm)
        elif tag == "XH":
            loads[0].wait()
            turn(raw.at[0], step, put_x)
            rows_loop(first_hat)
            save(x_v, xt_hbm)
        elif tag == "MV":
            mod_out[6:8, :] = jnp.zeros((2, width), F32)
            acc[...] = jnp.zeros_like(acc)
            biases()
        elif tag in ("R0", "R1", "R2", "R3"):
            b = int(tag[1])
            if b < 3:
                unpack(b, wq, width * b)
            else:
                unpack(b, wp, 0)
                save(wp, wp_hbm)
            if b == 2:
                save(wq, wq_hbm)
        elif tag == "LN":
            rows_loop(first_norm)
            n1_out.append(save(n_v, n1_hbm))
        elif tag == "QK":
            qkv_block(*span)
            if span == (2,):
                save(qkv, qkv_hbm)
        elif tag == "AT":
            attention(*span)
            if span[1] == 11:
                save(att, att_hbm)
        elif tag == "PR":
            proj()
            save(br, br_hbm)
            n1_out.append(save(mid, mid_hbm))
            finish(n1_out[0])
        elif tag == "L2":
            rows_loop(second_norm)
            save(n_v, n2_hbm)
        elif tag in ("R4", "R5"):
            b = 4 if tag == "R4" else 6
            unpack(b, wu, width * (b - 4))
            unpack(b + 1, wu, width * (b - 3))
            if tag == "R5":
                save(wu, wu_hbm)
        elif tag == "UP":
            up_tile(*span)
        elif tag == "GB":
            rows_loop(second_cot)
            mod_out[7:8, :] = jnp.sum(acc[...], axis=0, keepdims=True)
            save(gb, gb_hbm)
        elif tag == "DG":
            down_grad(*span)
        elif tag in ("R6", "R7"):
            unpack_down(int(tag[1]) - 6)
            if tag == "R7":
                save(wd, wd_hbm)
        elif tag == "DN0":
            finish(n1_out[1])
            down_half(0)
        elif tag == "DN1":
            down_half(1)
            turn_back(mid, step, raw.at[0])
            save(raw.at[0], bo_hbm.at[0])

    for tag in F_SEQ:
        do(*(tag if isinstance(tag, tuple) else (tag,)))
    for j in (4, 5):
        gp_copy(j).wait()
    for j in (6, 7):
        dg_copy(j).wait()
    for cp in outs:
        cp.wait()
    for g in gath:
        g.finish()
    red.finish()


def forward(tokens, out_grad, codes, *rest):
    _, frames, patches, d = tokens.shape
    t, hid = frames * patches, rest[9].shape[1]
    s = jax.ShapeDtypeStruct
    outs = [
        s(tokens.shape, BF), s((t, d), BF), s((t, d), BF), s((t, d), BF), s((t, 3 * d), BF), s((t, d), BF), s((t, d), BF), s((t, d), F32), s((t, d), BF),
        s((4, 2, 2, 2, 192, HALF), BF), s((t, hid), BF), s((t, d), BF),
        s((d, 3 * d), BF), s((d, d), BF), s((d, hid), BF), s((hid, d), BF),
        s((8, d), F32), s((32, 128), BF), s((32, 6 * d), BF),
    ]
    v = pltpu.VMEM
    scratch = [
        v((4, 2, 2, 2, SMALL, HALF), BF), v((6 * d // 128 * 32, 128), F32), v((4, 2, 2, 2, 40, 128), F32), *small_landing(40, 128), v((2, 2, 2, 192, HALF), BF),
        v((d, 3 * d), BF), v((d, d), BF), v((d, hid), BF), v((hid, d), BF),
        v((t, d), BF), v((t, d), BF), v((t, d), BF), v((t, 3 * d), BF), v((t, d), BF), v((t, d), BF), v((t, d), F32),
        v((t, hid), BF), v((2, t, 512), BF), v((2, frames, patches, d), BF), v((t, d), BF), v((2 * GROUP, GROUP), F32),
        v((1, 3 * d), F32), v((1, d), F32), v((1, hid), F32), v((1, d), F32), v((8, d), F32), v((2 * t, 128), F32), v((16, HALF), F32),
        pltpu.SemaphoreType.DMA((9, 11)), pltpu.SemaphoreType.DMA((9, 11)),
        pltpu.SemaphoreType.DMA((1, 11)), pltpu.SemaphoreType.DMA((1, 11)),
        pltpu.SemaphoreType.DMA((24,)), pltpu.SemaphoreType.DMA((2,)), pltpu.SemaphoreType.DMA((2,)),
    ]
    return pl.pallas_call(
        f_kernel,
        out_shape=outs,
        in_specs=[ANY, ANY, pl.BlockSpec(memory_space=pltpu.SMEM)] + [VMEM] * len(rest),
        out_specs=[ANY] * 16 + [VMEM] * 3,
        scratch_shapes=scratch,
        compiler_params=pltpu.CompilerParams(collective_id=0, has_side_effects=True, vmem_limit_bytes=VMEM_LIMIT),
        cost_estimate=pl.CostEstimate(flops=15 * 10**9, bytes_accessed=70 * 10**6, transcendentals=4 * 10**6),
        name="forward",
    )(tokens, out_grad, codes, *rest)


B_SEQ = (
    "LD", 0, "ST", 10, ("A", 0,), ("A", 1,), ("A", 2,), ("A", 3,), ("A", 4,), ("A", 5,), "U0", ("N0", 0,), 11, "U1",
    20, 1, ("N0", 1,), "U2", "U3", 21, 30, ("N0", 2,), 12, "L2", "PA", ("AB", 0, 1), ("AB", 1, 2), ("AB", 2, 3),
    ("AB", 3, 4), 22, 2, ("AB", 4, 5), ("AB", 5, 6), 13, 31, "PG", 23, 40, ("AB", 6, 7), ("AB", 7, 8), ("AB", 8, 9),
    24, 3, 41, ("AB", 9, 10), ("AB", 10, 11), "Q0", 32, 50, ("N1", 0,), "Q1", 4, 51, 14, 60, 42, ("N1", 1,),
    ("N1", 2,), 61, "Q2", 52, 70, 33, "L1", "MB", 90, 71, 34, 5, 15, 43, "BI", 53, 25, 91, 62, "BB", 35, 92, 80, 72,
    63, 54, 93, "GM", 100, 16, 6, 73, 64, 44, 81, "TG", 101, 55, 74, 36, 65, 82, 26, 45, 56, 75, 102, 66, 83, 46, 76,
    103, "CO",
)
CHUNKS = ((384, 96), (480, 96), (192, 96), (288, 96), (144, 48), (0, 48), (48, 48), (96, 48))


def ln_parts(v):
    center = v - jnp.mean(v, axis=-1, keepdims=True)
    spread = jnp.mean(center * center, axis=-1, keepdims=True)
    inv = lax.rsqrt(spread + 1e-06)
    return center * inv, inv


def ln_back(g, hat, inv, scale):
    dh = g * (1.0 + scale)
    return inv * (dh - jnp.mean(dh, axis=-1, keepdims=True) - hat * jnp.mean(dh * hat, axis=-1, keepdims=True))


def split_bias(vec, n):
    width = vec.shape[1]
    mine = iota((32, width), 1) // n == iota((32, width), 0)
    lane = iota((width, 128), 1)
    ones = jnp.where((iota((width, 128), 0) % n == lane) & (lane < n), 1.0, 0.0)
    return jnp.dot(jnp.where(mine, vec, 0.0), ones, precision=lax.Precision.HIGHEST, preferred_element_type=F32)


def b_kernel(
    x_hbm, og_hbm, code_ref, mod_ref, gmy_ref, mwp_ref,
    n1_hbm, qkv_hbm, att_hbm, br_hbm, mid_hbm, n2_hbm, dg_hbm, gp_hbm, gb_hbm, wq_hbm, wp_hbm, wu_hbm, wd_hbm,
    tg_hbm, gq_out, gp_out, gu_out, gd_out, bias_out, gmw_out, gmb_out, cg_out,
    gbuf, k0, k1, k2, k3, k4, k5, k6, sbuf, t0, t1, t2, mbuf, cbuf, stage,
    wa, wu, gh, gb, nb, mid, gn, br, amask, vec, accs, raw, step,
    rs, rr, ts, tr, gs, gr, lsem,
):
    p = Place()
    tokens, width = gb.shape
    frames = raw.shape[0]
    cw = (code_ref[0].astype(F32) + 1.0) * 0.25
    pending = {}

    def load(name, i, src, dst):
        pending[name] = pltpu.make_async_copy(src, dst, lsem.at[i])
        pending[name].start()

    def put48(dst_out, b, total):
        dst_out[:, width * b:width * b + HALF] = total[:24]
        dst_out[:, width * b + HALF:width * b + width] = total[24:48]

    def finals(k):
        def go(total):
            if k < 2:
                gd_out[:, HALF * k:HALF * k + HALF] = total
            elif k < 4:
                put48(gu_out, 2 * (k - 2), total[:48])
                put48(gu_out, 2 * (k - 2) + 1, total[48:])
            elif k == 4:
                put48(gp_out, 0, total)
            else:
                put48(gq_out, k - 5, total)
        return go

    land = (k0, k1, k2, k3, k4, k5, k6)
    reds = [Reduce(p, gbuf, land, rs, rr, k, pl.ds(a, n), finals(k)) for k, (a, n) in enumerate(CHUNKS)]

    def bias_final(total):
        bias_out[...] = total

    bred = SmallReduce(p, sbuf, (t0, t1, t2), ts, tr, 0, bias_final)
    mgath = SmallGather(p, mbuf, gs, gr, 0, pl.ds(0, 16))
    cgath = SmallGather(p, cbuf, gs, gr, 1, pl.ds(0, 32))

    def weight_grad(left_ref, right, b):
        @pl.loop(0, 2)
        def _(m):
            at = pl.ds(pl.multiple_of(m * HALF, HALF), HALF)
            grad = mm_tn(left_ref[:, at], right[...])
            for dd in range(16):
                gbuf[2 * m + dd // 8, dd // 4 % 2, dd // 2 % 2, dd % 2, 48 * b:48 * b + 48, :] = pack48(
                    grad[24 * dd:24 * dd + 24]
                )

    def act_grad(j):
        cols = slice(512 * j, 512 * j + 512)
        low = (mm_nt(gb[...], wa[cols, :]) * gh[:, cols].astype(F32)).astype(BF)
        gh[:, cols] = low
        vec[0:1, cols] = jnp.sum(low.astype(F32), axis=0, keepdims=True)

    def norm2_back():
        scale, gate = mod_ref[4:5, :], mod_ref[2:3, :]
        accs[...] = jnp.zeros_like(accs)

        @pl.loop(0, tokens // 48, unroll=3)
        def _(i):
            at = pl.ds(pl.multiple_of(i * 48, 16), 48)
            g = gn[at, :]
            hat, inv = ln_parts(mid[at, :])
            gm = gb[at, :].astype(F32) * cw + ln_back(g, hat, inv, scale)
            gn[at, :] = gm
            low = (gm * gate).astype(BF)
            gh[at, 3 * width:4 * width] = low
            accs[0:8, :] += fold(g)
            accs[8:16, :] += fold(g * hat)
            accs[16:24, :] += fold(gm * br[at, :].astype(F32))
            accs[24:32, :] += fold(low.astype(F32))

        for i, row in enumerate((3, 4, 2)):
            vec[1 + row:2 + row, 0:width] = jnp.sum(accs[8 * i:8 * i + 8, :], axis=0, keepdims=True)
        vec[8:9, 0:width] = jnp.sum(accs[24:32, :], axis=0, keepdims=True)

    def norm1_back():
        scale = mod_ref[1:2, :]
        accs[...] = jnp.zeros_like(accs)

        @pl.loop(0, tokens // 48, unroll=3)
        def _(i):
            at = pl.ds(pl.multiple_of(i * 48, 16), 48)
            g = mid[at, :]
            hat, inv = ln_parts(br[at, :].astype(F32))
            gn[at, :] += ln_back(g, hat, inv, scale)
            accs[0:8, :] += fold(g)
            accs[8:16, :] += fold(g * hat)

        for i in range(2):
            vec[1 + i:2 + i, 0:width] = jnp.sum(accs[8 * i:8 * i + 8, :], axis=0, keepdims=True)

    def attention_back(first, last):
        low_lane = iota((GROUP, 128), 1) < 64

        @pl.loop(first, last)
        def _(g):
            start = group_start(g, tokens)
            rows = pl.ds(start, GROUP)
            for h in range(width // 128):
                q, k, v = (gh[rows, width * i + 128 * h:width * i + 128 * h + 128] for i in range(3))
                ga = gb[rows, 128 * h:128 * h + 128]
                zero = jnp.zeros_like(q)
                qs = jnp.concatenate([jnp.where(low_lane, q, zero), jnp.where(low_lane, zero, q)], axis=0)
                gas = jnp.concatenate([jnp.where(low_lane, ga, zero), jnp.where(low_lane, zero, ga)], axis=0)
                scores = mm_nt(k, qs) * 0.125 + amask[...]
                e = jnp.exp(scores - jnp.max(scores, axis=0, keepdims=True))
                probs = e * (1.0 / jnp.sum(e, axis=0, keepdims=True))
                gprobs = mm_nt(v, gas)
                gv = mm(probs.astype(BF), gas)
                inner = jnp.sum(probs * gprobs, axis=0, keepdims=True)
                gsc = (probs * (gprobs - inner)).astype(BF)
                gk = mm(gsc, qs) * 0.125
                both = mm_tn(gsc, k)
                gq = jnp.where(low_lane, both[:GROUP], both[GROUP:]) * 0.125
                for i, g_part in enumerate((gq, gk, gv)):
                    at = pl.ds(pl.multiple_of(start + i * tokens, 16), GROUP)
                    wu[at, 128 * h:128 * h + 128] = g_part.astype(BF)

    def qkv_bias():
        accs[...] = jnp.zeros_like(accs)

        @pl.loop(0, tokens // 48, unroll=3)
        def _(i):
            at = pl.ds(pl.multiple_of(i * 48, 16), 48)
            accs[0:8, :] += fold(wu[at, :].astype(F32))
            accs[8:16, :] += fold(wu[pl.ds(pl.multiple_of(2 * tokens + i * 48, 16), 48), :].astype(F32))

        for i in range(2):
            vec[9:10, width * i:width * i + width] = jnp.sum(accs[8 * i:8 * i + 8, :], axis=0, keepdims=True)

    def bias_blocks():
        stage[0:32, :] = split_bias(vec[9:10, 0:2 * width], 48)
        stage[32:64, :] = split_bias(vec[8:9, 0:width], 24)
        stage[64:96, :] = split_bias(vec[0:1, :], 96)
        stage[96:128, :] = split_bias(vec[7:8, 0:width], 24)

        @pl.loop(0, 32)
        def _(d):
            at = (d // 8, (d // 4) % 2, (d // 2) % 2, d % 2)
            for r in range(4):
                sbuf[at + (slice(r, r + 1), slice(None))] = stage[pl.ds(32 * r + d, 1), :]
            sbuf[at + (slice(4, 8), slice(None))] = jnp.zeros((4, 128), F32)

    def mod_block():
        rows = []
        for m in range(6):
            row = vec[1 + m:2 + m, 0:width]
            rows += [row[:, :HALF], row[:, HALF:]]
        rows.append(jnp.zeros((4, HALF), F32))
        mbuf[p.z, p.c, p.y, p.x, :, :] = jnp.concatenate(rows, axis=0).astype(BF)

    def mod_grads():
        flat = mbuf[...].reshape(512, HALF)
        gmy = gmy_ref[:, 0:32]
        cond = jnp.zeros((32, 32), F32)
        gmb_out[:, 6 * width:] = jnp.zeros((1, 256), F32)
        for i in range(12):
            cols = slice(HALF * i, HALF * i + HALF)
            every = pick_row(flat, i)
            low = every.astype(BF)
            gmw_out[:, cols] = mm_tn(gmy, low)[:24]
            gmb_out[:, cols] = jnp.sum(every, axis=0, keepdims=True)
            cond = cond + mm_nt(low, mwp_ref[:, cols])
        mine = (p.z, p.c, p.y, p.x)
        cbuf[mine + (slice(None), slice(None))] = jnp.zeros((32, 128), F32)
        cbuf[mine + (slice(None), slice(0, 32))] = cond

    def cond_out():
        @pl.loop(0, 32)
        def _(d):
            cg_out[pl.ds(d, 1), :] = cbuf[d // 8, (d // 4) % 2, (d // 2) % 2, d % 2, pl.ds(p.me, 1), :]

    def do(tag, *span):
        if isinstance(tag, int):
            (reds + [bred, mgath, cgath])[tag // 10].step(tag % 10)
        elif tag == "MB":
            mod_block()
        elif tag == "BB":
            bias_blocks()
        elif tag == "LD":
            rows = pl.ds(384, 192)
            load("far", 16, dg_hbm.at[:, 1 - p.c], gbuf.at[:, 1 - p.c, :, :, rows, :])
            load("near", 17, dg_hbm.at[:, p.c], gbuf.at[:, p.c, :, :, rows, :])
            load("gb", 0, gb_hbm, gb)
            load("wd", 1, wd_hbm, wa)
            load("gp", 2, gp_hbm, gh)
            load("n2", 3, n2_hbm, nb)
            for i in range(4):
                load("u%d" % i, 12 + i, wu_hbm.at[:, pl.ds(width * i, width)], wu.at[pl.ds(width * i, width), :])
            load("mid", 5, mid_hbm, mid)
            load("br", 6, br_hbm, br)
            p.greet()
            pending["far"].wait()
        elif tag == "ST":
            vec[...] = jnp.zeros_like(vec)
            vec[6:7, 0:width] = mod_ref[6:7, :]
            vec[7:8, 0:width] = mod_ref[7:8, :]
            shape = amask.shape
            same = iota(shape, 0) // frames == iota(shape, 1) % GROUP // frames
            amask[...] = jnp.where(same, 0.0, -1e30)
            pending["near"].wait()
        elif tag == "A":
            if span == (0,):
                pending["gb"].wait()
                pending["wd"].wait()
                pending["gp"].wait()
            act_grad(*span)
            if span == (5,):
                load("og", 0, og_hbm, gb)
                for i in range(3):
                    load("w%d" % i, 7 + i, wq_hbm.at[:, pl.ds(width * i, width)], wa.at[pl.ds(width * i, width), :])
                load("wp", 10, wp_hbm, wa.at[pl.ds(3 * width, width), :])
        elif tag[0] == "U":
            i = int(tag[1])
            if i == 0:
                pending["n2"].wait()
            weight_grad(nb, gh.at[:, pl.ds(width * i, width)], 4 + i)
            if i == 3:
                load("att", 3, att_hbm, nb)
        elif tag == "N0":
            j = span[0]
            if j == 0:
                for i in range(4):
                    pending["u%d" % i].wait()
            total = mm_nt(gh[:, 0:width], wu[256 * j:256 * j + 256, :])
            for i in (1, 2, 3):
                total = total + mm_nt(
                    gh[:, width * i:width * i + width], wu[width * i + 256 * j:width * i + 256 * j + 256, :]
                )
            gn[:, 256 * j:256 * j + 256] = total
            if j == 2:
                load("qkv", 2, qkv_hbm, gh.at[:, pl.ds(0, 3 * width)])
        elif tag == "L2":
            for name in ("mid", "br", "og"):
                pending[name].wait()
            norm2_back()
            load("x", 6, x_hbm, br)
        elif tag == "PG":
            pending["att"].wait()
            weight_grad(nb, gh.at[:, pl.ds(3 * width, width)], 3)
            load("n1", 3, n1_hbm, nb)
        elif tag == "PA":
            for name in ("w0", "w1", "w2", "wp"):
                pending[name].wait()
            gb[...] = mm_nt(gh[:, 3 * width:4 * width], wa[3 * width:4 * width, :]).astype(BF)
        elif tag == "AB":
            if span[0] == 0:
                pending["qkv"].wait()
            attention_back(*span)
        elif tag in ("Q0", "Q1", "Q2"):
            if tag == "Q0":
                pending["n1"].wait()
            i = int(tag[1])
            weight_grad(nb, wu.at[pl.ds(tokens * i, tokens), :], i)
        elif tag == "N1":
            j = span[0]
            total = mm_nt(wu[0:tokens, :], wa[256 * j:256 * j + 256, :])
            for i in (1, 2):
                total = total + mm_nt(
                    wu[tokens * i:tokens * i + tokens, :], wa[width * i + 256 * j:width * i + 256 * j + 256, :]
                )
            mid[:, 256 * j:256 * j + 256] = total
        elif tag == "L1":
            pending["x"].wait()
            norm1_back()
        elif tag == "TG":
            turn_back(gn, step, raw)
            load("tg", 11, raw, tg_hbm.at[0])
        elif tag == "BI":
            qkv_bias()
        elif tag == "GM":
            mod_grads()
        elif tag == "CO":
            cond_out()

    for tag in B_SEQ:
        do(*(tag if isinstance(tag, tuple) else (tag,)))
    pending["tg"].wait()
    for item in reds + [bred, mgath, cgath]:
        item.finish()


def backward(shape, xt, ogt, codes, mod, gmy, mwp, n1, qkv, att, br, mid, n2, dg, gp, gb, wq, wp, wu, wd):
    t, d = xt.shape
    hid = gp.shape[1]
    s = jax.ShapeDtypeStruct
    outs = [
        s(shape, BF), s((24, 3 * d), F32), s((24, d), F32), s((24, hid), F32), s((96, d), F32), s((8, 128), F32),
        s((24, 6 * d), F32), s((1, 6 * d + 256), F32), s((32, 128), F32),
    ]
    v = pltpu.VMEM
    dma = pltpu.SemaphoreType.DMA
    scratch = [
        v((4, 2, 2, 2, SHARD, HALF), BF), *landing(SHARD, HALF, BF),
        v((4, 2, 2, 2, 8, 128), F32), *small_landing(8, 128),
        v((4, 2, 2, 2, 16, HALF), BF), v((4, 2, 2, 2, 32, 128), F32), v((128, 128), F32),
        v((hid, d), BF), v((hid, d), BF), v((t, hid), BF), v((t, d), BF), v((t, d), BF),
        v((t, d), F32), v((t, d), F32), v((t, d), BF), v((GROUP, 2 * GROUP), F32), v((16, hid), F32), v((32, d), F32), v(shape[1:], BF), v((2 * t, 128), F32),
        dma((8, 11)), dma((8, 11)), dma((1, 11)), dma((1, 11)), dma((2, 11)), dma((2, 11)), dma((18,)),
    ]
    return pl.pallas_call(
        b_kernel,
        out_shape=outs,
        in_specs=[ANY, ANY, pl.BlockSpec(memory_space=pltpu.SMEM)] + [VMEM] * 3 + [ANY] * 13,
        out_specs=[ANY] + [VMEM] * 8,
        scratch_shapes=scratch,
        compiler_params=pltpu.CompilerParams(collective_id=1, has_side_effects=True, vmem_limit_bytes=VMEM_LIMIT),
        cost_estimate=pl.CostEstimate(flops=29 * 10**9, bytes_accessed=70 * 10**6, transcendentals=10**6),
        name="backward",
    )(xt, ogt, codes, mod, gmy, mwp, n1, qkv, att, br, mid, n2, dg, gp, gb, wq, wp, wu, wd)


def o_kernel(bias_ref, gmb_ref, cg_ref, slope_ref, *refs):
    srcs, (cond, modb, qvb, projb, upb, downb), dsts, held, sem = refs[:7], refs[7:13], refs[13:20], refs[20:27], refs[27]
    loads = [pltpu.make_async_copy(a, b, sem.at[0, i]) for i, (a, b) in enumerate(zip(srcs, held))]
    stores = [pltpu.make_async_copy(a, b, sem.at[1, i]) for i, (a, b) in enumerate(zip(held, dsts))]
    for cp in loads:
        cp.start()
    p = Place()
    for i, ref in enumerate((qvb, projb, upb, downb)):
        ref[...] = bias_ref[i:i + 1, :ref.shape[1]]
    n = modb.shape[1]
    start = p.me * n
    window = gmb_ref[:, pl.ds(pl.multiple_of(start // 128 * 128, 128), 384)]
    modb[...] = pltpu.roll(window, 384 - start % 128, 1)[:, :n]
    width = cond.shape[1]
    rows = width // 32
    lane, col = iota((128, width), 0), iota((128, width), 1)
    ones = jnp.where((col % rows == lane) & (lane < rows), 1.0, 0.0)
    grid = jnp.dot(cg_ref[...], ones, precision=lax.Precision.HIGHEST, preferred_element_type=F32)
    mine = iota((32, width), 1) // rows == iota((32, width), 0)
    cond[...] = jnp.sum(jnp.where(mine, grid, 0.0), axis=0, keepdims=True) * slope_ref[...]
    for one, two in zip(loads, stores):
        one.wait()
        two.start()
    for cp in stores:
        cp.wait()


def outputs(big, bias, gmb, cg, slope, mod_n):
    d = slope.shape[1]
    s = jax.ShapeDtypeStruct
    small = [s((1, d), F32), s((1, mod_n), F32)] + [s((1, n), F32) for n in (48, 24, 96, 24)]
    return pl.pallas_call(
        o_kernel,
        out_shape=small + [s(a.shape, a.dtype) for a in big],
        in_specs=[VMEM] * 4 + [ANY] * 7,
        out_specs=[VMEM] * 6 + [ANY] * 7,
        scratch_shapes=[pltpu.VMEM(a.shape, a.dtype) for a in big] + [pltpu.SemaphoreType.DMA((2, 7))],
        compiler_params=pltpu.CompilerParams(vmem_limit_bytes=VMEM_LIMIT),
        name="place_outputs",
    )(bias, gmb, cg, slope, *big)


def time_embed(noise_steps, model_width):
    half_width = model_width // 2
    frequency = jnp.exp(-math.log(10000.0) * jnp.arange(half_width, dtype=jnp.float32) / half_width)
    angles = noise_steps.astype(jnp.float32)[:, None] * frequency[None, :]
    return jnp.concatenate([jnp.cos(angles), jnp.sin(angles)], axis=-1)


def fast_local(
    tokens, condition, timesteps, loss_codes, out_grad, mod_weight, mod_bias, qkv_weight, qv_bias,
    proj_weight, proj_bias, up_weight, up_bias, down_weight, down_bias,
):
    cond = condition + time_embed(timesteps, tokens.shape[3])
    gate = jax.nn.sigmoid(cond)
    gated = (cond * gate).astype(BF)
    slope = gate * (1.0 + cond * (1.0 - gate))
    row = lambda a: a[None]
    bo, xt, ogt, n1, qkv, att, br, mid, n2, dg, gp, gb, wq, wp, wu, wd, mod, gmy, mwp = forward(
        tokens, out_grad, loss_codes, gated, row(qv_bias), row(proj_bias), row(up_bias), row(down_bias), row(mod_bias),
        mod_weight, qkv_weight, proj_weight, up_weight, down_weight,
    )
    tg, g_qkv, g_proj, g_up, g_down, bias, g_mod, gb_mod, cg = backward(
        tokens.shape, xt, ogt, loss_codes, mod, gmy, mwp, n1, qkv, att, br, mid, n2, dg, gp, gb, wq, wp, wu, wd
    )
    big = (bo, tg, g_mod, g_qkv, g_proj, g_up, g_down)
    cond_grad, modb, qvb, projb, upb, downb, *big = outputs(big, bias, gb_mod, cg, slope, mod_bias.shape[0])
    bo, tg, g_mod, g_qkv, g_proj, g_up, g_down = big
    return (
        bo, tg, cond_grad, g_mod, modb[0], g_qkv, qvb[0], g_proj, projb[0], g_up, upb[0], g_down, downb[0],
    )


def layernorm(inputs):
    center = inputs - jnp.mean(inputs, axis=-1, keepdims=True)
    spread = jnp.mean(center * center, axis=-1, keepdims=True)
    return center * lax.rsqrt(spread + 1e-06)


def modulate(inputs, shift_part, scale_part):
    return layernorm(inputs) * (1.0 + scale_part) + shift_part


def softmax_last(scores):
    return jax.nn.softmax(scores, axis=-1)


def gelu_tanh(inputs):
    return jax.nn.gelu(inputs, approximate=True)


def product(left_side, right_side):
    return jnp.dot(left_side, right_side, preferred_element_type=jnp.float32)


def column_sum(inputs):
    return jnp.sum(inputs.astype(jnp.float32), axis=0)


def local(
    tokens,
    condition,
    timesteps,
    loss_codes,
    out_grad,
    mod_weight,
    mod_bias,
    qkv_weight,
    qv_bias,
    proj_weight,
    proj_bias,
    up_weight,
    up_bias,
    down_weight,
    down_bias,
):
    gathered = (
        lax.all_gather(mod_weight, ("wide", "narrow"), axis=0, tiled=True),
        lax.all_gather(mod_bias, ("wide", "narrow"), axis=0, tiled=True),
        lax.all_gather(qkv_weight, ("wide", "narrow"), axis=0, tiled=True),
        lax.all_gather(qv_bias, ("wide", "narrow"), axis=0, tiled=True),
        lax.all_gather(proj_weight, ("wide", "narrow"), axis=0, tiled=True),
        lax.all_gather(proj_bias, ("wide", "narrow"), axis=0, tiled=True),
        lax.all_gather(up_weight, ("wide", "narrow"), axis=0, tiled=True),
        lax.all_gather(up_bias, ("wide", "narrow"), axis=0, tiled=True),
        lax.all_gather(down_weight, ("wide", "narrow"), axis=0, tiled=True),
        lax.all_gather(down_bias, ("wide", "narrow"), axis=0, tiled=True),
    )
    (
        mod_full,
        modb_full,
        qkv_full,
        qvb_full,
        proj_full,
        projb_full,
        up_full,
        upb_full,
        down_full,
        downb_full,
    ) = gathered
    frames = tokens.shape[1]
    patches = tokens.shape[2]
    model_width = tokens.shape[3]
    head_count = model_width // HEAD_DIM
    scale_factor = HEAD_DIM ** (-0.5)
    shape_four = (frames, patches, head_count, HEAD_DIM)
    conditioning = condition[0] + time_embed(timesteps, model_width)[0]
    silu_value, silu_back = jax.vjp(jax.nn.silu, conditioning)
    gated = silu_value.astype(jnp.bfloat16)
    modulation = product(gated[None, :], mod_full)[0] + modb_full.astype(jnp.float32)
    shift_first, scale_first, gate_first, shift_second, scale_second, gate_second = jnp.split(
        modulation, 6
    )
    token_rows = tokens[0].reshape(frames * patches, model_width).astype(jnp.float32)
    normed_value, first_norm_back = jax.vjp(modulate, token_rows, shift_first, scale_first)
    normed = normed_value.astype(jnp.bfloat16)
    projected = product(normed, qkv_full)
    queries = (
        (projected[:, :model_width] + qvb_full[:model_width].astype(jnp.float32))
        .astype(jnp.bfloat16)
        .reshape(shape_four)
    )
    keys_all = projected[:, model_width : 2 * model_width].astype(jnp.bfloat16).reshape(shape_four)
    values_all = (
        (projected[:, 2 * model_width :] + qvb_full[model_width:].astype(jnp.float32))
        .astype(jnp.bfloat16)
        .reshape(shape_four)
    )
    scores = (
        jnp.einsum("fphd,gphd->phfg", queries, keys_all, preferred_element_type=jnp.float32)
        * scale_factor
    )
    soft_value, softmax_back = jax.vjp(softmax_last, scores)
    softened = soft_value.astype(jnp.bfloat16)
    attended_four = jnp.einsum(
        "phfg,gphd->fphd", softened, values_all, preferred_element_type=jnp.float32
    )
    attended = attended_four.reshape(frames * patches, model_width).astype(jnp.bfloat16)
    branch_first = product(attended, proj_full) + projb_full.astype(jnp.float32)
    middle = token_rows + gate_first * branch_first
    second_value, second_norm_back = jax.vjp(modulate, middle, shift_second, scale_second)
    normed_second = second_value.astype(jnp.bfloat16)
    hidden = product(normed_second, up_full) + upb_full.astype(jnp.float32)
    gelu_value, gelu_back = jax.vjp(gelu_tanh, hidden)
    activated = gelu_value.astype(jnp.bfloat16)
    branch_second = product(activated, down_full) + downb_full.astype(jnp.float32)
    result = middle + gate_second * branch_second
    block_output = result.astype(jnp.bfloat16).reshape(tokens.shape)
    mod_back, qkv_back, proj_back, up_back, down_back = (
        lax.all_gather(mod_weight, ("wide", "narrow"), axis=0, tiled=True),
        lax.all_gather(qkv_weight, ("wide", "narrow"), axis=0, tiled=True),
        lax.all_gather(proj_weight, ("wide", "narrow"), axis=0, tiled=True),
        lax.all_gather(up_weight, ("wide", "narrow"), axis=0, tiled=True),
        lax.all_gather(down_weight, ("wide", "narrow"), axis=0, tiled=True),
    )
    clip_weight = (loss_codes[0].astype(jnp.float32) + 1.0) * 0.25
    cotangent = out_grad[0].reshape(frames * patches, model_width).astype(jnp.float32) * clip_weight
    grad_gate_second = jnp.sum(cotangent * branch_second, axis=0)
    grad_branch_second = (cotangent * gate_second).astype(jnp.bfloat16)
    grad_down = jnp.einsum(
        "rk,rd->kd", activated, grad_branch_second, preferred_element_type=jnp.float32
    )
    grad_down_bias = column_sum(grad_branch_second)
    grad_activated = jnp.einsum(
        "rd,kd->rk", grad_branch_second, down_back, preferred_element_type=jnp.float32
    )
    grad_hidden = gelu_back(grad_activated)[0].astype(jnp.bfloat16)
    grad_up = jnp.einsum(
        "rd,rk->dk", normed_second, grad_hidden, preferred_element_type=jnp.float32
    )
    grad_up_bias = column_sum(grad_hidden)
    grad_normed_second = jnp.einsum(
        "rk,dk->rd", grad_hidden, up_back, preferred_element_type=jnp.float32
    )
    middle_part, grad_shift_second, grad_scale_second = second_norm_back(grad_normed_second)
    grad_middle = cotangent + middle_part
    grad_gate_first = jnp.sum(grad_middle * branch_first, axis=0)
    grad_branch_first = (grad_middle * gate_first).astype(jnp.bfloat16)
    grad_proj = jnp.einsum(
        "re,rd->ed", attended, grad_branch_first, preferred_element_type=jnp.float32
    )
    grad_proj_bias = column_sum(grad_branch_first)
    grad_attended = (
        jnp.einsum("rd,ed->re", grad_branch_first, proj_back, preferred_element_type=jnp.float32)
        .astype(jnp.bfloat16)
        .reshape(shape_four)
    )
    grad_softened = jnp.einsum(
        "fphd,gphd->phfg", grad_attended, values_all, preferred_element_type=jnp.float32
    )
    grad_values = jnp.einsum(
        "phfg,fphd->gphd", softened, grad_attended, preferred_element_type=jnp.float32
    ).astype(jnp.bfloat16)
    grad_scores = softmax_back(grad_softened)[0].astype(jnp.bfloat16)
    grad_queries = (
        jnp.einsum("phfg,gphd->fphd", grad_scores, keys_all, preferred_element_type=jnp.float32)
        * scale_factor
    ).astype(jnp.bfloat16)
    grad_keys = (
        jnp.einsum("phfg,fphd->gphd", grad_scores, queries, preferred_element_type=jnp.float32)
        * scale_factor
    ).astype(jnp.bfloat16)
    flat_shape = (frames * patches, model_width)
    grad_projected = jnp.concatenate(
        [
            grad_queries.reshape(flat_shape),
            grad_keys.reshape(flat_shape),
            grad_values.reshape(flat_shape),
        ],
        axis=1,
    )
    grad_qkv = jnp.einsum("rd,rk->dk", normed, grad_projected, preferred_element_type=jnp.float32)
    grad_qv_bias = jnp.concatenate(
        [column_sum(grad_queries.reshape(flat_shape)), column_sum(grad_values.reshape(flat_shape))]
    )
    grad_normed = jnp.einsum(
        "rk,dk->rd", grad_projected, qkv_back, preferred_element_type=jnp.float32
    )
    token_part, grad_shift_first, grad_scale_first = first_norm_back(grad_normed)
    tokens_grad = (grad_middle + token_part).astype(jnp.bfloat16).reshape(tokens.shape)
    grad_modulation = jnp.concatenate(
        [
            grad_shift_first,
            grad_scale_first,
            grad_gate_first,
            grad_shift_second,
            grad_scale_second,
            grad_gate_second,
        ]
    ).astype(jnp.bfloat16)
    grad_gated = jnp.einsum(
        "ij,j->i", mod_back, grad_modulation, preferred_element_type=jnp.float32
    )
    condition_grad = silu_back(grad_gated)[0][None, :]
    remaining = (
        grad_qkv,
        grad_qv_bias,
        grad_proj,
        grad_proj_bias,
        grad_up,
        grad_up_bias,
        grad_down,
        grad_down_bias,
    )
    grad_mod = jnp.einsum("i,j->ij", gated, grad_modulation, preferred_element_type=jnp.float32)
    grad_mod_bias = grad_modulation.astype(jnp.float32)
    gradients = (grad_mod, grad_mod_bias) + remaining
    owned = lax.psum_scatter(gradients, ("wide", "narrow"), scatter_dimension=0, tiled=True)
    owned_mod = owned[0]
    owned_mod_bias = owned[1]
    rest_owned = owned[2:]
    return (
        block_output,
        tokens_grad,
        condition_grad,
        owned_mod,
        owned_mod_bias,
        rest_owned[0],
        rest_owned[1],
        rest_owned[2],
        rest_owned[3],
        rest_owned[4],
        rest_owned[5],
        rest_owned[6],
        rest_owned[7],
    )


def solution(mesh):
    axes = ("wide", "narrow")
    four, two, one = P(axes, None, None, None), P(axes, None), P(axes)
    in_specs = (four, two, one, one, four, two, one, two, one, two, one, two, one, two, one)
    out_specs = (four, four, two, two, one, two, one, two, one, two, one, two, one)
    body = fast_local if (mesh.shape["wide"], mesh.shape["narrow"]) == (8, 4) else local
    return jax.shard_map(body, mesh=mesh, in_specs=in_specs, out_specs=out_specs, check_vma=False)
```

```python
import math

import jax
import jax.numpy as jnp
from jax import lax
from jax.experimental import pallas as pl
from jax.experimental.pallas import tpu as pltpu
from jax.sharding import PartitionSpec as P

HEAD_DIM = 64
VMEM_LIMIT = 63 * 2**20


BF = jnp.bfloat16
F32 = jnp.float32
MESH = pl.DeviceIdType.MESH
ANY = pl.BlockSpec(memory_space=pl.ANY)
VMEM = pl.BlockSpec(memory_space=pltpu.VMEM)
BLOCKS = 12
SHARD = 48 * BLOCKS
SMALL = SHARD + 16
HALF = 384
GROUP = 96


def mm(a, b):
    return jnp.dot(a, b, preferred_element_type=F32)


def mm_nt(a, b):
    return lax.dot_general(a, b, (((1,), (1,)), ((), ())), preferred_element_type=F32)


def mm_tn(a, b):
    return lax.dot_general(a, b, (((0,), (0,)), ((), ())), preferred_element_type=F32)


class Place:
    def __init__(self):
        wide = lax.axis_index("wide")
        narrow = lax.axis_index("narrow")
        self.z, self.c = wide // 2, wide % 2
        self.y, self.x = narrow // 2, narrow % 2
        self.me = wide * 4 + narrow

    def dev(self, z=None, c=None, y=None, x=None):
        z = self.z if z is None else z
        c = self.c if c is None else c
        y = self.y if y is None else y
        x = self.x if x is None else x
        return (z * 2 + c, y * 2 + x)

    def peers(self):
        column = [self.dev(z=(self.z + i) % 4) for i in (1, 2, 3)]
        plane = [self.dev(x=1 - self.x), self.dev(y=1 - self.y), self.dev(y=1 - self.y, x=1 - self.x)]
        return column, plane, self.dev(c=1 - self.c)

    def greet(self):
        bar = pltpu.get_barrier_semaphore()
        column, plane, sibling = self.peers()
        for target in column + plane + [sibling]:
            pl.semaphore_signal(bar, inc=1, device_id=target, device_id_type=MESH)
        pl.semaphore_wait(bar, 7)


def when(cond, act):
    pl.when(cond)(act)


class Gather:
    def __init__(self, place, buf, ssem, rsem, k, rows):
        self.p, self.buf, self.ssem, self.rsem, self.k, self.rows = place, buf, ssem, rsem, k, rows

    def copy(self, i, idx, dev):
        ref = self.buf.at[idx + (self.rows, slice(None))]
        return pltpu.make_async_remote_copy(
            ref, ref, self.ssem.at[self.k, i], self.rsem.at[self.k, i], device_id=dev, device_id_type=MESH
        )

    def up(self, h, op):
        p = self.p
        if op == "recv":
            when(p.z >= h, lambda: self.copy(h - 1, (p.z - h, p.c, p.y, p.x), p.dev(x=1 - p.x)).wait_recv())
            return
        cp = lambda: self.copy(h - 1, (p.z - (h - 1), p.c, p.y, p.x), p.dev(z=p.z + 1))
        when((p.z <= 2) & (p.z >= h - 1), (lambda: cp().start()) if op == "start" else (lambda: cp().wait_send()))

    def down(self, h, op):
        p = self.p
        if op == "recv":
            when(p.z + h <= 3, lambda: self.copy(h + 2, (p.z + h, p.c, p.y, p.x), p.dev(x=1 - p.x)).wait_recv())
            return
        cp = lambda: self.copy(h + 2, (p.z + (h - 1), p.c, p.y, p.x), p.dev(z=p.z - 1))
        when((p.z >= 1) & (p.z + (h - 1) <= 3), (lambda: cp().start()) if op == "start" else (lambda: cp().wait_send()))

    def plane(self):
        p = self.p
        low, high, every = pl.ds(0, 2), pl.ds(2, 2), slice(None)
        return (
            ((low, p.c, p.y, p.x), p.dev(x=1 - p.x), (low, p.c, p.y, 1 - p.x)),
            ((high, p.c, p.y, p.x), p.dev(y=1 - p.y), (high, p.c, 1 - p.y, p.x)),
            ((low, p.c, p.y, every), p.dev(y=1 - p.y), (low, p.c, 1 - p.y, every)),
            ((high, p.c, every, p.x), p.dev(x=1 - p.x), (high, p.c, every, 1 - p.x)),
            ((every, p.c, every, every), p.dev(c=1 - p.c), (every, 1 - p.c, every, every)),
        )

    def step(self, s):
        if 1 <= s <= 3:
            self.up(s, "recv")
            if s < 3:
                self.up(s + 1, "start")
            self.down(s, "recv")
            if s < 3:
                self.down(s + 1, "start")
        if s == 0:
            self.up(1, "start")
            self.down(1, "start")
        table = self.plane()
        starts = {3: (0, 1), 4: (2, 3), 5: (4,)}.get(s, ())
        recvs = {4: (0, 1), 5: (2, 3), 6: (4,)}.get(s, ())
        for i in recvs:
            self.copy(6 + i, table[i][2], table[i][1]).wait_recv()
        for i in starts:
            self.copy(6 + i, table[i][0], table[i][1]).start()

    def finish(self):
        for h in (1, 2, 3):
            self.up(h, "sent")
            self.down(h, "sent")
        for i, row in enumerate(self.plane()):
            self.copy(6 + i, row[0], row[1]).wait_send()


class GatherZ(Gather):
    def table(self):
        p = self.p
        every = slice(None)
        return (
            (0, (p.z, p.c, p.y, p.x), p.dev(x=1 - p.x), (p.z, p.c, p.y, 1 - p.x)),
            (1, (p.z, p.c, p.y, p.x), p.dev(y=1 - p.y), (p.z, p.c, 1 - p.y, p.x)),
            (0, (p.z, p.c, p.y, every), p.dev(y=1 - p.y), (p.z, p.c, 1 - p.y, every)),
            (1, (p.z, p.c, every, p.x), p.dev(x=1 - p.x), (p.z, p.c, every, 1 - p.x)),
        )

    def part(self, i, half, idx, dev):
        n = self.rows.size // 2
        ref = self.buf.at[idx + (pl.ds(self.rows.start + half * n, n), slice(None))]
        return pltpu.make_async_remote_copy(
            ref, ref, self.ssem.at[self.k, i], self.rsem.at[self.k, i], device_id=dev, device_id_type=MESH
        )

    def line(self, h, op, sign):
        p = self.p
        every = slice(None)
        i = (3 if sign > 0 else 6) + h
        reach = (lambda n: p.z - n >= 0) if sign > 0 else (lambda n: p.z + n <= 3)
        if op == "recv":
            when(reach(h), lambda: self.copy(i, (p.z - sign * h, p.c, every, every), p.dev(x=1 - p.x)).wait_recv())
            return
        cp = lambda: self.copy(i, (p.z - sign * (h - 1), p.c, every, every), p.dev(z=p.z + sign))
        can = (p.z <= 2) if sign > 0 else (p.z >= 1)
        when(can & reach(h - 1), (lambda: cp().start()) if op == "start" else (lambda: cp().wait_send()))

    def step(self, s):
        table = self.table()
        for i in {1: (0, 1), 2: (2, 3)}.get(s, ()):
            self.part(i, table[i][0], table[i][3], table[i][2]).wait_recv()
        for i in {0: (0, 1), 1: (2, 3)}.get(s, ()):
            self.part(i, *table[i][:3]).start()
        for sign in (1, -1):
            if 3 <= s <= 5:
                self.line(s - 2, "recv", sign)
            if 2 <= s <= 4:
                self.line(s - 1, "start", sign)
        last = self.plane()[4]
        if s == 5:
            self.copy(10, last[0], last[1]).start()
        if s == 6:
            self.copy(10, last[2], last[1]).wait_recv()

    def finish(self):
        for i, row in enumerate(self.table()):
            self.part(i, *row[:3]).wait_send()
        for h in (1, 2, 3):
            self.line(h, "sent", 1)
            self.line(h, "sent", -1)
        last = self.plane()[4]
        self.copy(10, last[0], last[1]).wait_send()


class Reduce:
    def __init__(self, place, buf, land, ssem, rsem, k, rows, final):
        self.p, self.buf, self.land, self.ssem, self.rsem, self.k, self.rows = place, buf, land, ssem, rsem, k, rows
        self.final = final

    def copy(self, i, idx, land, lidx, dev):
        tail = (self.rows, slice(None))
        return pltpu.make_async_remote_copy(
            self.buf.at[idx + tail], land.at[lidx + tail], self.ssem.at[self.k, i], self.rsem.at[self.k, i],
            device_id=dev, device_id_type=MESH,
        )

    def table(self):
        p = self.p
        low, high, every = pl.ds(0, 2), pl.ds(2, 2), slice(None)
        core, a2, b2, a1, b1, zd, zu = self.land
        return (
            ((every, 1 - p.c, every, every), core, (every, every, every), p.dev(c=1 - p.c)),
            ((low, p.c, 1 - p.y, every), a2, (every, every), p.dev(y=1 - p.y)),
            ((high, p.c, every, 1 - p.x), b2, (every, every), p.dev(x=1 - p.x)),
            ((low, p.c, p.y, 1 - p.x), a1, (every,), p.dev(x=1 - p.x)),
            ((high, p.c, 1 - p.y, p.x), b1, (every,), p.dev(y=1 - p.y)),
        )

    def add(self, idx, land, lidx):
        tail = (self.rows, slice(None))
        self.buf[idx + tail] = self.buf[idx + tail] + land[lidx + tail]

    def down(self, t, op):
        p, zd = self.p, self.land[5]
        if op == "recv":
            def take():
                self.copy(4 + t, (p.z - 3 + t, p.c, p.y, p.x), zd, (t - 1,), p.dev(x=1 - p.x)).wait_recv()
                if t < 3:
                    self.add((p.z - 3 + t, p.c, p.y, p.x), zd, (t - 1,))
            when((p.z <= 2) & (p.z - 3 + t >= 0), take)
            return
        cp = lambda: self.copy(4 + t, (p.z - 4 + t, p.c, p.y, p.x), zd, (t - 1,), p.dev(z=p.z - 1))
        when((p.z >= 1) & (p.z - 4 + t >= 0), (lambda: cp().start()) if op == "start" else (lambda: cp().wait_send()))

    def up(self, t, op):
        p, zu = self.p, self.land[6]
        if op == "recv":
            def take():
                self.copy(7 + t, (p.z + 3 - t, p.c, p.y, p.x), zu, (t - 1,), p.dev(x=1 - p.x)).wait_recv()
                if t < 3:
                    self.add((p.z + 3 - t, p.c, p.y, p.x), zu, (t - 1,))
            when((p.z >= 1) & (p.z + 3 - t <= 3), take)
            return
        cp = lambda: self.copy(7 + t, (p.z + 4 - t, p.c, p.y, p.x), zu, (t - 1,), p.dev(z=p.z + 1))
        when((p.z <= 2) & (p.z + 4 - t <= 3), (lambda: cp().start()) if op == "start" else (lambda: cp().wait_send()))

    def step(self, s):
        p = self.p
        core, a2, b2, a1, b1, zd, zu = self.land
        table = self.table()
        starts = {0: (0,), 1: (1, 2), 2: (3, 4)}.get(s, ())
        recvs = {1: (0,), 2: (1, 2), 3: (3, 4)}.get(s, ())
        for i in recvs:
            row = table[i]
            self.copy(i, row[0], row[1], row[2], row[3]).wait_recv()
        if s == 1:
            @pl.loop(0, 16)
            def _(i):
                zi, yi, xi = i // 4, (i // 2) % 2, i % 2
                self.add((zi, p.c, yi, xi), core, (zi, yi, xi))
        if s == 2:
            @pl.loop(0, 4)
            def _(i):
                self.add((i // 2, p.c, p.y, i % 2), a2, (i // 2, i % 2))
                self.add((2 + i // 2, p.c, i % 2, p.x), b2, (i // 2, i % 2))
        if s == 3:
            @pl.loop(0, 2)
            def _(i):
                self.add((i, p.c, p.y, p.x), a1, (i,))
                self.add((2 + i, p.c, p.y, p.x), b1, (i,))
        for i in starts:
            row = table[i]
            self.copy(i, row[0], row[1], row[2], row[3]).start()
        if s == 3:
            self.down(1, "start")
            self.up(1, "start")
        if s in (4, 5):
            t = s - 3
            self.down(t, "recv")
            self.down(t + 1, "start")
            self.up(t, "recv")
            self.up(t + 1, "start")
        if s == 6:
            self.down(3, "recv")
            self.up(3, "recv")
            tail = (self.rows, slice(None))
            own = self.buf[(p.z, p.c, p.y, p.x) + tail].astype(F32)
            from_above = zd[(2,) + tail].astype(F32)
            from_below = zu[(2,) + tail].astype(F32)
            self.final(
                jnp.where(p.z < 3, own + from_above, own) + jnp.where(p.z > 0, from_below, jnp.zeros_like(own))
            )

    def finish(self):
        for t in (1, 2, 3):
            self.down(t, "sent")
            self.up(t, "sent")
        for i, row in enumerate(self.table()):
            self.copy(i, row[0], row[1], row[2], row[3]).wait_send()


class ReduceZ:
    def __init__(self, place, buf, land, ssem, rsem, k, rows, final):
        self.p, self.buf, self.land, self.ssem, self.rsem, self.k, self.rows = place, buf, land, ssem, rsem, k, rows
        self.final = final
        n = rows.size // 2
        self.half = [pl.ds(rows.start, n), pl.ds(rows.start + n, n)]

    def copy(self, i, src, dst, dev):
        return pltpu.make_async_remote_copy(
            src, dst, self.ssem.at[self.k, i], self.rsem.at[self.k, i], device_id=dev, device_id_type=MESH
        )

    def at(self, idx, rows):
        return self.buf.at[idx + (rows, slice(None))]

    def core(self):
        p, every = self.p, slice(None)
        land = self.land[0].at[:, :, :, self.rows, :]
        return self.copy(0, self.at((every, 1 - p.c, every, every), self.rows), land, p.dev(c=1 - p.c))

    def flat(self, i):
        p, every = self.p, slice(None)
        _, _, _, a2, b2, a1, b1 = self.land
        far_x, far_y = p.dev(x=1 - p.x), p.dev(y=1 - p.y)
        row = (
            ((p.z, p.c, 1 - p.y, every), 0, a2, far_y), ((p.z, p.c, every, 1 - p.x), 1, b2, far_x),
            ((p.z, p.c, p.y, 1 - p.x), 0, a1, far_x), ((p.z, p.c, 1 - p.y, p.x), 1, b1, far_y),
        )[i]
        return self.copy(7 + i, self.at(row[0], self.half[row[1]]), row[2], row[3])

    def line(self, t, op, sign):
        p, every = self.p, slice(None)
        i = (0 if sign > 0 else 3) + t
        land = self.land[1 if sign > 0 else 2].at[t - 1]
        fits = (lambda n: p.z - n >= 0) if sign > 0 else (lambda n: p.z + n <= 3)
        can_take = (p.z <= 2) if sign > 0 else (p.z >= 1)
        can_send = (p.z >= 1) if sign > 0 else (p.z <= 2)
        if op == "recv":
            s = p.z - sign * (3 - t)

            def take():
                self.copy(i, self.at((s, p.c, every, every), self.rows), land, p.dev(x=1 - p.x)).wait_recv()
                for j in range(4):
                    at = (s, p.c, j // 2, j % 2, self.rows, slice(None))
                    self.buf[at] = self.buf[at] + land[j // 2, j % 2]
            when(can_take & fits(3 - t), take)
            return
        cp = lambda: self.copy(
            i, self.at((p.z - sign * (4 - t), p.c, every, every), self.rows), land, p.dev(z=p.z - sign)
        )
        when(can_send & fits(4 - t), (lambda: cp().start()) if op == "start" else (lambda: cp().wait_send()))

    def step(self, s):
        p = self.p
        core, _, _, a2, b2, a1, b1 = self.land
        tail = slice(None)
        if s == 0:
            self.core().start()
        if s == 1:
            self.core().wait_recv()

            @pl.loop(0, 16)
            def _(i):
                zi, yi, xi = i // 4, (i // 2) % 2, i % 2
                at = (zi, p.c, yi, xi, self.rows, tail)
                self.buf[at] = self.buf[at] + core[zi, yi, xi, self.rows, :]
        for sign in (1, -1):
            if 2 <= s <= 4:
                self.line(s - 1, "recv", sign)
            if 1 <= s <= 3:
                self.line(s, "start", sign)
        one, two = self.half
        if s == 4:
            self.flat(0).start()
            self.flat(1).start()
        if s == 5:
            self.flat(0).wait_recv()
            self.flat(1).wait_recv()
            for j in range(2):
                at = (p.z, p.c, p.y, j, one, tail)
                self.buf[at] = self.buf[at] + a2[j]
                at = (p.z, p.c, j, p.x, two, tail)
                self.buf[at] = self.buf[at] + b2[j]
            self.flat(2).start()
            self.flat(3).start()
        if s == 6:
            self.flat(2).wait_recv()
            self.flat(3).wait_recv()
            mine = (p.z, p.c, p.y, p.x)
            top = self.buf[mine + (one, tail)].astype(F32) + a1[...].astype(F32)
            low = self.buf[mine + (two, tail)].astype(F32) + b1[...].astype(F32)
            self.final(jnp.concatenate([top, low], axis=0))

    def finish(self):
        self.core().wait_send()
        for t in (1, 2, 3):
            self.line(t, "sent", 1)
            self.line(t, "sent", -1)
        for i in range(4):
            self.flat(i).wait_send()


def landing_z(rows, cols, dtype):
    v = pltpu.VMEM
    half = rows // 2
    return [
        v((3, 2, 2, rows, cols), dtype), v((3, 2, 2, rows, cols), dtype), v((2, half, cols), dtype),
        v((2, half, cols), dtype), v((half, cols), dtype), v((half, cols), dtype),
    ]


class SmallGather:
    def __init__(self, place, buf, ssem, rsem, k, rows):
        self.p, self.buf, self.ssem, self.rsem, self.k, self.rows = place, buf, ssem, rsem, k, rows

    def copy(self, i, idx, dev):
        ref = self.buf.at[idx + (self.rows, slice(None))]
        return pltpu.make_async_remote_copy(
            ref, ref, self.ssem.at[self.k, i], self.rsem.at[self.k, i], device_id=dev, device_id_type=MESH
        )

    def table(self):
        p = self.p
        column, plane, sibling = p.peers()
        every = slice(None)
        first = [(i, (p.z, p.c, p.y, p.x), column[i], ((p.z + 3 - i) % 4, p.c, p.y, p.x)) for i in range(3)]
        far = [(p.y, 1 - p.x), (1 - p.y, p.x), (1 - p.y, 1 - p.x)]
        second = [(3 + i, (every, p.c, p.y, p.x), plane[i], (every, p.c) + far[i]) for i in range(3)]
        third = [(6, (every, p.c, every, every), sibling, (every, 1 - p.c, every, every))]
        return first, second, third

    def step(self, s):
        hops = self.table()
        if s > 0:
            for i, _, dev, came in hops[s - 1]:
                self.copy(i, came, dev).wait_recv()
        if s < 3:
            for i, idx, dev, _ in hops[s]:
                self.copy(i, idx, dev).start()

    def finish(self):
        for hop in self.table():
            for i, idx, dev, _ in hop:
                self.copy(i, idx, dev).wait_send()


class SmallReduce:
    def __init__(self, place, buf, land, ssem, rsem, k, rows, final):
        self.p, self.buf, self.land, self.ssem, self.rsem, self.k = place, buf, land, ssem, rsem, k
        self.final = final
        self.tail = (rows, slice(None))

    def copy(self, i, idx, dst, dev):
        return pltpu.make_async_remote_copy(
            self.buf.at[idx + self.tail], dst, self.ssem.at[self.k, i], self.rsem.at[self.k, i], device_id=dev, device_id_type=MESH
        )

    def table(self):
        p = self.p
        column, plane, sibling = p.peers()
        every = slice(None)
        core, flat, line = self.land
        tail = self.tail
        far = [(p.y, 1 - p.x), (1 - p.y, p.x), (1 - p.y, 1 - p.x)]
        first = [(0, (every, 1 - p.c, every, every), core.at[(every, every, every) + tail], sibling)]
        second = [(1 + i, (every, p.c) + far[i], flat.at[(i, every) + tail], plane[i]) for i in range(3)]
        third = [(4 + i, ((p.z + 1 + i) % 4, p.c, p.y, p.x), line.at[(i,) + tail], column[i]) for i in range(3)]
        return first, second, third

    def step(self, s):
        p = self.p
        core, flat, line = self.land
        hops = self.table()
        tail = self.tail
        every = slice(None)
        if s > 0:
            for i, idx, dst, dev in hops[s - 1]:
                self.copy(i, idx, dst, dev).wait_recv()
        if s == 1:
            at = (every, p.c, every, every) + tail
            self.buf[at] = self.buf[at] + core[(every, every, every) + tail]
        if s == 2:
            at = (every, p.c, p.y, p.x) + tail
            came = [flat[(i, every) + tail] for i in range(3)]
            self.buf[at] = self.buf[at] + (came[0] + came[1] + came[2])
        if s < 3:
            for i, idx, dst, dev in hops[s]:
                self.copy(i, idx, dst, dev).start()
        else:
            came = [line[(i,) + tail] for i in range(3)]
            self.final(self.buf[(p.z, p.c, p.y, p.x) + tail] + came[0] + came[1] + came[2])

    def finish(self):
        for hop in self.table():
            for i, idx, dst, dev in hop:
                self.copy(i, idx, dst, dev).wait_send()


def small_landing(rows, cols):
    return [
        pltpu.VMEM((4, 2, 2, rows, cols), F32), pltpu.VMEM((3, 4, rows, cols), F32), pltpu.VMEM((3, rows, cols), F32)
    ]


def landing(rows, cols, dtype, kept):
    return [
        pltpu.VMEM((4, 2, 2, rows, cols), dtype),
        pltpu.VMEM((2, 2, kept, cols), dtype),
        pltpu.VMEM((2, 2, kept, cols), dtype),
        pltpu.VMEM((2, kept, cols), dtype),
        pltpu.VMEM((2, kept, cols), dtype),
        pltpu.VMEM((3, kept, cols), dtype),
        pltpu.VMEM((3, kept, cols), dtype),
    ]


def pack48(block):
    wide = block.astype(F32)
    return jnp.concatenate([wide[:, :HALF], wide[:, HALF:]], axis=0).astype(BF)


def iota(shape, dim):
    return lax.broadcasted_iota(jnp.int32, shape, dim)


def onehot(cond):
    return jnp.where(cond, 1.0, 0.0).astype(BF)


def ln_hat(v):
    center = v - jnp.mean(v, axis=-1, keepdims=True)
    spread = jnp.mean(center * center, axis=-1, keepdims=True)
    return center * lax.rsqrt(spread + 1e-06)


def fold(v):
    total = v[0:8]
    for i in range(1, v.shape[0] // 8):
        total = total + v[8 * i:8 * i + 8]
    return total


def turn(src, step, put):
    frames, patches, width = src.shape
    count = frames * patches
    for h in range(width // 128):
        base = count * (h % 2)
        cols = slice(128 * h, 128 * h + 128)
        for f in range(frames):
            step[pl.ds(base + f, patches, stride=frames), :] = src[f, :, cols].astype(F32)
        put(cols, step[base:base + count, :])


def turn_back(src, step, dst):
    frames, patches, width = dst.shape
    count = frames * patches
    for h in range(width // 128):
        base = count * (h % 2)
        cols = slice(128 * h, 128 * h + 128)
        step[base:base + count, :] = src[:, cols]
        for f in range(frames):
            dst[f, :, cols] = step[pl.ds(base + f, patches, stride=frames), :].astype(BF)


def pick_row(flat, r):
    return mm(onehot(iota((32, 512), 1) == iota((32, 512), 0) * 16 + r), flat)


def spread_bias(rows, n, start, width):
    k = rows.shape[1]
    lane = iota((k, width), 0)
    col = iota((k, width), 1) + start
    grid = mm(rows.astype(BF), onehot((col % n == lane) & (lane < n)))
    dev = iota((32, width), 0)
    mine = (iota((32, width), 1) + start) // n == dev
    return jnp.sum(jnp.where(mine, grid, 0.0), axis=0, keepdims=True)


def softmax_rows(scores):
    e = jnp.exp(scores - jnp.max(scores, axis=-1, keepdims=True))
    return e * (1.0 / jnp.sum(e, axis=-1, keepdims=True))


def group_start(g, tokens):
    return pl.multiple_of(jnp.minimum(g * GROUP, tokens - GROUP), 16)


def fill_mask(mask_ref, frames):
    shape = mask_ref.shape
    row = iota(shape, 0) % GROUP
    mask_ref[...] = jnp.where(row // frames == iota(shape, 1) // frames, 0.0, -1e30)


F_SEQ = (
    30, 80, 10, 20, 0, "IO", 81, 31, 11, 21, 1, 32, 40, 12, 22, 33, 50, 70, 60, 2, 13, 23, 3, 41, 34, "PM", 51, 90,
    "PN", 100, 91, 42, 14, 61, 24, "XH", 43, 35, 92, 52, 101, "BI", 71, 93, 36, "R2", 62, 15, 82, "MV", 53, 25, "LN",
    16, 26, 63, 102, "R0", ("QK", 0,), 44, "R1", 72, ("QK", 1,), 54, ("QK", 2,), 83, 103, ("AT", 0, 1), "MW",
    ("AT", 1, 2), ("AT", 2, 3), 64, ("AT", 3, 4), ("AT", 4, 5), ("AT", 5, 6), 45, 73, ("AT", 6, 7), ("AT", 7, 8), 46,
    "R3", ("AT", 8, 9), ("AT", 9, 10), "GB", 84, 55, ("AT", 10, 11), "PR", "L2", 56, "R4", ("UP", 0,), 65, ("UP", 1,),
    85, 74, ("UP", 2,), 66, "R5", ("UP", 3,), ("UP", 4,), ("UP", 5,), 86, 75, ("DG", 0,), ("DG", 1,), ("DG", 2,),
    ("DG", 3,), ("DG", 4,), 76, "R6", "R7", ("DG", 5,), ("DG", 6,), "DN0", ("DG", 7,), "DN1",
)


F_LAST = (8,)
F_ROWS = ((0, 48), (48, 48), (96, 48), (144, 48), (192, 96), (288, 96), (384, 96), (480, 96))


def f_kernel(
    x_hbm, og_hbm, code_ref, gated_ref, qv_ref, pb_ref, ub_ref, db_ref, mb_ref, mw_ref, qw_ref, pw_ref, uw_ref, dw_ref,
    bo_hbm, xt_hbm, ogt_hbm, n1_hbm, qkv_hbm, att_hbm, br_hbm, mid_hbm, n2_hbm, dg_hbm, gp_hbm, gb_hbm,
    wq_hbm, wp_hbm, wu_hbm, wd_hbm, mod_out, gmy_out, mwp_out,
    gbuf, pm, pbuf, l0, l1, l2, dbuf,
    wq, wp, wu, wd, x_v, og_v, n_v, qkv, att, br, mid, act, gpt, raw, gb, amask, bq, bp, bu, bd, acc, step, sm, mb,
    gs, gr, ps, pr, lsem, gpsem, dsem,
):
    p = Place()
    tokens, width = x_v.shape
    rows_of = [slice(SHARD, SMALL)] + [slice(a, a + n) for a, n in F_ROWS]
    gath = [
        (SmallGather if k == 0 else GatherZ if k in F_LAST else Gather)(p, gbuf, gs, gr, k, pl.ds(r.start, r.stop - r.start)) for k, r in enumerate(rows_of)
    ]
    loads = [pltpu.make_async_copy(h.at[0], raw.at[i], lsem.at[i]) for i, h in enumerate((x_hbm, og_hbm))]
    for cp in loads:
        cp.start()
    outs = []
    saved = []

    def save(src, dst):
        cp = pltpu.make_async_copy(src, dst, lsem.at[2 + len(saved)])
        cp.start()
        outs.append(cp)
        saved.append(cp)
        return cp

    def finish(cp):
        cp.wait()
        outs[:] = [o for o in outs if o is not cp]

    own = (p.z, p.c, p.y, p.x)
    weight = (code_ref[0].astype(F32) + 1.0) * 0.25
    sm[...] = jnp.zeros_like(sm)
    sm[0:1, :] = gated_ref[:, :HALF].astype(F32)
    sm[1:2, :] = gated_ref[:, HALF:].astype(F32)
    for i, ref in enumerate((qv_ref, pb_ref, ub_ref, db_ref, mb_ref)):
        sm[2 + i:3 + i, 0:ref.shape[1]] = ref[...].astype(F32)
    gbuf[own + (slice(SHARD, SMALL), slice(None))] = sm[...].astype(BF)
    for b in range(3):
        gbuf[own + (slice(48 * b, 48 * b + 48), slice(None))] = pack48(qw_ref[:, width * b:width * b + width])
    gbuf[own + (slice(144, 192), slice(None))] = pack48(pw_ref[...])
    for b in range(4):
        gbuf[own + (slice(192 + 48 * b, 240 + 48 * b), slice(None))] = pack48(uw_ref[:, width * b:width * b + width])
    gbuf[own + (slice(384, 480), slice(None))] = dw_ref[:, :HALF]
    gbuf[own + (slice(480, 576), slice(None))] = dw_ref[:, HALF:]
    p.greet()

    frames = x_hbm.shape[1]

    def final_mod(pieces):
        def go(total):
            for i, m in enumerate(pieces):
                for j in range(6):
                    mod_out[m:m + 1, 128 * j:128 * j + 128] = total[6 * i + j:6 * i + j + 1, :]
        return go

    land = (l0, l1, l2)
    first = SmallReduce(p, pbuf, land, ps, pr, 0, pl.ds(0, 16), final_mod((0, 1)))
    second = SmallReduce(p, pbuf, land, ps, pr, 1, pl.ds(16, 24), final_mod((2, 3, 4, 5)))
    items = gath + [first, second]

    def small_rows():
        fill_mask(amask, frames)
        acc[...] = jnp.zeros_like(acc)
        mod_out[6:8, :] = jnp.zeros((2, width), F32)
        flat = gbuf[:, :, :, :, SHARD:SMALL, :].reshape(512, HALF)
        gated = jnp.concatenate([pick_row(flat, 0), pick_row(flat, 1)], axis=1).astype(BF)
        sel = onehot((iota((width, 128), 0) == p.me * 24 + iota((width, 128), 1)) & (iota((width, 128), 1) < 24))
        gmy_out[...] = mm(gated, sel).astype(BF)

    def small_work(pieces, base, rows):
        pad = jnp.zeros((8, width), F32)
        for m in pieces:
            cols = slice(width * m, width * m + width)
            part = jnp.concatenate([mw_ref[:, cols].astype(F32), pad], axis=0).astype(BF)
            mwp_out[:, cols] = part
            prod = mm(gmy_out[:, :32], part)
            for j in range(6):
                pm[32 * (6 * m + j):32 * (6 * m + j) + 32, :] = prod[:, 128 * j:128 * j + 128]
        count = 6 * len(pieces)

        @pl.loop(0, 32)
        def _(d):
            at = (d // 8, (d // 4) % 2, (d // 2) % 2, d % 2)
            for j in range(count):
                pbuf[at + (slice(base + j, base + j + 1), slice(None))] = pm[pl.ds(32 * (6 * pieces[0] + j) + d, 1), :]
            if rows > count:
                pbuf[at + (slice(base + count, base + rows), slice(None))] = jnp.zeros((rows - count, 128), F32)

    def biases():
        flat = gbuf[:, :, :, :, SHARD:SMALL, :].reshape(512, HALF)
        qv, prj, up, dn, md = (pick_row(flat, r) for r in (2, 3, 4, 5, 6))
        bq[:, 0:width] = spread_bias(qv[:, :128], 48, 0, width)
        bq[:, width:2 * width] = jnp.zeros((1, width), F32)
        bq[:, 2 * width:] = spread_bias(qv[:, :128], 48, width, width)
        bp[...] = spread_bias(prj[:, :128], 24, 0, width)
        bd[...] = spread_bias(dn[:, :128], 24, 0, width)
        for m in range(4):
            bu[:, width * m:width * m + width] = spread_bias(up[:, :128], 96, width * m, width)
        for m in range(6):
            mb[m:m + 1, :] = spread_bias(md[:, :256], 144, width * m, width)

    def unpack(b, dst, col):
        @pl.loop(0, 16)
        def _(i):
            src = (i // 4, (i // 2) % 2, i % 2)
            one = gbuf[src + (0, slice(48 * b, 48 * b + 48), slice(None))].astype(F32)
            two = gbuf[src + (1, slice(48 * b, 48 * b + 48), slice(None))].astype(F32)
            at = pl.ds(pl.multiple_of(i * 48, 16), 48)
            dst[at, col:col + HALF] = jnp.concatenate([one[:24], two[:24]], axis=0).astype(BF)
            dst[at, col + HALF:col + 2 * HALF] = jnp.concatenate([one[24:], two[24:]], axis=0).astype(BF)

    def unpack_down(h):
        @pl.loop(0, 32)
        def _(d):
            wd[pl.ds(pl.multiple_of(d * 96, 16), 96), HALF * h:HALF * h + HALF] = gbuf[
                d // 8, (d // 4) % 2, (d // 2) % 2, d % 2, 384 + 96 * h:480 + 96 * h, :
            ]

    def rows_loop(body):
        @pl.loop(0, tokens // 48, unroll=3)
        def _(i):
            body(pl.ds(pl.multiple_of(i * 48, 16), 48))

    def put_x(cols, value):
        mid[:, cols] = value
        x_v[:, cols] = value.astype(BF)

    def put_og(cols, value):
        og_v[:, cols] = value.astype(BF)

    def first_hat(at):
        mid[at, :] = ln_hat(mid[at, :])

    def first_norm(at):
        n_v[at, :] = (mid[at, :] * (1.0 + mod_out[1:2, :]) + mod_out[0:1, :]).astype(BF)

    def second_norm(at):
        n_v[at, :] = (ln_hat(mid[at, :]) * (1.0 + mod_out[4:5, :]) + mod_out[3:4, :]).astype(BF)

    def qkv_block(i):
        for j in range(width * i, width * i + width, 256):
            cols = slice(j, j + 256)
            qkv[:, cols] = (mm(n_v[...], wq[:, cols]) + bq[:, cols]).astype(BF)

    def attention(first, last):
        low_lane = iota((GROUP, 128), 1) < 64

        @pl.loop(first, last)
        def _(g):
            rows = pl.ds(group_start(g, tokens), GROUP)
            heads = [slice(128 * h, 128 * h + 128) for h in range(width // 128)]
            values = [qkv[rows, 2 * width + c.start:2 * width + c.stop] for c in heads]
            scores = []
            for c in heads:
                q = qkv[rows, c]
                k = qkv[rows, width + c.start:width + c.stop]
                zero = jnp.zeros_like(q)
                qs = jnp.concatenate([jnp.where(low_lane, q, zero), jnp.where(low_lane, zero, q)], axis=0)
                scores.append(mm_nt(qs, k))
            probs = [softmax_rows(a * 0.125 + amask[...]).astype(BF) for a in scores]
            both = [mm(a, v) for a, v in zip(probs, values)]
            for c, a in zip(heads, both):
                att[rows, c] = jnp.where(low_lane, a[:GROUP], a[GROUP:]).astype(BF)

    def proj():
        branch = mm(att[...], wp[...]) + bp[...]
        br[...] = branch.astype(BF)
        mid[...] = x_v[...].astype(F32) + mod_out[2:3, :] * branch

    def second_cot(at):
        low = (og_v[at, :].astype(F32) * weight * mod_out[5:6, :]).astype(BF)
        gb[at, :] = low
        acc[...] += fold(low.astype(F32))

    def dg_copy(j):
        return pltpu.make_async_copy(dbuf.at[j % 2], dg_hbm.at[j // 2, j % 2], dsem.at[j % 2])

    def down_grad(j):
        if j >= 2:
            dg_copy(j - 2).wait()
        grad = mm_tn(act[:, HALF * j:HALF * j + HALF], gb[...])
        for dd in range(4):
            part = grad[96 * dd:96 * dd + 96].astype(BF)
            dbuf[j % 2, dd // 2, dd % 2, 0:96, :] = part[:, :HALF]
            dbuf[j % 2, dd // 2, dd % 2, 96:192, :] = part[:, HALF:]
        dg_copy(j).start()

    def gp_copy(j):
        return pltpu.make_async_copy(gpt.at[j % 2], gp_hbm.at[:, pl.ds(256 * j, 256)], gpsem.at[j % 2])

    def up_tile(j):
        cols = slice(256 * j, 256 * j + 256)
        if j >= 2:
            gp_copy(j - 2).wait()
        hid = mm(n_v[...], wu[:, cols]) + bu[:, cols]
        sq = hid * hid
        slope_in = 0.7978845608 + (0.7978845608 * 0.044715) * sq
        half = 0.5 + 0.5 * jnp.tanh(hid * slope_in)
        act[:, cols] = (hid * half).astype(BF)
        rate = 2.0 * 0.7978845608 + (6.0 * 0.7978845608 * 0.044715) * sq
        gpt[j % 2] = (half + (hid * rate) * (half - half * half)).astype(BF)
        gp_copy(j).start()

    def down_tile(j):
        cols = slice(256 * j, 256 * j + 256)
        branch = mm(act[...], wd[:, cols]) + bd[:, cols]
        mid[:, cols] += mod_out[5:6, cols] * branch
        cot = og_v[:, cols].astype(F32) * weight
        mod_out[6:7, cols] = jnp.sum(cot * branch, axis=0, keepdims=True)

    n1_out = []

    def do(tag, *span):
        if isinstance(tag, int):
            items[tag // 10].step(tag % 10)
        elif tag == "PM":
            small_rows()
            small_work((0, 1), 0, 16)
        elif tag == "PN":
            small_work((2, 3, 4, 5), 16, 24)
        elif tag == "IO":
            loads[1].wait()
            turn(raw.at[1], step, put_og)
            save(og_v, ogt_hbm)
        elif tag == "XH":
            loads[0].wait()
            turn(raw.at[0], step, put_x)
            rows_loop(first_hat)
            save(x_v, xt_hbm)
        elif tag == "BI":
            biases()
        elif tag == "MV":
            mod_out[0:2, :] += mb[0:2, :]
        elif tag == "MW":
            mod_out[2:6, :] += mb[2:6, :]
        elif tag in ("R0", "R1", "R2", "R3"):
            b = int(tag[1])
            if b < 3:
                unpack(b, wq, width * b)
            else:
                unpack(b, wp, 0)
                save(wp, wp_hbm)
        elif tag == "LN":
            rows_loop(first_norm)
            n1_out.append(save(n_v, n1_hbm))
        elif tag == "QK":
            qkv_block(*span)
            if span == (2,):
                save(wq, wq_hbm)
                save(qkv, qkv_hbm)
        elif tag == "AT":
            attention(*span)
            if span[1] == 11:
                save(att, att_hbm)
        elif tag == "PR":
            proj()
            save(br, br_hbm)
            n1_out.append(save(mid, mid_hbm))
            finish(n1_out[0])
        elif tag == "L2":
            rows_loop(second_norm)
            save(n_v, n2_hbm)
        elif tag in ("R4", "R5"):
            b = 4 if tag == "R4" else 6
            unpack(b, wu, width * (b - 4))
            unpack(b + 1, wu, width * (b - 3))
        elif tag == "UP":
            if span == (3,):
                save(wu, wu_hbm)
            up_tile(2 * span[0])
            up_tile(2 * span[0] + 1)
        elif tag == "GB":
            rows_loop(second_cot)
            mod_out[7:8, :] = jnp.sum(acc[...], axis=0, keepdims=True)
            save(gb, gb_hbm)
        elif tag == "DG":
            down_grad(*span)
        elif tag in ("R6", "R7"):
            unpack_down(int(tag[1]) - 6)
        elif tag == "DN0":
            finish(n1_out[1])
            down_tile(0)
        elif tag == "DN1":
            save(wd, wd_hbm)
            down_tile(1)
            down_tile(2)
            turn_back(mid, step, raw.at[0])
            save(raw.at[0], bo_hbm.at[0])

    for tag in F_SEQ:
        do(*(tag if isinstance(tag, tuple) else (tag,)))
    for j in (10, 11):
        gp_copy(j).wait()
    for j in (6, 7):
        dg_copy(j).wait()
    for cp in outs:
        cp.wait()
    for item in items:
        item.finish()


def forward(tokens, out_grad, codes, *rest):
    _, frames, patches, d = tokens.shape
    t, hid = frames * patches, rest[9].shape[1]
    s = jax.ShapeDtypeStruct
    outs = [
        s(tokens.shape, BF), s((t, d), BF), s((t, d), BF), s((t, d), BF), s((t, 3 * d), BF), s((t, d), BF), s((t, d), BF), s((t, d), F32), s((t, d), BF),
        s((4, 2, 2, 2, 192, HALF), BF), s((t, hid), BF), s((t, d), BF),
        s((d, 3 * d), BF), s((d, d), BF), s((d, hid), BF), s((hid, d), BF),
        s((8, d), F32), s((32, 128), BF), s((32, 6 * d), BF),
    ]
    v = pltpu.VMEM
    scratch = [
        v((4, 2, 2, 2, SMALL, HALF), BF), v((6 * d // 128 * 32, 128), F32), v((4, 2, 2, 2, 40, 128), F32), *small_landing(40, 128), v((2, 2, 2, 192, HALF), BF),
        v((d, 3 * d), BF), v((d, d), BF), v((d, hid), BF), v((hid, d), BF),
        v((t, d), BF), v((t, d), BF), v((t, d), BF), v((t, 3 * d), BF), v((t, d), BF), v((t, d), BF), v((t, d), F32),
        v((t, hid), BF), v((2, t, 256), BF), v((2, frames, patches, d), BF), v((t, d), BF), v((2 * GROUP, GROUP), F32),
        v((1, 3 * d), F32), v((1, d), F32), v((1, hid), F32), v((1, d), F32), v((8, d), F32), v((2 * t, 128), F32), v((16, HALF), F32), v((8, d), F32),
        pltpu.SemaphoreType.DMA((9, 11)), pltpu.SemaphoreType.DMA((9, 11)),
        pltpu.SemaphoreType.DMA((2, 11)), pltpu.SemaphoreType.DMA((2, 11)),
        pltpu.SemaphoreType.DMA((24,)), pltpu.SemaphoreType.DMA((2,)), pltpu.SemaphoreType.DMA((2,)),
    ]
    return pl.pallas_call(
        f_kernel,
        out_shape=outs,
        in_specs=[ANY, ANY, pl.BlockSpec(memory_space=pltpu.SMEM)] + [VMEM] * len(rest),
        out_specs=[ANY] * 16 + [VMEM] * 3,
        scratch_shapes=scratch,
        compiler_params=pltpu.CompilerParams(collective_id=0, has_side_effects=True, vmem_limit_bytes=VMEM_LIMIT),
        cost_estimate=pl.CostEstimate(flops=15 * 10**9, bytes_accessed=70 * 10**6, transcendentals=4 * 10**6),
        name="forward",
    )(tokens, out_grad, codes, *rest)


B_SEQ = (
    "LD", "ST", 10, 0, ("A", 0,), ("A", 1,), ("A", 2,), ("A", 3,), ("A", 4,), ("A", 5,), "U0", "U1", 11, 20, "U2",
    "U3", 30, ("N0", 0,), ("N0", 1,), 1, 21, ("N0", 2,), 12, "L2", "PA", ("AB", 0, 1), 2, 22, "PG", 40, ("AB", 1, 2),
    ("AB", 2, 3), ("AB", 3, 4), 31, ("AB", 4, 5), ("AB", 5, 6), 13, ("AB", 6, 7), ("AB", 7, 8), 41, 23, ("AB", 8, 9),
    ("AB", 9, 10), ("AB", 10, 11), "Q0", 14, "Q1", 50, 32, 24, ("N1", 0,), 60, ("N1", 1,), 51, 15, ("N1", 2,), 61, 25,
    33, "L1", "MB", 90, 42, "Q2", 26, 34, "BI", 3, 91, 70, 62, "BB", 80, 35, 71, 92, 52, "TG", 63, 81, 43, 93, "GM",
    100, 72, 4, 36, 16, 53, 44, 73, 101, 64, 54, 45, 74, 82, 65, 5, 55, 102, 46, 75, 66, 6, 103, "CO", 56, 83, 76,
)
B_FIRST = (0,)
CHUNKS = ((480, 96), (384, 96), (192, 96), (288, 96), (144, 48), (0, 48), (48, 48), (96, 48))


def ln_parts(v):
    center = v - jnp.mean(v, axis=-1, keepdims=True)
    spread = jnp.mean(center * center, axis=-1, keepdims=True)
    inv = lax.rsqrt(spread + 1e-06)
    return center * inv, inv


def ln_back(g, hat, inv, scale):
    dh = g * (1.0 + scale)
    return inv * (dh - jnp.mean(dh, axis=-1, keepdims=True) - hat * jnp.mean(dh * hat, axis=-1, keepdims=True))


def split_bias(vec, n):
    width = vec.shape[1]
    mine = iota((32, width), 1) // n == iota((32, width), 0)
    lane = iota((width, 128), 1)
    ones = jnp.where((iota((width, 128), 0) % n == lane) & (lane < n), 1.0, 0.0)
    return jnp.dot(jnp.where(mine, vec, 0.0), ones, precision=lax.Precision.HIGHEST, preferred_element_type=F32)


def b_kernel(
    x_hbm, og_hbm, code_ref, mod_ref, gmy_ref, mwp_ref,
    n1_hbm, qkv_hbm, att_hbm, br_hbm, mid_hbm, n2_hbm, dg_hbm, gp_hbm, gb_hbm, wq_hbm, wp_hbm, wu_hbm, wd_hbm,
    tg_hbm, gq_out, gp_out, gu_out, gd_out, bias_out, gmw_out, gmb_out, cg_out,
    gbuf, k0, k1, k2, k3, k4, k5, k6, y1, y2, y3, y4, y5, y6, sbuf, t0, t1, t2, mbuf, cbuf, stage,
    wa, wu, gh, gb, nb, mid, gn, br, amask, vec, accs, raw, step,
    rs, rr, ts, tr, gs, gr, lsem,
):
    p = Place()
    tokens, width = gb.shape
    frames = raw.shape[0]
    cw = (code_ref[0].astype(F32) + 1.0) * 0.25
    pending = {}

    def load(name, i, src, dst):
        pending[name] = pltpu.make_async_copy(src, dst, lsem.at[i])
        pending[name].start()

    def put48(dst_out, b, total):
        dst_out[:, width * b:width * b + HALF] = total[:24]
        dst_out[:, width * b + HALF:width * b + width] = total[24:48]

    def finals(k):
        def go(total):
            if k < 2:
                gd_out[:, HALF * (1 - k):HALF * (2 - k)] = total
            elif k < 4:
                put48(gu_out, 2 * (k - 2), total[:48])
                put48(gu_out, 2 * (k - 2) + 1, total[48:])
            elif k == 4:
                put48(gp_out, 0, total)
            else:
                put48(gq_out, k - 5, total)
        return go

    land = (k0, k1, k2, k3, k4, k5, k6)
    lands = {k: land for k in range(len(CHUNKS))}
    if B_FIRST:
        lands[B_FIRST[0]] = (k0, y1, y2, y3, y4, y5, y6)
    reds = [
        (ReduceZ if k in B_FIRST else Reduce)(p, gbuf, lands[k], rs, rr, k, pl.ds(a, n), finals(k))
        for k, (a, n) in enumerate(CHUNKS)
    ]

    def bias_final(total):
        bias_out[...] = total

    bred = SmallReduce(p, sbuf, (t0, t1, t2), ts, tr, 0, pl.ds(0, 8), bias_final)
    mgath = SmallGather(p, mbuf, gs, gr, 0, pl.ds(0, 16))
    cgath = SmallGather(p, cbuf, gs, gr, 1, pl.ds(0, 32))

    def weight_grad(left_ref, right, b):
        for m in range(2):
            grad = mm_tn(left_ref[:, HALF * m:HALF * m + HALF], right[...])
            for dd in range(16):
                gbuf[2 * m + dd // 8, dd // 4 % 2, dd // 2 % 2, dd % 2, 48 * b:48 * b + 48, :] = pack48(
                    grad[24 * dd:24 * dd + 24]
                )

    def act_grad(j):
        cols = slice(512 * j, 512 * j + 512)
        low = (mm_nt(gb[...], wa[cols, :]) * gh[:, cols].astype(F32)).astype(BF)
        gh[:, cols] = low
        vec[0:1, cols] = jnp.sum(low.astype(F32), axis=0, keepdims=True)

    def norm2_back():
        scale, gate = mod_ref[4:5, :], mod_ref[2:3, :]
        accs[...] = jnp.zeros_like(accs)

        @pl.loop(0, tokens // 48, unroll=3)
        def _(i):
            at = pl.ds(pl.multiple_of(i * 48, 16), 48)
            g = gn[at, :]
            hat, inv = ln_parts(mid[at, :])
            gm = gb[at, :].astype(F32) * cw + ln_back(g, hat, inv, scale)
            gn[at, :] = gm
            low = (gm * gate).astype(BF)
            gh[at, 3 * width:4 * width] = low
            accs[0:8, :] += fold(g)
            accs[8:16, :] += fold(g * hat)
            accs[16:24, :] += fold(gm * br[at, :].astype(F32))
            accs[24:32, :] += fold(low.astype(F32))

        for i, row in enumerate((3, 4, 2)):
            vec[1 + row:2 + row, 0:width] = jnp.sum(accs[8 * i:8 * i + 8, :], axis=0, keepdims=True)
        vec[8:9, 0:width] = jnp.sum(accs[24:32, :], axis=0, keepdims=True)

    def norm1_back():
        scale = mod_ref[1:2, :]
        accs[...] = jnp.zeros_like(accs)

        @pl.loop(0, tokens // 48, unroll=3)
        def _(i):
            at = pl.ds(pl.multiple_of(i * 48, 16), 48)
            g = mid[at, :]
            hat, inv = ln_parts(br[at, :].astype(F32))
            gn[at, :] += ln_back(g, hat, inv, scale)
            accs[0:8, :] += fold(g)
            accs[8:16, :] += fold(g * hat)

        for i in range(2):
            vec[1 + i:2 + i, 0:width] = jnp.sum(accs[8 * i:8 * i + 8, :], axis=0, keepdims=True)

    def attention_back(first, last):
        low_lane = iota((GROUP, 128), 1) < 64

        @pl.loop(first, last)
        def _(g):
            start = group_start(g, tokens)
            rows = pl.ds(start, GROUP)
            heads = [slice(128 * h, 128 * h + 128) for h in range(width // 128)]
            units = []
            for c in heads:
                q, k, v = (gh[rows, width * i + c.start:width * i + c.stop] for i in range(3))
                ga = gb[rows, c]
                zero = jnp.zeros_like(q)
                qs = jnp.concatenate([jnp.where(low_lane, q, zero), jnp.where(low_lane, zero, q)], axis=0)
                gas = jnp.concatenate([jnp.where(low_lane, ga, zero), jnp.where(low_lane, zero, ga)], axis=0)
                units.append((k, qs, gas, mm_nt(k, qs), mm_nt(v, gas)))
            soft = []
            for _, _, _, scores, gprobs in units:
                scores = scores * 0.125 + amask[...]
                e = jnp.exp(scores - jnp.max(scores, axis=0, keepdims=True))
                probs = e * (1.0 / jnp.sum(e, axis=0, keepdims=True))
                inner = jnp.sum(probs * gprobs, axis=0, keepdims=True)
                soft.append((probs.astype(BF), (probs * (gprobs - inner)).astype(BF)))
            grads = [
                (mm_tn(gsc, k), mm(gsc, qs), mm(probs, gas))
                for (k, qs, gas, _, _), (probs, gsc) in zip(units, soft)
            ]
            for c, (both, gk, gv) in zip(heads, grads):
                gq = jnp.where(low_lane, both[:GROUP], both[GROUP:])
                for i, part in enumerate((gq * 0.125, gk * 0.125, gv)):
                    at = pl.ds(pl.multiple_of(start + i * tokens, 16), GROUP)
                    wu[at, c] = part.astype(BF)

    def qkv_bias():
        accs[...] = jnp.zeros_like(accs)

        @pl.loop(0, tokens // 48, unroll=3)
        def _(i):
            at = pl.ds(pl.multiple_of(i * 48, 16), 48)
            accs[0:8, :] += fold(wu[at, :].astype(F32))
            accs[8:16, :] += fold(wu[pl.ds(pl.multiple_of(2 * tokens + i * 48, 16), 48), :].astype(F32))

        for i in range(2):
            vec[9:10, width * i:width * i + width] = jnp.sum(accs[8 * i:8 * i + 8, :], axis=0, keepdims=True)

    def bias_blocks():
        stage[0:32, :] = split_bias(vec[9:10, 0:2 * width], 48)
        stage[32:64, :] = split_bias(vec[8:9, 0:width], 24)
        stage[64:96, :] = split_bias(vec[0:1, :], 96)
        stage[96:128, :] = split_bias(vec[7:8, 0:width], 24)

        @pl.loop(0, 32)
        def _(d):
            at = (d // 8, (d // 4) % 2, (d // 2) % 2, d % 2)
            for r in range(4):
                sbuf[at + (slice(r, r + 1), slice(None))] = stage[pl.ds(32 * r + d, 1), :]
            sbuf[at + (slice(4, 8), slice(None))] = jnp.zeros((4, 128), F32)

    def mod_block():
        rows = []
        for m in range(6):
            row = vec[1 + m:2 + m, 0:width]
            rows += [row[:, :HALF], row[:, HALF:]]
        rows.append(jnp.zeros((4, HALF), F32))
        mbuf[p.z, p.c, p.y, p.x, :, :] = jnp.concatenate(rows, axis=0).astype(BF)

    def mod_grads():
        flat = mbuf[...].reshape(512, HALF)
        gmy = gmy_ref[:, 0:32]
        cond = jnp.zeros((32, 32), F32)
        gmb_out[:, 6 * width:] = jnp.zeros((1, 256), F32)
        for i in range(12):
            cols = slice(HALF * i, HALF * i + HALF)
            every = pick_row(flat, i)
            low = every.astype(BF)
            gmw_out[:, cols] = mm_tn(gmy, low)[:24]
            gmb_out[:, cols] = jnp.sum(every, axis=0, keepdims=True)
            cond = cond + mm_nt(low, mwp_ref[:, cols])
        mine = (p.z, p.c, p.y, p.x)
        cbuf[mine + (slice(None), slice(None))] = jnp.zeros((32, 128), F32)
        cbuf[mine + (slice(None), slice(0, 32))] = cond

    def cond_out():
        @pl.loop(0, 32)
        def _(d):
            cg_out[pl.ds(d, 1), :] = cbuf[d // 8, (d // 4) % 2, (d // 2) % 2, d % 2, pl.ds(p.me, 1), :]

    def do(tag, *span):
        if isinstance(tag, int):
            (reds + [bred, mgath, cgath])[tag // 10].step(tag % 10)
        elif tag == "MB":
            mod_block()
        elif tag == "BB":
            bias_blocks()
        elif tag == "LD":
            rows = pl.ds(384, 192)
            load("far", 16, dg_hbm.at[:, 1 - p.c], gbuf.at[:, 1 - p.c, :, :, rows, :])
            load("near", 17, dg_hbm.at[:, p.c], gbuf.at[:, p.c, :, :, rows, :])
            load("gb", 0, gb_hbm, gb)
            load("wd", 1, wd_hbm, wa)
            load("gp", 2, gp_hbm, gh)
            load("n2", 3, n2_hbm, nb)
            for i in range(4):
                load("u%d" % i, 12 + i, wu_hbm.at[:, pl.ds(width * i, width)], wu.at[pl.ds(width * i, width), :])
            load("mid", 5, mid_hbm, mid)
            load("br", 6, br_hbm, br)
            p.greet()
            pending["far"].wait()
        elif tag == "ST":
            vec[...] = jnp.zeros_like(vec)
            vec[6:7, 0:width] = mod_ref[6:7, :]
            vec[7:8, 0:width] = mod_ref[7:8, :]
            shape = amask.shape
            same = iota(shape, 0) // frames == iota(shape, 1) % GROUP // frames
            amask[...] = jnp.where(same, 0.0, -1e30)
            pending["near"].wait()
        elif tag == "A":
            if span == (0,):
                pending["gb"].wait()
                pending["wd"].wait()
                pending["gp"].wait()
            act_grad(*span)
            if span == (5,):
                load("og", 0, og_hbm, gb)
                for i in range(3):
                    load("w%d" % i, 7 + i, wq_hbm.at[:, pl.ds(width * i, width)], wa.at[pl.ds(width * i, width), :])
                load("wp", 10, wp_hbm, wa.at[pl.ds(3 * width, width), :])
        elif tag[0] == "U":
            i = int(tag[1])
            if i == 0:
                pending["n2"].wait()
            weight_grad(nb, gh.at[:, pl.ds(width * i, width)], 4 + i)
            if i == 3:
                load("att", 3, att_hbm, nb)
        elif tag == "N0":
            j = span[0]
            if j == 0:
                for i in range(4):
                    pending["u%d" % i].wait()
            wide = [wu[width * i + 256 * j:width * i + 256 * j + 256, :] for i in range(4)]
            total = mm_nt(gh[...], jnp.concatenate(wide, axis=1))
            gn[:, 256 * j:256 * j + 256] = total
            if j == 2:
                load("qkv", 2, qkv_hbm, gh.at[:, pl.ds(0, 3 * width)])
        elif tag == "L2":
            for name in ("mid", "br", "og"):
                pending[name].wait()
            norm2_back()
            load("x", 6, x_hbm, br)
        elif tag == "PG":
            pending["att"].wait()
            weight_grad(nb, gh.at[:, pl.ds(3 * width, width)], 3)
            load("n1", 3, n1_hbm, nb)
        elif tag == "PA":
            for name in ("w0", "w1", "w2", "wp"):
                pending[name].wait()
            gb[...] = mm_nt(gh[:, 3 * width:4 * width], wa[3 * width:4 * width, :]).astype(BF)
        elif tag == "AB":
            if span[0] == 0:
                pending["qkv"].wait()
            attention_back(*span)
        elif tag in ("Q0", "Q1", "Q2"):
            if tag == "Q0":
                pending["n1"].wait()
            i = int(tag[1])
            weight_grad(nb, wu.at[pl.ds(tokens * i, tokens), :], i)
        elif tag == "N1":
            j = span[0]
            total = mm_nt(wu[0:tokens, :], wa[256 * j:256 * j + 256, :])
            for i in (1, 2):
                total = total + mm_nt(
                    wu[tokens * i:tokens * i + tokens, :], wa[width * i + 256 * j:width * i + 256 * j + 256, :]
                )
            mid[:, 256 * j:256 * j + 256] = total
        elif tag == "L1":
            pending["x"].wait()
            norm1_back()
        elif tag == "TG":
            turn_back(gn, step, raw)
            load("tg", 11, raw, tg_hbm.at[0])
        elif tag == "BI":
            qkv_bias()
        elif tag == "GM":
            mod_grads()
        elif tag == "CO":
            cond_out()

    for tag in B_SEQ:
        do(*(tag if isinstance(tag, tuple) else (tag,)))
    pending["tg"].wait()
    for item in reds + [bred, mgath, cgath]:
        item.finish()


def backward(shape, xt, ogt, codes, mod, gmy, mwp, n1, qkv, att, br, mid, n2, dg, gp, gb, wq, wp, wu, wd):
    t, d = xt.shape
    hid = gp.shape[1]
    s = jax.ShapeDtypeStruct
    outs = [
        s(shape, BF), s((24, 3 * d), F32), s((24, d), F32), s((24, hid), F32), s((96, d), F32), s((8, 128), F32),
        s((24, 6 * d), F32), s((1, 6 * d + 256), F32), s((32, 128), F32),
    ]
    v = pltpu.VMEM
    dma = pltpu.SemaphoreType.DMA
    scratch = [
        v((4, 2, 2, 2, SHARD, HALF), BF), *landing(SHARD, HALF, BF, SHARD - 96), *landing_z(96, HALF, BF),
        v((4, 2, 2, 2, 8, 128), F32), *small_landing(8, 128),
        v((4, 2, 2, 2, 16, HALF), BF), v((4, 2, 2, 2, 32, 128), F32), v((128, 128), F32),
        v((hid, d), BF), v((hid, d), BF), v((t, hid), BF), v((t, d), BF), v((t, d), BF),
        v((t, d), F32), v((t, d), F32), v((t, d), BF), v((GROUP, 2 * GROUP), F32), v((16, hid), F32), v((32, d), F32), v(shape[1:], BF), v((2 * t, 128), F32),
        dma((8, 11)), dma((8, 11)), dma((1, 11)), dma((1, 11)), dma((2, 11)), dma((2, 11)), dma((18,)),
    ]
    return pl.pallas_call(
        b_kernel,
        out_shape=outs,
        in_specs=[ANY, ANY, pl.BlockSpec(memory_space=pltpu.SMEM)] + [VMEM] * 3 + [ANY] * 13,
        out_specs=[ANY] + [VMEM] * 8,
        scratch_shapes=scratch,
        compiler_params=pltpu.CompilerParams(collective_id=1, has_side_effects=True, vmem_limit_bytes=VMEM_LIMIT),
        cost_estimate=pl.CostEstimate(flops=29 * 10**9, bytes_accessed=70 * 10**6, transcendentals=10**6),
        name="backward",
    )(xt, ogt, codes, mod, gmy, mwp, n1, qkv, att, br, mid, n2, dg, gp, gb, wq, wp, wu, wd)


def o_kernel(bias_ref, gmb_ref, cg_ref, slope_ref, *refs):
    srcs, (cond, modb, qvb, projb, upb, downb), dsts, held, sem = refs[:7], refs[7:13], refs[13:20], refs[20:27], refs[27]
    loads = [pltpu.make_async_copy(a, b, sem.at[0, i]) for i, (a, b) in enumerate(zip(srcs, held))]
    stores = [pltpu.make_async_copy(a, b, sem.at[1, i]) for i, (a, b) in enumerate(zip(held, dsts))]
    for cp in loads:
        cp.start()
    p = Place()
    for i, ref in enumerate((qvb, projb, upb, downb)):
        ref[...] = bias_ref[i:i + 1, :ref.shape[1]]
    n = modb.shape[1]
    start = p.me * n
    window = gmb_ref[:, pl.ds(pl.multiple_of(start // 128 * 128, 128), 384)]
    modb[...] = pltpu.roll(window, 384 - start % 128, 1)[:, :n]
    width = cond.shape[1]
    rows = width // 32
    lane, col = iota((128, width), 0), iota((128, width), 1)
    ones = jnp.where((col % rows == lane) & (lane < rows), 1.0, 0.0)
    grid = jnp.dot(cg_ref[...], ones, precision=lax.Precision.HIGHEST, preferred_element_type=F32)
    mine = iota((32, width), 1) // rows == iota((32, width), 0)
    cond[...] = jnp.sum(jnp.where(mine, grid, 0.0), axis=0, keepdims=True) * slope_ref[...]
    for one, two in zip(loads, stores):
        one.wait()
        two.start()
    for cp in stores:
        cp.wait()


def outputs(big, bias, gmb, cg, slope, mod_n):
    d = slope.shape[1]
    s = jax.ShapeDtypeStruct
    small = [s((1, d), F32), s((1, mod_n), F32)] + [s((1, n), F32) for n in (48, 24, 96, 24)]
    return pl.pallas_call(
        o_kernel,
        out_shape=small + [s(a.shape, a.dtype) for a in big],
        in_specs=[VMEM] * 4 + [ANY] * 7,
        out_specs=[VMEM] * 6 + [ANY] * 7,
        scratch_shapes=[pltpu.VMEM(a.shape, a.dtype) for a in big] + [pltpu.SemaphoreType.DMA((2, 7))],
        compiler_params=pltpu.CompilerParams(vmem_limit_bytes=VMEM_LIMIT),
        name="place_outputs",
    )(bias, gmb, cg, slope, *big)


def time_embed(noise_steps, model_width):
    half_width = model_width // 2
    frequency = jnp.exp(-math.log(10000.0) * jnp.arange(half_width, dtype=jnp.float32) / half_width)
    angles = noise_steps.astype(jnp.float32)[:, None] * frequency[None, :]
    return jnp.concatenate([jnp.cos(angles), jnp.sin(angles)], axis=-1)


def fast_local(
    tokens, condition, timesteps, loss_codes, out_grad, mod_weight, mod_bias, qkv_weight, qv_bias,
    proj_weight, proj_bias, up_weight, up_bias, down_weight, down_bias,
):
    cond = condition + time_embed(timesteps, tokens.shape[3])
    gate = jax.nn.sigmoid(cond)
    gated = (cond * gate).astype(BF)
    slope = gate * (1.0 + cond * (1.0 - gate))
    row = lambda a: a[None]
    bo, xt, ogt, n1, qkv, att, br, mid, n2, dg, gp, gb, wq, wp, wu, wd, mod, gmy, mwp = forward(
        tokens, out_grad, loss_codes, gated, row(qv_bias), row(proj_bias), row(up_bias), row(down_bias), row(mod_bias),
        mod_weight, qkv_weight, proj_weight, up_weight, down_weight,
    )
    tg, g_qkv, g_proj, g_up, g_down, bias, g_mod, gb_mod, cg = backward(
        tokens.shape, xt, ogt, loss_codes, mod, gmy, mwp, n1, qkv, att, br, mid, n2, dg, gp, gb, wq, wp, wu, wd
    )
    big = (bo, tg, g_mod, g_qkv, g_proj, g_up, g_down)
    cond_grad, modb, qvb, projb, upb, downb, *big = outputs(big, bias, gb_mod, cg, slope, mod_bias.shape[0])
    bo, tg, g_mod, g_qkv, g_proj, g_up, g_down = big
    return (
        bo, tg, cond_grad, g_mod, modb[0], g_qkv, qvb[0], g_proj, projb[0], g_up, upb[0], g_down, downb[0],
    )


def layernorm(inputs):
    center = inputs - jnp.mean(inputs, axis=-1, keepdims=True)
    spread = jnp.mean(center * center, axis=-1, keepdims=True)
    return center * lax.rsqrt(spread + 1e-06)


def modulate(inputs, shift_part, scale_part):
    return layernorm(inputs) * (1.0 + scale_part) + shift_part


def softmax_last(scores):
    return jax.nn.softmax(scores, axis=-1)


def gelu_tanh(inputs):
    return jax.nn.gelu(inputs, approximate=True)


def product(left_side, right_side):
    return jnp.dot(left_side, right_side, preferred_element_type=jnp.float32)


def column_sum(inputs):
    return jnp.sum(inputs.astype(jnp.float32), axis=0)


def local(
    tokens,
    condition,
    timesteps,
    loss_codes,
    out_grad,
    mod_weight,
    mod_bias,
    qkv_weight,
    qv_bias,
    proj_weight,
    proj_bias,
    up_weight,
    up_bias,
    down_weight,
    down_bias,
):
    gathered = (
        lax.all_gather(mod_weight, ("wide", "narrow"), axis=0, tiled=True),
        lax.all_gather(mod_bias, ("wide", "narrow"), axis=0, tiled=True),
        lax.all_gather(qkv_weight, ("wide", "narrow"), axis=0, tiled=True),
        lax.all_gather(qv_bias, ("wide", "narrow"), axis=0, tiled=True),
        lax.all_gather(proj_weight, ("wide", "narrow"), axis=0, tiled=True),
        lax.all_gather(proj_bias, ("wide", "narrow"), axis=0, tiled=True),
        lax.all_gather(up_weight, ("wide", "narrow"), axis=0, tiled=True),
        lax.all_gather(up_bias, ("wide", "narrow"), axis=0, tiled=True),
        lax.all_gather(down_weight, ("wide", "narrow"), axis=0, tiled=True),
        lax.all_gather(down_bias, ("wide", "narrow"), axis=0, tiled=True),
    )
    (
        mod_full,
        modb_full,
        qkv_full,
        qvb_full,
        proj_full,
        projb_full,
        up_full,
        upb_full,
        down_full,
        downb_full,
    ) = gathered
    frames = tokens.shape[1]
    patches = tokens.shape[2]
    model_width = tokens.shape[3]
    head_count = model_width // HEAD_DIM
    scale_factor = HEAD_DIM ** (-0.5)
    shape_four = (frames, patches, head_count, HEAD_DIM)
    conditioning = condition[0] + time_embed(timesteps, model_width)[0]
    silu_value, silu_back = jax.vjp(jax.nn.silu, conditioning)
    gated = silu_value.astype(jnp.bfloat16)
    modulation = product(gated[None, :], mod_full)[0] + modb_full.astype(jnp.float32)
    shift_first, scale_first, gate_first, shift_second, scale_second, gate_second = jnp.split(
        modulation, 6
    )
    token_rows = tokens[0].reshape(frames * patches, model_width).astype(jnp.float32)
    normed_value, first_norm_back = jax.vjp(modulate, token_rows, shift_first, scale_first)
    normed = normed_value.astype(jnp.bfloat16)
    projected = product(normed, qkv_full)
    queries = (
        (projected[:, :model_width] + qvb_full[:model_width].astype(jnp.float32))
        .astype(jnp.bfloat16)
        .reshape(shape_four)
    )
    keys_all = projected[:, model_width : 2 * model_width].astype(jnp.bfloat16).reshape(shape_four)
    values_all = (
        (projected[:, 2 * model_width :] + qvb_full[model_width:].astype(jnp.float32))
        .astype(jnp.bfloat16)
        .reshape(shape_four)
    )
    scores = (
        jnp.einsum("fphd,gphd->phfg", queries, keys_all, preferred_element_type=jnp.float32)
        * scale_factor
    )
    soft_value, softmax_back = jax.vjp(softmax_last, scores)
    softened = soft_value.astype(jnp.bfloat16)
    attended_four = jnp.einsum(
        "phfg,gphd->fphd", softened, values_all, preferred_element_type=jnp.float32
    )
    attended = attended_four.reshape(frames * patches, model_width).astype(jnp.bfloat16)
    branch_first = product(attended, proj_full) + projb_full.astype(jnp.float32)
    middle = token_rows + gate_first * branch_first
    second_value, second_norm_back = jax.vjp(modulate, middle, shift_second, scale_second)
    normed_second = second_value.astype(jnp.bfloat16)
    hidden = product(normed_second, up_full) + upb_full.astype(jnp.float32)
    gelu_value, gelu_back = jax.vjp(gelu_tanh, hidden)
    activated = gelu_value.astype(jnp.bfloat16)
    branch_second = product(activated, down_full) + downb_full.astype(jnp.float32)
    result = middle + gate_second * branch_second
    block_output = result.astype(jnp.bfloat16).reshape(tokens.shape)
    mod_back, qkv_back, proj_back, up_back, down_back = (
        lax.all_gather(mod_weight, ("wide", "narrow"), axis=0, tiled=True),
        lax.all_gather(qkv_weight, ("wide", "narrow"), axis=0, tiled=True),
        lax.all_gather(proj_weight, ("wide", "narrow"), axis=0, tiled=True),
        lax.all_gather(up_weight, ("wide", "narrow"), axis=0, tiled=True),
        lax.all_gather(down_weight, ("wide", "narrow"), axis=0, tiled=True),
    )
    clip_weight = (loss_codes[0].astype(jnp.float32) + 1.0) * 0.25
    cotangent = out_grad[0].reshape(frames * patches, model_width).astype(jnp.float32) * clip_weight
    grad_gate_second = jnp.sum(cotangent * branch_second, axis=0)
    grad_branch_second = (cotangent * gate_second).astype(jnp.bfloat16)
    grad_down = jnp.einsum(
        "rk,rd->kd", activated, grad_branch_second, preferred_element_type=jnp.float32
    )
    grad_down_bias = column_sum(grad_branch_second)
    grad_activated = jnp.einsum(
        "rd,kd->rk", grad_branch_second, down_back, preferred_element_type=jnp.float32
    )
    grad_hidden = gelu_back(grad_activated)[0].astype(jnp.bfloat16)
    grad_up = jnp.einsum(
        "rd,rk->dk", normed_second, grad_hidden, preferred_element_type=jnp.float32
    )
    grad_up_bias = column_sum(grad_hidden)
    grad_normed_second = jnp.einsum(
        "rk,dk->rd", grad_hidden, up_back, preferred_element_type=jnp.float32
    )
    middle_part, grad_shift_second, grad_scale_second = second_norm_back(grad_normed_second)
    grad_middle = cotangent + middle_part
    grad_gate_first = jnp.sum(grad_middle * branch_first, axis=0)
    grad_branch_first = (grad_middle * gate_first).astype(jnp.bfloat16)
    grad_proj = jnp.einsum(
        "re,rd->ed", attended, grad_branch_first, preferred_element_type=jnp.float32
    )
    grad_proj_bias = column_sum(grad_branch_first)
    grad_attended = (
        jnp.einsum("rd,ed->re", grad_branch_first, proj_back, preferred_element_type=jnp.float32)
        .astype(jnp.bfloat16)
        .reshape(shape_four)
    )
    grad_softened = jnp.einsum(
        "fphd,gphd->phfg", grad_attended, values_all, preferred_element_type=jnp.float32
    )
    grad_values = jnp.einsum(
        "phfg,fphd->gphd", softened, grad_attended, preferred_element_type=jnp.float32
    ).astype(jnp.bfloat16)
    grad_scores = softmax_back(grad_softened)[0].astype(jnp.bfloat16)
    grad_queries = (
        jnp.einsum("phfg,gphd->fphd", grad_scores, keys_all, preferred_element_type=jnp.float32)
        * scale_factor
    ).astype(jnp.bfloat16)
    grad_keys = (
        jnp.einsum("phfg,fphd->gphd", grad_scores, queries, preferred_element_type=jnp.float32)
        * scale_factor
    ).astype(jnp.bfloat16)
    flat_shape = (frames * patches, model_width)
    grad_projected = jnp.concatenate(
        [
            grad_queries.reshape(flat_shape),
            grad_keys.reshape(flat_shape),
            grad_values.reshape(flat_shape),
        ],
        axis=1,
    )
    grad_qkv = jnp.einsum("rd,rk->dk", normed, grad_projected, preferred_element_type=jnp.float32)
    grad_qv_bias = jnp.concatenate(
        [column_sum(grad_queries.reshape(flat_shape)), column_sum(grad_values.reshape(flat_shape))]
    )
    grad_normed = jnp.einsum(
        "rk,dk->rd", grad_projected, qkv_back, preferred_element_type=jnp.float32
    )
    token_part, grad_shift_first, grad_scale_first = first_norm_back(grad_normed)
    tokens_grad = (grad_middle + token_part).astype(jnp.bfloat16).reshape(tokens.shape)
    grad_modulation = jnp.concatenate(
        [
            grad_shift_first,
            grad_scale_first,
            grad_gate_first,
            grad_shift_second,
            grad_scale_second,
            grad_gate_second,
        ]
    ).astype(jnp.bfloat16)
    grad_gated = jnp.einsum(
        "ij,j->i", mod_back, grad_modulation, preferred_element_type=jnp.float32
    )
    condition_grad = silu_back(grad_gated)[0][None, :]
    remaining = (
        grad_qkv,
        grad_qv_bias,
        grad_proj,
        grad_proj_bias,
        grad_up,
        grad_up_bias,
        grad_down,
        grad_down_bias,
    )
    grad_mod = jnp.einsum("i,j->ij", gated, grad_modulation, preferred_element_type=jnp.float32)
    grad_mod_bias = grad_modulation.astype(jnp.float32)
    gradients = (grad_mod, grad_mod_bias) + remaining
    owned = lax.psum_scatter(gradients, ("wide", "narrow"), scatter_dimension=0, tiled=True)
    owned_mod = owned[0]
    owned_mod_bias = owned[1]
    rest_owned = owned[2:]
    return (
        block_output,
        tokens_grad,
        condition_grad,
        owned_mod,
        owned_mod_bias,
        rest_owned[0],
        rest_owned[1],
        rest_owned[2],
        rest_owned[3],
        rest_owned[4],
        rest_owned[5],
        rest_owned[6],
        rest_owned[7],
    )


def solution(mesh):
    axes = ("wide", "narrow")
    four, two, one = P(axes, None, None, None), P(axes, None), P(axes)
    in_specs = (four, two, one, one, four, two, one, two, one, two, one, two, one, two, one)
    out_specs = (four, four, two, two, one, two, one, two, one, two, one, two, one)
    body = fast_local if (mesh.shape["wide"], mesh.shape["narrow"]) == (8, 4) else local
    return jax.shard_map(body, mesh=mesh, in_specs=in_specs, out_specs=out_specs, check_vma=False)
```

```python
import math

import jax
import jax.numpy as jnp
from jax import lax
from jax.experimental import pallas as pl
from jax.experimental.pallas import tpu as pltpu
from jax.sharding import PartitionSpec as P

HEAD_DIM = 64
VMEM_LIMIT = 63 * 2**20


BF = jnp.bfloat16
F32 = jnp.float32
MESH = pl.DeviceIdType.MESH
ANY = pl.BlockSpec(memory_space=pl.ANY)
VMEM = pl.BlockSpec(memory_space=pltpu.VMEM)
BLOCKS = 12
SHARD = 48 * BLOCKS
SMALL = SHARD + 16
HALF = 384
GROUP = 96


def mm(a, b):
    return jnp.dot(a, b, preferred_element_type=F32)


def mm_nt(a, b):
    return lax.dot_general(a, b, (((1,), (1,)), ((), ())), preferred_element_type=F32)


def mm_tn(a, b):
    return lax.dot_general(a, b, (((0,), (0,)), ((), ())), preferred_element_type=F32)


class Place:
    def __init__(self):
        wide = lax.axis_index("wide")
        narrow = lax.axis_index("narrow")
        self.z, self.c = wide // 2, wide % 2
        self.y, self.x = narrow // 2, narrow % 2
        self.me = wide * 4 + narrow

    def dev(self, z=None, c=None, y=None, x=None):
        z = self.z if z is None else z
        c = self.c if c is None else c
        y = self.y if y is None else y
        x = self.x if x is None else x
        return (z * 2 + c, y * 2 + x)

    def peers(self):
        column = [self.dev(z=(self.z + i) % 4) for i in (1, 2, 3)]
        plane = [self.dev(x=1 - self.x), self.dev(y=1 - self.y), self.dev(y=1 - self.y, x=1 - self.x)]
        return column, plane, self.dev(c=1 - self.c)

    def greet(self):
        bar = pltpu.get_barrier_semaphore()
        column, plane, sibling = self.peers()
        for target in column + plane + [sibling]:
            pl.semaphore_signal(bar, inc=1, device_id=target, device_id_type=MESH)
        pl.semaphore_wait(bar, 7)


def when(cond, act):
    pl.when(cond)(act)


class Gather:
    def __init__(self, place, buf, ssem, rsem, k, rows):
        self.p, self.buf, self.ssem, self.rsem, self.k, self.rows = place, buf, ssem, rsem, k, rows

    def copy(self, i, idx, dev):
        ref = self.buf.at[idx + (self.rows, slice(None))]
        return pltpu.make_async_remote_copy(
            ref, ref, self.ssem.at[self.k, i], self.rsem.at[self.k, i], device_id=dev, device_id_type=MESH
        )

    def up(self, h, op):
        p = self.p
        if op == "recv":
            when(p.z >= h, lambda: self.copy(h - 1, (p.z - h, p.c, p.y, p.x), p.dev(x=1 - p.x)).wait_recv())
            return
        cp = lambda: self.copy(h - 1, (p.z - (h - 1), p.c, p.y, p.x), p.dev(z=p.z + 1))
        when((p.z <= 2) & (p.z >= h - 1), (lambda: cp().start()) if op == "start" else (lambda: cp().wait_send()))

    def down(self, h, op):
        p = self.p
        if op == "recv":
            when(p.z + h <= 3, lambda: self.copy(h + 2, (p.z + h, p.c, p.y, p.x), p.dev(x=1 - p.x)).wait_recv())
            return
        cp = lambda: self.copy(h + 2, (p.z + (h - 1), p.c, p.y, p.x), p.dev(z=p.z - 1))
        when((p.z >= 1) & (p.z + (h - 1) <= 3), (lambda: cp().start()) if op == "start" else (lambda: cp().wait_send()))

    def plane(self):
        p = self.p
        low, high, every = pl.ds(0, 2), pl.ds(2, 2), slice(None)
        return (
            ((low, p.c, p.y, p.x), p.dev(x=1 - p.x), (low, p.c, p.y, 1 - p.x)),
            ((high, p.c, p.y, p.x), p.dev(y=1 - p.y), (high, p.c, 1 - p.y, p.x)),
            ((low, p.c, p.y, every), p.dev(y=1 - p.y), (low, p.c, 1 - p.y, every)),
            ((high, p.c, every, p.x), p.dev(x=1 - p.x), (high, p.c, every, 1 - p.x)),
            ((every, p.c, every, every), p.dev(c=1 - p.c), (every, 1 - p.c, every, every)),
        )

    def step(self, s):
        if 1 <= s <= 3:
            self.up(s, "recv")
            if s < 3:
                self.up(s + 1, "start")
            self.down(s, "recv")
            if s < 3:
                self.down(s + 1, "start")
        if s == 0:
            self.up(1, "start")
            self.down(1, "start")
        table = self.plane()
        starts = {3: (0, 1), 4: (2, 3), 5: (4,)}.get(s, ())
        recvs = {4: (0, 1), 5: (2, 3), 6: (4,)}.get(s, ())
        for i in recvs:
            self.copy(6 + i, table[i][2], table[i][1]).wait_recv()
        for i in starts:
            self.copy(6 + i, table[i][0], table[i][1]).start()

    def finish(self):
        for h in (1, 2, 3):
            self.up(h, "sent")
            self.down(h, "sent")
        for i, row in enumerate(self.plane()):
            self.copy(6 + i, row[0], row[1]).wait_send()


class GatherZ(Gather):
    def table(self):
        p = self.p
        every = slice(None)
        return (
            (0, (p.z, p.c, p.y, p.x), p.dev(x=1 - p.x), (p.z, p.c, p.y, 1 - p.x)),
            (1, (p.z, p.c, p.y, p.x), p.dev(y=1 - p.y), (p.z, p.c, 1 - p.y, p.x)),
            (0, (p.z, p.c, p.y, every), p.dev(y=1 - p.y), (p.z, p.c, 1 - p.y, every)),
            (1, (p.z, p.c, every, p.x), p.dev(x=1 - p.x), (p.z, p.c, every, 1 - p.x)),
        )

    def part(self, i, half, idx, dev):
        n = self.rows.size // 2
        ref = self.buf.at[idx + (pl.ds(self.rows.start + half * n, n), slice(None))]
        return pltpu.make_async_remote_copy(
            ref, ref, self.ssem.at[self.k, i], self.rsem.at[self.k, i], device_id=dev, device_id_type=MESH
        )

    def line(self, h, op, sign):
        p = self.p
        every = slice(None)
        i = (3 if sign > 0 else 6) + h
        reach = (lambda n: p.z - n >= 0) if sign > 0 else (lambda n: p.z + n <= 3)
        if op == "recv":
            when(reach(h), lambda: self.copy(i, (p.z - sign * h, p.c, every, every), p.dev(x=1 - p.x)).wait_recv())
            return
        cp = lambda: self.copy(i, (p.z - sign * (h - 1), p.c, every, every), p.dev(z=p.z + sign))
        can = (p.z <= 2) if sign > 0 else (p.z >= 1)
        when(can & reach(h - 1), (lambda: cp().start()) if op == "start" else (lambda: cp().wait_send()))

    def step(self, s):
        table = self.table()
        for i in {1: (0, 1), 2: (2, 3)}.get(s, ()):
            self.part(i, table[i][0], table[i][3], table[i][2]).wait_recv()
        for i in {0: (0, 1), 1: (2, 3)}.get(s, ()):
            self.part(i, *table[i][:3]).start()
        for sign in (1, -1):
            if 3 <= s <= 5:
                self.line(s - 2, "recv", sign)
            if 2 <= s <= 4:
                self.line(s - 1, "start", sign)
        last = self.plane()[4]
        if s == 5:
            self.copy(10, last[0], last[1]).start()
        if s == 6:
            self.copy(10, last[2], last[1]).wait_recv()

    def finish(self):
        for i, row in enumerate(self.table()):
            self.part(i, *row[:3]).wait_send()
        for h in (1, 2, 3):
            self.line(h, "sent", 1)
            self.line(h, "sent", -1)
        last = self.plane()[4]
        self.copy(10, last[0], last[1]).wait_send()


class Reduce:
    def __init__(self, place, buf, land, ssem, rsem, k, rows, final):
        self.p, self.buf, self.land, self.ssem, self.rsem, self.k, self.rows = place, buf, land, ssem, rsem, k, rows
        self.final = final

    def copy(self, i, idx, land, lidx, dev):
        tail = (self.rows, slice(None))
        return pltpu.make_async_remote_copy(
            self.buf.at[idx + tail], land.at[lidx + tail], self.ssem.at[self.k, i], self.rsem.at[self.k, i],
            device_id=dev, device_id_type=MESH,
        )

    def table(self):
        p = self.p
        low, high, every = pl.ds(0, 2), pl.ds(2, 2), slice(None)
        core, a2, b2, a1, b1, zd, zu = self.land
        return (
            ((every, 1 - p.c, every, every), core, (every, every, every), p.dev(c=1 - p.c)),
            ((low, p.c, 1 - p.y, every), a2, (every, every), p.dev(y=1 - p.y)),
            ((high, p.c, every, 1 - p.x), b2, (every, every), p.dev(x=1 - p.x)),
            ((low, p.c, p.y, 1 - p.x), a1, (every,), p.dev(x=1 - p.x)),
            ((high, p.c, 1 - p.y, p.x), b1, (every,), p.dev(y=1 - p.y)),
        )

    def add(self, idx, land, lidx):
        tail = (self.rows, slice(None))
        self.buf[idx + tail] = self.buf[idx + tail] + land[lidx + tail]

    def down(self, t, op):
        p, zd = self.p, self.land[5]
        if op == "recv":
            def take():
                self.copy(4 + t, (p.z - 3 + t, p.c, p.y, p.x), zd, (t - 1,), p.dev(x=1 - p.x)).wait_recv()
                if t < 3:
                    self.add((p.z - 3 + t, p.c, p.y, p.x), zd, (t - 1,))
            when((p.z <= 2) & (p.z - 3 + t >= 0), take)
            return
        cp = lambda: self.copy(4 + t, (p.z - 4 + t, p.c, p.y, p.x), zd, (t - 1,), p.dev(z=p.z - 1))
        when((p.z >= 1) & (p.z - 4 + t >= 0), (lambda: cp().start()) if op == "start" else (lambda: cp().wait_send()))

    def up(self, t, op):
        p, zu = self.p, self.land[6]
        if op == "recv":
            def take():
                self.copy(7 + t, (p.z + 3 - t, p.c, p.y, p.x), zu, (t - 1,), p.dev(x=1 - p.x)).wait_recv()
                if t < 3:
                    self.add((p.z + 3 - t, p.c, p.y, p.x), zu, (t - 1,))
            when((p.z >= 1) & (p.z + 3 - t <= 3), take)
            return
        cp = lambda: self.copy(7 + t, (p.z + 4 - t, p.c, p.y, p.x), zu, (t - 1,), p.dev(z=p.z + 1))
        when((p.z <= 2) & (p.z + 4 - t <= 3), (lambda: cp().start()) if op == "start" else (lambda: cp().wait_send()))

    def step(self, s):
        p = self.p
        core, a2, b2, a1, b1, zd, zu = self.land
        table = self.table()
        starts = {0: (0,), 1: (1, 2), 2: (3, 4)}.get(s, ())
        recvs = {1: (0,), 2: (1, 2), 3: (3, 4)}.get(s, ())
        for i in recvs:
            row = table[i]
            self.copy(i, row[0], row[1], row[2], row[3]).wait_recv()
        if s == 1:
            @pl.loop(0, 16)
            def _(i):
                zi, yi, xi = i // 4, (i // 2) % 2, i % 2
                self.add((zi, p.c, yi, xi), core, (zi, yi, xi))
        if s == 2:
            @pl.loop(0, 4)
            def _(i):
                self.add((i // 2, p.c, p.y, i % 2), a2, (i // 2, i % 2))
                self.add((2 + i // 2, p.c, i % 2, p.x), b2, (i // 2, i % 2))
        if s == 3:
            @pl.loop(0, 2)
            def _(i):
                self.add((i, p.c, p.y, p.x), a1, (i,))
                self.add((2 + i, p.c, p.y, p.x), b1, (i,))
        for i in starts:
            row = table[i]
            self.copy(i, row[0], row[1], row[2], row[3]).start()
        if s == 3:
            self.down(1, "start")
            self.up(1, "start")
        if s in (4, 5):
            t = s - 3
            self.down(t, "recv")
            self.down(t + 1, "start")
            self.up(t, "recv")
            self.up(t + 1, "start")
        if s == 6:
            self.down(3, "recv")
            self.up(3, "recv")
            tail = (self.rows, slice(None))
            own = self.buf[(p.z, p.c, p.y, p.x) + tail].astype(F32)
            from_above = zd[(2,) + tail].astype(F32)
            from_below = zu[(2,) + tail].astype(F32)
            self.final(
                jnp.where(p.z < 3, own + from_above, own) + jnp.where(p.z > 0, from_below, jnp.zeros_like(own))
            )

    def finish(self):
        for t in (1, 2, 3):
            self.down(t, "sent")
            self.up(t, "sent")
        for i, row in enumerate(self.table()):
            self.copy(i, row[0], row[1], row[2], row[3]).wait_send()


class ReduceZ:
    def __init__(self, place, buf, land, ssem, rsem, k, rows, final):
        self.p, self.buf, self.land, self.ssem, self.rsem, self.k, self.rows = place, buf, land, ssem, rsem, k, rows
        self.final = final
        n = rows.size // 2
        self.half = [pl.ds(rows.start, n), pl.ds(rows.start + n, n)]

    def copy(self, i, src, dst, dev):
        return pltpu.make_async_remote_copy(
            src, dst, self.ssem.at[self.k, i], self.rsem.at[self.k, i], device_id=dev, device_id_type=MESH
        )

    def at(self, idx, rows):
        return self.buf.at[idx + (rows, slice(None))]

    def core(self):
        p, every = self.p, slice(None)
        land = self.land[0].at[:, :, :, self.rows, :]
        return self.copy(0, self.at((every, 1 - p.c, every, every), self.rows), land, p.dev(c=1 - p.c))

    def flat(self, i):
        p, every = self.p, slice(None)
        _, _, _, a2, b2, a1, b1 = self.land
        far_x, far_y = p.dev(x=1 - p.x), p.dev(y=1 - p.y)
        row = (
            ((p.z, p.c, 1 - p.y, every), 0, a2, far_y), ((p.z, p.c, every, 1 - p.x), 1, b2, far_x),
            ((p.z, p.c, p.y, 1 - p.x), 0, a1, far_x), ((p.z, p.c, 1 - p.y, p.x), 1, b1, far_y),
        )[i]
        return self.copy(7 + i, self.at(row[0], self.half[row[1]]), row[2], row[3])

    def line(self, t, op, sign):
        p, every = self.p, slice(None)
        i = (0 if sign > 0 else 3) + t
        land = self.land[1 if sign > 0 else 2].at[t - 1]
        fits = (lambda n: p.z - n >= 0) if sign > 0 else (lambda n: p.z + n <= 3)
        can_take = (p.z <= 2) if sign > 0 else (p.z >= 1)
        can_send = (p.z >= 1) if sign > 0 else (p.z <= 2)
        if op == "recv":
            s = p.z - sign * (3 - t)

            def take():
                self.copy(i, self.at((s, p.c, every, every), self.rows), land, p.dev(x=1 - p.x)).wait_recv()
                for j in range(4):
                    at = (s, p.c, j // 2, j % 2, self.rows, slice(None))
                    self.buf[at] = self.buf[at] + land[j // 2, j % 2]
            when(can_take & fits(3 - t), take)
            return
        cp = lambda: self.copy(
            i, self.at((p.z - sign * (4 - t), p.c, every, every), self.rows), land, p.dev(z=p.z - sign)
        )
        when(can_send & fits(4 - t), (lambda: cp().start()) if op == "start" else (lambda: cp().wait_send()))

    def step(self, s):
        p = self.p
        core, _, _, a2, b2, a1, b1 = self.land
        tail = slice(None)
        if s == 0:
            self.core().start()
        if s == 1:
            self.core().wait_recv()

            @pl.loop(0, 16)
            def _(i):
                zi, yi, xi = i // 4, (i // 2) % 2, i % 2
                at = (zi, p.c, yi, xi, self.rows, tail)
                self.buf[at] = self.buf[at] + core[zi, yi, xi, self.rows, :]
        for sign in (1, -1):
            if 2 <= s <= 4:
                self.line(s - 1, "recv", sign)
            if 1 <= s <= 3:
                self.line(s, "start", sign)
        one, two = self.half
        if s == 4:
            self.flat(0).start()
            self.flat(1).start()
        if s == 5:
            self.flat(0).wait_recv()
            self.flat(1).wait_recv()
            for j in range(2):
                at = (p.z, p.c, p.y, j, one, tail)
                self.buf[at] = self.buf[at] + a2[j]
                at = (p.z, p.c, j, p.x, two, tail)
                self.buf[at] = self.buf[at] + b2[j]
            self.flat(2).start()
            self.flat(3).start()
        if s == 6:
            self.flat(2).wait_recv()
            self.flat(3).wait_recv()
            mine = (p.z, p.c, p.y, p.x)
            top = self.buf[mine + (one, tail)].astype(F32) + a1[...].astype(F32)
            low = self.buf[mine + (two, tail)].astype(F32) + b1[...].astype(F32)
            self.final(jnp.concatenate([top, low], axis=0))

    def finish(self):
        self.core().wait_send()
        for t in (1, 2, 3):
            self.line(t, "sent", 1)
            self.line(t, "sent", -1)
        for i in range(4):
            self.flat(i).wait_send()


def landing_z(rows, cols, dtype):
    v = pltpu.VMEM
    half = rows // 2
    return [
        v((3, 2, 2, rows, cols), dtype), v((3, 2, 2, rows, cols), dtype), v((2, half, cols), dtype),
        v((2, half, cols), dtype), v((half, cols), dtype), v((half, cols), dtype),
    ]


class SmallGather:
    def __init__(self, place, buf, ssem, rsem, k, rows):
        self.p, self.buf, self.ssem, self.rsem, self.k, self.rows = place, buf, ssem, rsem, k, rows

    def copy(self, i, idx, dev):
        ref = self.buf.at[idx + (self.rows, slice(None))]
        return pltpu.make_async_remote_copy(
            ref, ref, self.ssem.at[self.k, i], self.rsem.at[self.k, i], device_id=dev, device_id_type=MESH
        )

    def table(self):
        p = self.p
        column, plane, sibling = p.peers()
        every = slice(None)
        first = [(i, (p.z, p.c, p.y, p.x), column[i], ((p.z + 3 - i) % 4, p.c, p.y, p.x)) for i in range(3)]
        far = [(p.y, 1 - p.x), (1 - p.y, p.x), (1 - p.y, 1 - p.x)]
        second = [(3 + i, (every, p.c, p.y, p.x), plane[i], (every, p.c) + far[i]) for i in range(3)]
        third = [(6, (every, p.c, every, every), sibling, (every, 1 - p.c, every, every))]
        return first, second, third

    def step(self, s):
        hops = self.table()
        if s > 0:
            for i, _, dev, came in hops[s - 1]:
                self.copy(i, came, dev).wait_recv()
        if s < 3:
            for i, idx, dev, _ in hops[s]:
                self.copy(i, idx, dev).start()

    def finish(self):
        for hop in self.table():
            for i, idx, dev, _ in hop:
                self.copy(i, idx, dev).wait_send()


class SmallReduce:
    def __init__(self, place, buf, land, ssem, rsem, k, rows, final):
        self.p, self.buf, self.land, self.ssem, self.rsem, self.k = place, buf, land, ssem, rsem, k
        self.final = final
        self.tail = (rows, slice(None))

    def copy(self, i, idx, dst, dev):
        return pltpu.make_async_remote_copy(
            self.buf.at[idx + self.tail], dst, self.ssem.at[self.k, i], self.rsem.at[self.k, i], device_id=dev, device_id_type=MESH
        )

    def table(self):
        p = self.p
        column, plane, sibling = p.peers()
        every = slice(None)
        core, flat, line = self.land
        tail = self.tail
        far = [(p.y, 1 - p.x), (1 - p.y, p.x), (1 - p.y, 1 - p.x)]
        first = [(0, (every, 1 - p.c, every, every), core.at[(every, every, every) + tail], sibling)]
        second = [(1 + i, (every, p.c) + far[i], flat.at[(i, every) + tail], plane[i]) for i in range(3)]
        third = [(4 + i, ((p.z + 1 + i) % 4, p.c, p.y, p.x), line.at[(i,) + tail], column[i]) for i in range(3)]
        return first, second, third

    def step(self, s):
        p = self.p
        core, flat, line = self.land
        hops = self.table()
        tail = self.tail
        every = slice(None)
        if s > 0:
            for i, idx, dst, dev in hops[s - 1]:
                self.copy(i, idx, dst, dev).wait_recv()
        if s == 1:
            at = (every, p.c, every, every) + tail
            self.buf[at] = self.buf[at] + core[(every, every, every) + tail]
        if s == 2:
            at = (every, p.c, p.y, p.x) + tail
            came = [flat[(i, every) + tail] for i in range(3)]
            self.buf[at] = self.buf[at] + (came[0] + came[1] + came[2])
        if s < 3:
            for i, idx, dst, dev in hops[s]:
                self.copy(i, idx, dst, dev).start()
        else:
            came = [line[(i,) + tail] for i in range(3)]
            self.final(self.buf[(p.z, p.c, p.y, p.x) + tail] + came[0] + came[1] + came[2])

    def finish(self):
        for hop in self.table():
            for i, idx, dst, dev in hop:
                self.copy(i, idx, dst, dev).wait_send()


def small_landing(rows, cols):
    return [
        pltpu.VMEM((4, 2, 2, rows, cols), F32), pltpu.VMEM((3, 4, rows, cols), F32), pltpu.VMEM((3, rows, cols), F32)
    ]


def landing(rows, cols, dtype, kept):
    return [
        pltpu.VMEM((4, 2, 2, rows, cols), dtype),
        pltpu.VMEM((2, 2, kept, cols), dtype),
        pltpu.VMEM((2, 2, kept, cols), dtype),
        pltpu.VMEM((2, kept, cols), dtype),
        pltpu.VMEM((2, kept, cols), dtype),
        pltpu.VMEM((3, kept, cols), dtype),
        pltpu.VMEM((3, kept, cols), dtype),
    ]


def pack48(block):
    wide = block.astype(F32)
    return jnp.concatenate([wide[:, :HALF], wide[:, HALF:]], axis=0).astype(BF)


def iota(shape, dim):
    return lax.broadcasted_iota(jnp.int32, shape, dim)


def onehot(cond):
    return jnp.where(cond, 1.0, 0.0).astype(BF)


def ln_hat(v):
    center = v - jnp.mean(v, axis=-1, keepdims=True)
    spread = jnp.mean(center * center, axis=-1, keepdims=True)
    return center * lax.rsqrt(spread + 1e-06)


def fold(v):
    total = v[0:8]
    for i in range(1, v.shape[0] // 8):
        total = total + v[8 * i:8 * i + 8]
    return total


def turn(src, step, put):
    frames, patches, width = src.shape
    count = frames * patches
    for h in range(width // 128):
        base = count * (h % 2)
        cols = slice(128 * h, 128 * h + 128)
        for f in range(frames):
            step[pl.ds(base + f, patches, stride=frames), :] = src[f, :, cols].astype(F32)
        put(cols, step[base:base + count, :])


def turn_back(src, step, dst):
    frames, patches, width = dst.shape
    count = frames * patches
    for h in range(width // 128):
        base = count * (h % 2)
        cols = slice(128 * h, 128 * h + 128)
        step[base:base + count, :] = src[:, cols]
        for f in range(frames):
            dst[f, :, cols] = step[pl.ds(base + f, patches, stride=frames), :].astype(BF)


def pick_row(flat, r):
    return mm(onehot(iota((32, 512), 1) == iota((32, 512), 0) * 16 + r), flat)


def spread_bias(rows, n, start, width):
    k = rows.shape[1]
    lane = iota((k, width), 0)
    col = iota((k, width), 1) + start
    grid = mm(rows.astype(BF), onehot((col % n == lane) & (lane < n)))
    dev = iota((32, width), 0)
    mine = (iota((32, width), 1) + start) // n == dev
    return jnp.sum(jnp.where(mine, grid, 0.0), axis=0, keepdims=True)


def softmax_rows(scores):
    e = jnp.exp(scores - jnp.max(scores, axis=-1, keepdims=True))
    return e * (1.0 / jnp.sum(e, axis=-1, keepdims=True))


def group_start(g, tokens):
    return pl.multiple_of(jnp.minimum(g * GROUP, tokens - GROUP), 16)


def fill_mask(mask_ref, frames):
    shape = mask_ref.shape
    row = iota(shape, 0) % GROUP
    mask_ref[...] = jnp.where(row // frames == iota(shape, 1) // frames, 0.0, -1e30)


F_SEQ = (
    30, 80, 10, 20, 0, "IO", 81, 31, 11, 21, 1, 32, 40, 12, 22, 33, 50, 70, 60, 2, 13, 23, 3, 41, 34, "PM", 51, 90,
    "PN", 100, 91, 42, 14, 61, 24, "XH", 43, 35, 92, 52, 101, "BI", 71, 93, 36, "R2", 62, 15, 82, "MV", 53, 25, "LN",
    16, 26, 63, 102, "R0", ("QK", 0,), 44, "R1", 72, ("QK", 1,), 54, ("QK", 2,), 83, 103, ("AT", 0, 1), "MW",
    ("AT", 1, 2), ("AT", 2, 3), 64, ("AT", 3, 4), ("AT", 4, 5), ("AT", 5, 6), 45, 73, ("AT", 6, 7), ("AT", 7, 8), 46,
    "R3", ("AT", 8, 9), ("AT", 9, 10), "GB", 84, 55, ("AT", 10, 11), "PR", "L2", 56, "R4", ("UP", 0,), 65, ("UP", 1,),
    85, 74, ("UP", 2,), 66, "R5", ("UP", 3,), ("UP", 4,), ("UP", 5,), 86, 75, ("DG", 0,), ("DG", 1,), ("DG", 2,),
    ("DG", 3,), ("DG", 4,), 76, "R6", "R7", ("DG", 5,), ("DG", 6,), "DN0", ("DG", 7,), "DN1",
)


F_LAST = (8,)
F_ROWS = ((0, 48), (48, 48), (96, 48), (144, 48), (192, 96), (288, 96), (384, 96), (480, 96))


def f_kernel(
    x_hbm, og_hbm, code_ref, gated_ref, qv_ref, pb_ref, ub_ref, db_ref, mb_ref, mw_ref, qw_ref, pw_ref, uw_ref, dw_ref,
    bo_hbm, xt_hbm, ogt_hbm, n1_hbm, qkv_hbm, att_hbm, br_hbm, mid_hbm, n2_hbm, dg_hbm, gp_hbm, gb_hbm,
    wq_hbm, wp_hbm, wu_hbm, wd_hbm, mod_out, gmy_out, mwp_out,
    gbuf, pm, pbuf, l0, l1, l2, dbuf,
    wq, wp, wu, wd, x_v, og_v, n_v, qkv, att, br, mid, act, gpt, raw, gb, amask, bq, bp, bu, bd, acc, step, sm, mb,
    gs, gr, ps, pr, lsem, gpsem, dsem,
):
    p = Place()
    tokens, width = x_v.shape
    rows_of = [slice(SHARD, SMALL)] + [slice(a, a + n) for a, n in F_ROWS]
    gath = [
        (SmallGather if k == 0 else GatherZ if k in F_LAST else Gather)(p, gbuf, gs, gr, k, pl.ds(r.start, r.stop - r.start)) for k, r in enumerate(rows_of)
    ]
    loads = [pltpu.make_async_copy(h.at[0], raw.at[i], lsem.at[i]) for i, h in enumerate((x_hbm, og_hbm))]
    for cp in loads:
        cp.start()
    outs = []
    saved = []

    def save(src, dst):
        cp = pltpu.make_async_copy(src, dst, lsem.at[2 + len(saved)])
        cp.start()
        outs.append(cp)
        saved.append(cp)
        return cp

    def finish(cp):
        cp.wait()
        outs[:] = [o for o in outs if o is not cp]

    own = (p.z, p.c, p.y, p.x)
    weight = (code_ref[0].astype(F32) + 1.0) * 0.25
    sm[...] = jnp.zeros_like(sm)
    sm[0:1, :] = gated_ref[:, :HALF].astype(F32)
    sm[1:2, :] = gated_ref[:, HALF:].astype(F32)
    for i, ref in enumerate((qv_ref, pb_ref, ub_ref, db_ref, mb_ref)):
        sm[2 + i:3 + i, 0:ref.shape[1]] = ref[...].astype(F32)
    gbuf[own + (slice(SHARD, SMALL), slice(None))] = sm[...].astype(BF)
    for b in range(3):
        gbuf[own + (slice(48 * b, 48 * b + 48), slice(None))] = pack48(qw_ref[:, width * b:width * b + width])
    gbuf[own + (slice(144, 192), slice(None))] = pack48(pw_ref[...])
    for b in range(4):
        gbuf[own + (slice(192 + 48 * b, 240 + 48 * b), slice(None))] = pack48(uw_ref[:, width * b:width * b + width])
    gbuf[own + (slice(384, 480), slice(None))] = dw_ref[:, :HALF]
    gbuf[own + (slice(480, 576), slice(None))] = dw_ref[:, HALF:]
    p.greet()

    frames = x_hbm.shape[1]

    def final_mod(pieces):
        def go(total):
            for i, m in enumerate(pieces):
                for j in range(6):
                    mod_out[m:m + 1, 128 * j:128 * j + 128] = total[6 * i + j:6 * i + j + 1, :]
        return go

    land = (l0, l1, l2)
    first = SmallReduce(p, pbuf, land, ps, pr, 0, pl.ds(0, 16), final_mod((0, 1)))
    second = SmallReduce(p, pbuf, land, ps, pr, 1, pl.ds(16, 24), final_mod((2, 3, 4, 5)))
    items = gath + [first, second]

    def small_rows():
        fill_mask(amask, frames)
        acc[...] = jnp.zeros_like(acc)
        mod_out[6:8, :] = jnp.zeros((2, width), F32)
        flat = gbuf[:, :, :, :, SHARD:SMALL, :].reshape(512, HALF)
        gated = jnp.concatenate([pick_row(flat, 0), pick_row(flat, 1)], axis=1).astype(BF)
        sel = onehot((iota((width, 128), 0) == p.me * 24 + iota((width, 128), 1)) & (iota((width, 128), 1) < 24))
        gmy_out[...] = mm(gated, sel).astype(BF)

    def small_work(pieces, base, rows):
        pad = jnp.zeros((8, width), F32)
        for m in pieces:
            cols = slice(width * m, width * m + width)
            part = jnp.concatenate([mw_ref[:, cols].astype(F32), pad], axis=0).astype(BF)
            mwp_out[:, cols] = part
            prod = mm(gmy_out[:, :32], part)
            for j in range(6):
                pm[32 * (6 * m + j):32 * (6 * m + j) + 32, :] = prod[:, 128 * j:128 * j + 128]
        count = 6 * len(pieces)

        @pl.loop(0, 32)
        def _(d):
            at = (d // 8, (d // 4) % 2, (d // 2) % 2, d % 2)
            for j in range(count):
                pbuf[at + (slice(base + j, base + j + 1), slice(None))] = pm[pl.ds(32 * (6 * pieces[0] + j) + d, 1), :]
            if rows > count:
                pbuf[at + (slice(base + count, base + rows), slice(None))] = jnp.zeros((rows - count, 128), F32)

    def biases():
        flat = gbuf[:, :, :, :, SHARD:SMALL, :].reshape(512, HALF)
        qv, prj, up, dn, md = (pick_row(flat, r) for r in (2, 3, 4, 5, 6))
        bq[:, 0:width] = spread_bias(qv[:, :128], 48, 0, width)
        bq[:, width:2 * width] = jnp.zeros((1, width), F32)
        bq[:, 2 * width:] = spread_bias(qv[:, :128], 48, width, width)
        bp[...] = spread_bias(prj[:, :128], 24, 0, width)
        bd[...] = spread_bias(dn[:, :128], 24, 0, width)
        for m in range(4):
            bu[:, width * m:width * m + width] = spread_bias(up[:, :128], 96, width * m, width)
        for m in range(6):
            mb[m:m + 1, :] = spread_bias(md[:, :256], 144, width * m, width)

    def unpack(b, dst, col):
        @pl.loop(0, 16)
        def _(i):
            src = (i // 4, (i // 2) % 2, i % 2)
            one = gbuf[src + (0, slice(48 * b, 48 * b + 48), slice(None))].astype(F32)
            two = gbuf[src + (1, slice(48 * b, 48 * b + 48), slice(None))].astype(F32)
            at = pl.ds(pl.multiple_of(i * 48, 16), 48)
            dst[at, col:col + HALF] = jnp.concatenate([one[:24], two[:24]], axis=0).astype(BF)
            dst[at, col + HALF:col + 2 * HALF] = jnp.concatenate([one[24:], two[24:]], axis=0).astype(BF)

    def unpack_down(h):
        @pl.loop(0, 32)
        def _(d):
            wd[pl.ds(pl.multiple_of(d * 96, 16), 96), HALF * h:HALF * h + HALF] = gbuf[
                d // 8, (d // 4) % 2, (d // 2) % 2, d % 2, 384 + 96 * h:480 + 96 * h, :
            ]

    def rows_loop(body):
        @pl.loop(0, tokens // 48, unroll=7)
        def _(i):
            body(pl.ds(pl.multiple_of(i * 48, 16), 48))

    def put_x(cols, value):
        mid[:, cols] = value
        x_v[:, cols] = value.astype(BF)

    def put_og(cols, value):
        og_v[:, cols] = value.astype(BF)

    def first_hat(at):
        mid[at, :] = ln_hat(mid[at, :])

    def first_norm(at):
        n_v[at, :] = (mid[at, :] * (1.0 + mod_out[1:2, :]) + mod_out[0:1, :]).astype(BF)

    def second_norm(at):
        n_v[at, :] = (ln_hat(mid[at, :]) * (1.0 + mod_out[4:5, :]) + mod_out[3:4, :]).astype(BF)

    def qkv_block(i):
        for j in range(width * i, width * i + width, 256):
            cols = slice(j, j + 256)
            qkv[:, cols] = (mm(n_v[...], wq[:, cols]) + bq[:, cols]).astype(BF)

    def attention(first, last):
        low_lane = iota((GROUP, 128), 1) < 64

        @pl.loop(first, last)
        def _(g):
            rows = pl.ds(group_start(g, tokens), GROUP)
            heads = [slice(128 * h, 128 * h + 128) for h in range(width // 128)]
            values = [qkv[rows, 2 * width + c.start:2 * width + c.stop] for c in heads]
            scores = []
            for c in heads:
                q = qkv[rows, c]
                k = qkv[rows, width + c.start:width + c.stop]
                zero = jnp.zeros_like(q)
                qs = jnp.concatenate([jnp.where(low_lane, q, zero), jnp.where(low_lane, zero, q)], axis=0)
                scores.append(mm_nt(qs, k))
            probs = [softmax_rows(a * 0.125 + amask[...]).astype(BF) for a in scores]
            both = [mm(a, v) for a, v in zip(probs, values)]
            for c, a in zip(heads, both):
                att[rows, c] = jnp.where(low_lane, a[:GROUP], a[GROUP:]).astype(BF)

    def proj():
        branch = mm(att[...], wp[...]) + bp[...]
        br[...] = branch.astype(BF)
        mid[...] = x_v[...].astype(F32) + mod_out[2:3, :] * branch

    def second_cot(at):
        low = (og_v[at, :].astype(F32) * weight * mod_out[5:6, :]).astype(BF)
        gb[at, :] = low
        acc[...] += fold(low.astype(F32))

    def dg_copy(j):
        return pltpu.make_async_copy(dbuf.at[j % 2], dg_hbm.at[j // 2, j % 2], dsem.at[j % 2])

    def down_grad(j):
        if j >= 2:
            dg_copy(j - 2).wait()
        grad = mm_tn(act[:, HALF * j:HALF * j + HALF], gb[...])
        for dd in range(4):
            part = grad[96 * dd:96 * dd + 96].astype(BF)
            dbuf[j % 2, dd // 2, dd % 2, 0:96, :] = part[:, :HALF]
            dbuf[j % 2, dd // 2, dd % 2, 96:192, :] = part[:, HALF:]
        dg_copy(j).start()

    def gp_copy(j):
        return pltpu.make_async_copy(gpt.at[j % 2], gp_hbm.at[:, pl.ds(256 * j, 256)], gpsem.at[j % 2])

    def up_tile(j):
        cols = slice(256 * j, 256 * j + 256)
        if j >= 2:
            gp_copy(j - 2).wait()
        hid = mm(n_v[...], wu[:, cols]) + bu[:, cols]
        sq = hid * hid
        slope_in = 0.7978845608 + (0.7978845608 * 0.044715) * sq
        half = 0.5 + 0.5 * jnp.tanh(hid * slope_in)
        act[:, cols] = (hid * half).astype(BF)
        rate = 2.0 * 0.7978845608 + (6.0 * 0.7978845608 * 0.044715) * sq
        gpt[j % 2] = (half + (hid * rate) * (half - half * half)).astype(BF)
        gp_copy(j).start()

    def down_tile(j):
        cols = slice(256 * j, 256 * j + 256)
        branch = mm(act[...], wd[:, cols]) + bd[:, cols]
        mid[:, cols] += mod_out[5:6, cols] * branch
        cot = og_v[:, cols].astype(F32) * weight
        mod_out[6:7, cols] = jnp.sum(cot * branch, axis=0, keepdims=True)

    n1_out = []

    def do(tag, *span):
        if isinstance(tag, int):
            items[tag // 10].step(tag % 10)
        elif tag == "PM":
            small_rows()
            small_work((0, 1), 0, 16)
        elif tag == "PN":
            small_work((2, 3, 4, 5), 16, 24)
        elif tag == "IO":
            loads[1].wait()
            turn(raw.at[1], step, put_og)
            save(og_v, ogt_hbm)
        elif tag == "XH":
            loads[0].wait()
            turn(raw.at[0], step, put_x)
            rows_loop(first_hat)
            save(x_v, xt_hbm)
        elif tag == "BI":
            biases()
        elif tag == "MV":
            mod_out[0:2, :] += mb[0:2, :]
        elif tag == "MW":
            mod_out[2:6, :] += mb[2:6, :]
        elif tag in ("R0", "R1", "R2", "R3"):
            b = int(tag[1])
            if b < 3:
                unpack(b, wq, width * b)
            else:
                unpack(b, wp, 0)
                save(wp, wp_hbm)
        elif tag == "LN":
            rows_loop(first_norm)
            n1_out.append(save(n_v, n1_hbm))
        elif tag == "QK":
            qkv_block(*span)
            if span == (2,):
                save(wq, wq_hbm)
                save(qkv, qkv_hbm)
        elif tag == "AT":
            attention(*span)
            if span[1] == 11:
                save(att, att_hbm)
        elif tag == "PR":
            proj()
            save(br, br_hbm)
            n1_out.append(save(mid, mid_hbm))
            finish(n1_out[0])
        elif tag == "L2":
            rows_loop(second_norm)
            save(n_v, n2_hbm)
        elif tag in ("R4", "R5"):
            b = 4 if tag == "R4" else 6
            unpack(b, wu, width * (b - 4))
            unpack(b + 1, wu, width * (b - 3))
        elif tag == "UP":
            if span == (3,):
                save(wu, wu_hbm)
            up_tile(2 * span[0])
            up_tile(2 * span[0] + 1)
        elif tag == "GB":
            rows_loop(second_cot)
            mod_out[7:8, :] = jnp.sum(acc[...], axis=0, keepdims=True)
            save(gb, gb_hbm)
        elif tag == "DG":
            down_grad(*span)
        elif tag in ("R6", "R7"):
            unpack_down(int(tag[1]) - 6)
        elif tag == "DN0":
            finish(n1_out[1])
            down_tile(0)
        elif tag == "DN1":
            save(wd, wd_hbm)
            down_tile(1)
            down_tile(2)
            turn_back(mid, step, raw.at[0])
            save(raw.at[0], bo_hbm.at[0])

    for tag in F_SEQ:
        do(*(tag if isinstance(tag, tuple) else (tag,)))
    for j in (10, 11):
        gp_copy(j).wait()
    for j in (6, 7):
        dg_copy(j).wait()
    for cp in outs:
        cp.wait()
    for item in items:
        item.finish()


def forward(tokens, out_grad, codes, *rest):
    _, frames, patches, d = tokens.shape
    t, hid = frames * patches, rest[9].shape[1]
    s = jax.ShapeDtypeStruct
    outs = [
        s(tokens.shape, BF), s((t, d), BF), s((t, d), BF), s((t, d), BF), s((t, 3 * d), BF), s((t, d), BF), s((t, d), BF), s((t, d), F32), s((t, d), BF),
        s((4, 2, 2, 2, 192, HALF), BF), s((t, hid), BF), s((t, d), BF),
        s((d, 3 * d), BF), s((d, d), BF), s((d, hid), BF), s((hid, d), BF),
        s((8, d), F32), s((32, 128), BF), s((32, 6 * d), BF),
    ]
    v = pltpu.VMEM
    scratch = [
        v((4, 2, 2, 2, SMALL, HALF), BF), v((6 * d // 128 * 32, 128), F32), v((4, 2, 2, 2, 40, 128), F32), *small_landing(40, 128), v((2, 2, 2, 192, HALF), BF),
        v((d, 3 * d), BF), v((d, d), BF), v((d, hid), BF), v((hid, d), BF),
        v((t, d), BF), v((t, d), BF), v((t, d), BF), v((t, 3 * d), BF), v((t, d), BF), v((t, d), BF), v((t, d), F32),
        v((t, hid), BF), v((2, t, 256), BF), v((2, frames, patches, d), BF), v((t, d), BF), v((2 * GROUP, GROUP), F32),
        v((1, 3 * d), F32), v((1, d), F32), v((1, hid), F32), v((1, d), F32), v((8, d), F32), v((2 * t, 128), F32), v((16, HALF), F32), v((8, d), F32),
        pltpu.SemaphoreType.DMA((9, 11)), pltpu.SemaphoreType.DMA((9, 11)),
        pltpu.SemaphoreType.DMA((2, 11)), pltpu.SemaphoreType.DMA((2, 11)),
        pltpu.SemaphoreType.DMA((24,)), pltpu.SemaphoreType.DMA((2,)), pltpu.SemaphoreType.DMA((2,)),
    ]
    return pl.pallas_call(
        f_kernel,
        out_shape=outs,
        in_specs=[ANY, ANY, pl.BlockSpec(memory_space=pltpu.SMEM)] + [VMEM] * len(rest),
        out_specs=[ANY] * 16 + [VMEM] * 3,
        scratch_shapes=scratch,
        compiler_params=pltpu.CompilerParams(collective_id=0, has_side_effects=True, vmem_limit_bytes=VMEM_LIMIT),
        cost_estimate=pl.CostEstimate(flops=15 * 10**9, bytes_accessed=70 * 10**6, transcendentals=4 * 10**6),
        name="forward",
    )(tokens, out_grad, codes, *rest)


B_SEQ = (
    "LD", "ST", 10, 0, ("A", 0,), ("A", 1,), ("A", 2,), ("A", 3,), ("A", 4,), ("A", 5,), "U0", "U1", 11, 20, "U2",
    "U3", 30, ("N0", 0,), ("N0", 1,), 1, 21, ("N0", 2,), 12, "L2", "PA", ("AB", 0, 1), 2, 22, "PG", 40, ("AB", 1, 2),
    ("AB", 2, 3), ("AB", 3, 4), 31, ("AB", 4, 5), ("AB", 5, 6), 13, ("AB", 6, 7), ("AB", 7, 8), 41, 23, ("AB", 8, 9),
    ("AB", 9, 10), ("AB", 10, 11), "Q0", 14, "Q1", 50, 32, 24, ("N1", 0,), 60, ("N1", 1,), 51, 15, ("N1", 2,), 61, 25,
    33, "L1", "MB", 90, 42, "Q2", 26, 34, "BI", 3, 91, 70, 62, "BB", 80, 35, 71, 92, 52, "TG", 63, 81, 43, 93, "GM",
    100, 72, 4, 36, 16, 53, 44, 73, 101, 64, 54, 45, 74, 82, 65, 5, 55, 102, 46, 75, 66, 6, 103, "CO", 56, 83, 76,
)
B_FIRST = (0,)
CHUNKS = ((480, 96), (384, 96), (192, 96), (288, 96), (144, 48), (0, 48), (48, 48), (96, 48))


def ln_parts(v):
    center = v - jnp.mean(v, axis=-1, keepdims=True)
    spread = jnp.mean(center * center, axis=-1, keepdims=True)
    inv = lax.rsqrt(spread + 1e-06)
    return center * inv, inv


def ln_back(g, hat, inv, scale):
    dh = g * (1.0 + scale)
    return inv * (dh - jnp.mean(dh, axis=-1, keepdims=True) - hat * jnp.mean(dh * hat, axis=-1, keepdims=True))


def split_bias(vec, n):
    width = vec.shape[1]
    mine = iota((32, width), 1) // n == iota((32, width), 0)
    lane = iota((width, 128), 1)
    ones = jnp.where((iota((width, 128), 0) % n == lane) & (lane < n), 1.0, 0.0)
    return jnp.dot(jnp.where(mine, vec, 0.0), ones, precision=lax.Precision.HIGHEST, preferred_element_type=F32)


def b_kernel(
    x_hbm, og_hbm, code_ref, mod_ref, gmy_ref, mwp_ref,
    n1_hbm, qkv_hbm, att_hbm, br_hbm, mid_hbm, n2_hbm, dg_hbm, gp_hbm, gb_hbm, wq_hbm, wp_hbm, wu_hbm, wd_hbm,
    tg_hbm, gq_out, gp_out, gu_out, gd_out, bias_out, gmw_out, gmb_out, cg_out,
    gbuf, k0, k1, k2, k3, k4, k5, k6, y1, y2, y3, y4, y5, y6, sbuf, t0, t1, t2, mbuf, cbuf, stage,
    wa, wu, gh, gb, nb, mid, gn, br, amask, vec, accs, raw, step,
    rs, rr, ts, tr, gs, gr, lsem,
):
    p = Place()
    tokens, width = gb.shape
    frames = raw.shape[0]
    cw = (code_ref[0].astype(F32) + 1.0) * 0.25
    pending = {}

    def load(name, i, src, dst):
        pending[name] = pltpu.make_async_copy(src, dst, lsem.at[i])
        pending[name].start()

    def put48(dst_out, b, total):
        dst_out[:, width * b:width * b + HALF] = total[:24]
        dst_out[:, width * b + HALF:width * b + width] = total[24:48]

    def finals(k):
        def go(total):
            if k < 2:
                gd_out[:, HALF * (1 - k):HALF * (2 - k)] = total
            elif k < 4:
                put48(gu_out, 2 * (k - 2), total[:48])
                put48(gu_out, 2 * (k - 2) + 1, total[48:])
            elif k == 4:
                put48(gp_out, 0, total)
            else:
                put48(gq_out, k - 5, total)
        return go

    land = (k0, k1, k2, k3, k4, k5, k6)
    lands = {k: land for k in range(len(CHUNKS))}
    if B_FIRST:
        lands[B_FIRST[0]] = (k0, y1, y2, y3, y4, y5, y6)
    reds = [
        (ReduceZ if k in B_FIRST else Reduce)(p, gbuf, lands[k], rs, rr, k, pl.ds(a, n), finals(k))
        for k, (a, n) in enumerate(CHUNKS)
    ]

    def bias_final(total):
        bias_out[...] = total

    bred = SmallReduce(p, sbuf, (t0, t1, t2), ts, tr, 0, pl.ds(0, 8), bias_final)
    mgath = SmallGather(p, mbuf, gs, gr, 0, pl.ds(0, 16))
    cgath = SmallGather(p, cbuf, gs, gr, 1, pl.ds(0, 32))

    def weight_grad(left_ref, right, b):
        for m in range(2):
            grad = mm_tn(left_ref[:, HALF * m:HALF * m + HALF], right[...])
            for dd in range(16):
                gbuf[2 * m + dd // 8, dd // 4 % 2, dd // 2 % 2, dd % 2, 48 * b:48 * b + 48, :] = pack48(
                    grad[24 * dd:24 * dd + 24]
                )

    def act_grad(j):
        cols = slice(512 * j, 512 * j + 512)
        low = (mm_nt(gb[...], wa[cols, :]) * gh[:, cols].astype(F32)).astype(BF)
        gh[:, cols] = low
        vec[0:1, cols] = jnp.sum(low.astype(F32), axis=0, keepdims=True)

    def norm2_back():
        scale, gate = mod_ref[4:5, :], mod_ref[2:3, :]
        accs[...] = jnp.zeros_like(accs)

        @pl.loop(0, tokens // 48, unroll=3)
        def _(i):
            at = pl.ds(pl.multiple_of(i * 48, 16), 48)
            g = gn[at, :]
            hat, inv = ln_parts(mid[at, :])
            gm = gb[at, :].astype(F32) * cw + ln_back(g, hat, inv, scale)
            gn[at, :] = gm
            low = (gm * gate).astype(BF)
            gh[at, 3 * width:4 * width] = low
            accs[0:8, :] += fold(g)
            accs[8:16, :] += fold(g * hat)
            accs[16:24, :] += fold(gm * br[at, :].astype(F32))
            accs[24:32, :] += fold(low.astype(F32))

        for i, row in enumerate((3, 4, 2)):
            vec[1 + row:2 + row, 0:width] = jnp.sum(accs[8 * i:8 * i + 8, :], axis=0, keepdims=True)
        vec[8:9, 0:width] = jnp.sum(accs[24:32, :], axis=0, keepdims=True)

    def norm1_back():
        scale = mod_ref[1:2, :]
        accs[...] = jnp.zeros_like(accs)

        @pl.loop(0, tokens // 48, unroll=3)
        def _(i):
            at = pl.ds(pl.multiple_of(i * 48, 16), 48)
            g = mid[at, :]
            hat, inv = ln_parts(br[at, :].astype(F32))
            gn[at, :] += ln_back(g, hat, inv, scale)
            accs[0:8, :] += fold(g)
            accs[8:16, :] += fold(g * hat)

        for i in range(2):
            vec[1 + i:2 + i, 0:width] = jnp.sum(accs[8 * i:8 * i + 8, :], axis=0, keepdims=True)

    def attention_back(first, last):
        low_lane = iota((GROUP, 128), 1) < 64

        @pl.loop(first, last)
        def _(g):
            start = group_start(g, tokens)
            rows = pl.ds(start, GROUP)
            heads = [slice(128 * h, 128 * h + 128) for h in range(width // 128)]
            units = []
            for c in heads:
                q, k, v = (gh[rows, width * i + c.start:width * i + c.stop] for i in range(3))
                ga = gb[rows, c]
                zero = jnp.zeros_like(q)
                qs = jnp.concatenate([jnp.where(low_lane, q, zero), jnp.where(low_lane, zero, q)], axis=0)
                gas = jnp.concatenate([jnp.where(low_lane, ga, zero), jnp.where(low_lane, zero, ga)], axis=0)
                units.append((k, qs, gas, mm_nt(k, qs), mm_nt(v, gas)))
            soft = []
            for _, _, _, scores, gprobs in units:
                scores = scores * 0.125 + amask[...]
                e = jnp.exp(scores - jnp.max(scores, axis=0, keepdims=True))
                probs = e * (1.0 / jnp.sum(e, axis=0, keepdims=True))
                inner = jnp.sum(probs * gprobs, axis=0, keepdims=True)
                soft.append((probs.astype(BF), (probs * (gprobs - inner)).astype(BF)))
            grads = [
                (mm_tn(gsc, k), mm(gsc, qs), mm(probs, gas))
                for (k, qs, gas, _, _), (probs, gsc) in zip(units, soft)
            ]
            for c, (both, gk, gv) in zip(heads, grads):
                gq = jnp.where(low_lane, both[:GROUP], both[GROUP:])
                for i, part in enumerate((gq * 0.125, gk * 0.125, gv)):
                    at = pl.ds(pl.multiple_of(start + i * tokens, 16), GROUP)
                    wu[at, c] = part.astype(BF)

    def qkv_bias():
        accs[...] = jnp.zeros_like(accs)

        @pl.loop(0, tokens // 48, unroll=3)
        def _(i):
            at = pl.ds(pl.multiple_of(i * 48, 16), 48)
            accs[0:8, :] += fold(wu[at, :].astype(F32))
            accs[8:16, :] += fold(wu[pl.ds(pl.multiple_of(2 * tokens + i * 48, 16), 48), :].astype(F32))

        for i in range(2):
            vec[9:10, width * i:width * i + width] = jnp.sum(accs[8 * i:8 * i + 8, :], axis=0, keepdims=True)

    def bias_blocks():
        stage[0:32, :] = split_bias(vec[9:10, 0:2 * width], 48)
        stage[32:64, :] = split_bias(vec[8:9, 0:width], 24)
        stage[64:96, :] = split_bias(vec[0:1, :], 96)
        stage[96:128, :] = split_bias(vec[7:8, 0:width], 24)

        @pl.loop(0, 32)
        def _(d):
            at = (d // 8, (d // 4) % 2, (d // 2) % 2, d % 2)
            for r in range(4):
                sbuf[at + (slice(r, r + 1), slice(None))] = stage[pl.ds(32 * r + d, 1), :]
            sbuf[at + (slice(4, 8), slice(None))] = jnp.zeros((4, 128), F32)

    def mod_block():
        rows = []
        for m in range(6):
            row = vec[1 + m:2 + m, 0:width]
            rows += [row[:, :HALF], row[:, HALF:]]
        rows.append(jnp.zeros((4, HALF), F32))
        mbuf[p.z, p.c, p.y, p.x, :, :] = jnp.concatenate(rows, axis=0).astype(BF)

    def mod_grads():
        flat = mbuf[...].reshape(512, HALF)
        gmy = gmy_ref[:, 0:32]
        cond = jnp.zeros((32, 32), F32)
        gmb_out[:, 6 * width:] = jnp.zeros((1, 256), F32)
        for i in range(12):
            cols = slice(HALF * i, HALF * i + HALF)
            every = pick_row(flat, i)
            low = every.astype(BF)
            gmw_out[:, cols] = mm_tn(gmy, low)[:24]
            gmb_out[:, cols] = jnp.sum(every, axis=0, keepdims=True)
            cond = cond + mm_nt(low, mwp_ref[:, cols])
        mine = (p.z, p.c, p.y, p.x)
        cbuf[mine + (slice(None), slice(None))] = jnp.zeros((32, 128), F32)
        cbuf[mine + (slice(None), slice(0, 32))] = cond

    def cond_out():
        @pl.loop(0, 32)
        def _(d):
            cg_out[pl.ds(d, 1), :] = cbuf[d // 8, (d // 4) % 2, (d // 2) % 2, d % 2, pl.ds(p.me, 1), :]

    def do(tag, *span):
        if isinstance(tag, int):
            (reds + [bred, mgath, cgath])[tag // 10].step(tag % 10)
        elif tag == "MB":
            mod_block()
        elif tag == "BB":
            bias_blocks()
        elif tag == "LD":
            rows = pl.ds(384, 192)
            load("far", 16, dg_hbm.at[:, 1 - p.c], gbuf.at[:, 1 - p.c, :, :, rows, :])
            load("near", 17, dg_hbm.at[:, p.c], gbuf.at[:, p.c, :, :, rows, :])
            load("gb", 0, gb_hbm, gb)
            load("wd", 1, wd_hbm, wa)
            load("gp", 2, gp_hbm, gh)
            load("n2", 3, n2_hbm, nb)
            for i in range(4):
                load("u%d" % i, 12 + i, wu_hbm.at[:, pl.ds(width * i, width)], wu.at[pl.ds(width * i, width), :])
            load("mid", 5, mid_hbm, mid)
            load("br", 6, br_hbm, br)
            p.greet()
            pending["far"].wait()
        elif tag == "ST":
            vec[...] = jnp.zeros_like(vec)
            vec[6:7, 0:width] = mod_ref[6:7, :]
            vec[7:8, 0:width] = mod_ref[7:8, :]
            shape = amask.shape
            same = iota(shape, 0) // frames == iota(shape, 1) % GROUP // frames
            amask[...] = jnp.where(same, 0.0, -1e30)
            pending["near"].wait()
        elif tag == "A":
            if span == (0,):
                pending["gb"].wait()
                pending["wd"].wait()
                pending["gp"].wait()
            act_grad(*span)
            if span == (5,):
                load("og", 0, og_hbm, gb)
                for i in range(3):
                    load("w%d" % i, 7 + i, wq_hbm.at[:, pl.ds(width * i, width)], wa.at[pl.ds(width * i, width), :])
                load("wp", 10, wp_hbm, wa.at[pl.ds(3 * width, width), :])
        elif tag[0] == "U":
            i = int(tag[1])
            if i == 0:
                pending["n2"].wait()
            weight_grad(nb, gh.at[:, pl.ds(width * i, width)], 4 + i)
            if i == 3:
                load("att", 3, att_hbm, nb)
        elif tag == "N0":
            j = span[0]
            if j == 0:
                for i in range(4):
                    pending["u%d" % i].wait()
            wide = [wu[width * i + 256 * j:width * i + 256 * j + 256, :] for i in range(4)]
            total = mm_nt(gh[...], jnp.concatenate(wide, axis=1))
            gn[:, 256 * j:256 * j + 256] = total
            if j == 2:
                load("qkv", 2, qkv_hbm, gh.at[:, pl.ds(0, 3 * width)])
        elif tag == "L2":
            for name in ("mid", "br", "og"):
                pending[name].wait()
            norm2_back()
            load("x", 6, x_hbm, br)
        elif tag == "PG":
            pending["att"].wait()
            weight_grad(nb, gh.at[:, pl.ds(3 * width, width)], 3)
            load("n1", 3, n1_hbm, nb)
        elif tag == "PA":
            for name in ("w0", "w1", "w2", "wp"):
                pending[name].wait()
            gb[...] = mm_nt(gh[:, 3 * width:4 * width], wa[3 * width:4 * width, :]).astype(BF)
        elif tag == "AB":
            if span[0] == 0:
                pending["qkv"].wait()
            attention_back(*span)
        elif tag in ("Q0", "Q1", "Q2"):
            if tag == "Q0":
                pending["n1"].wait()
            i = int(tag[1])
            weight_grad(nb, wu.at[pl.ds(tokens * i, tokens), :], i)
        elif tag == "N1":
            j = span[0]
            total = mm_nt(wu[0:tokens, :], wa[256 * j:256 * j + 256, :])
            for i in (1, 2):
                total = total + mm_nt(
                    wu[tokens * i:tokens * i + tokens, :], wa[width * i + 256 * j:width * i + 256 * j + 256, :]
                )
            mid[:, 256 * j:256 * j + 256] = total
        elif tag == "L1":
            pending["x"].wait()
            norm1_back()
        elif tag == "TG":
            turn_back(gn, step, raw)
            load("tg", 11, raw, tg_hbm.at[0])
        elif tag == "BI":
            qkv_bias()
        elif tag == "GM":
            mod_grads()
        elif tag == "CO":
            cond_out()

    for tag in B_SEQ:
        do(*(tag if isinstance(tag, tuple) else (tag,)))
    pending["tg"].wait()
    for item in reds + [bred, mgath, cgath]:
        item.finish()


def backward(shape, xt, ogt, codes, mod, gmy, mwp, n1, qkv, att, br, mid, n2, dg, gp, gb, wq, wp, wu, wd):
    t, d = xt.shape
    hid = gp.shape[1]
    s = jax.ShapeDtypeStruct
    outs = [
        s(shape, BF), s((24, 3 * d), F32), s((24, d), F32), s((24, hid), F32), s((96, d), F32), s((8, 128), F32),
        s((24, 6 * d), F32), s((1, 6 * d + 256), F32), s((32, 128), F32),
    ]
    v = pltpu.VMEM
    dma = pltpu.SemaphoreType.DMA
    scratch = [
        v((4, 2, 2, 2, SHARD, HALF), BF), *landing(SHARD, HALF, BF, SHARD - 96), *landing_z(96, HALF, BF),
        v((4, 2, 2, 2, 8, 128), F32), *small_landing(8, 128),
        v((4, 2, 2, 2, 16, HALF), BF), v((4, 2, 2, 2, 32, 128), F32), v((128, 128), F32),
        v((hid, d), BF), v((hid, d), BF), v((t, hid), BF), v((t, d), BF), v((t, d), BF),
        v((t, d), F32), v((t, d), F32), v((t, d), BF), v((GROUP, 2 * GROUP), F32), v((16, hid), F32), v((32, d), F32), v(shape[1:], BF), v((2 * t, 128), F32),
        dma((8, 11)), dma((8, 11)), dma((1, 11)), dma((1, 11)), dma((2, 11)), dma((2, 11)), dma((18,)),
    ]
    return pl.pallas_call(
        b_kernel,
        out_shape=outs,
        in_specs=[ANY, ANY, pl.BlockSpec(memory_space=pltpu.SMEM)] + [VMEM] * 3 + [ANY] * 13,
        out_specs=[ANY] + [VMEM] * 8,
        scratch_shapes=scratch,
        compiler_params=pltpu.CompilerParams(collective_id=1, has_side_effects=True, vmem_limit_bytes=VMEM_LIMIT),
        cost_estimate=pl.CostEstimate(flops=29 * 10**9, bytes_accessed=70 * 10**6, transcendentals=10**6),
        name="backward",
    )(xt, ogt, codes, mod, gmy, mwp, n1, qkv, att, br, mid, n2, dg, gp, gb, wq, wp, wu, wd)


def o_kernel(bias_ref, gmb_ref, cg_ref, slope_ref, *refs):
    srcs, (cond, modb, qvb, projb, upb, downb), dsts, held, sem = refs[:7], refs[7:13], refs[13:20], refs[20:27], refs[27]
    loads = [pltpu.make_async_copy(a, b, sem.at[0, i]) for i, (a, b) in enumerate(zip(srcs, held))]
    stores = [pltpu.make_async_copy(a, b, sem.at[1, i]) for i, (a, b) in enumerate(zip(held, dsts))]
    for cp in loads:
        cp.start()
    p = Place()
    for i, ref in enumerate((qvb, projb, upb, downb)):
        ref[...] = bias_ref[i:i + 1, :ref.shape[1]]
    n = modb.shape[1]
    start = p.me * n
    window = gmb_ref[:, pl.ds(pl.multiple_of(start // 128 * 128, 128), 384)]
    modb[...] = pltpu.roll(window, 384 - start % 128, 1)[:, :n]
    width = cond.shape[1]
    rows = width // 32
    lane, col = iota((128, width), 0), iota((128, width), 1)
    ones = jnp.where((col % rows == lane) & (lane < rows), 1.0, 0.0)
    grid = jnp.dot(cg_ref[...], ones, precision=lax.Precision.HIGHEST, preferred_element_type=F32)
    mine = iota((32, width), 1) // rows == iota((32, width), 0)
    cond[...] = jnp.sum(jnp.where(mine, grid, 0.0), axis=0, keepdims=True) * slope_ref[...]
    for one, two in zip(loads, stores):
        one.wait()
        two.start()
    for cp in stores:
        cp.wait()


def outputs(big, bias, gmb, cg, slope, mod_n):
    d = slope.shape[1]
    s = jax.ShapeDtypeStruct
    small = [s((1, d), F32), s((1, mod_n), F32)] + [s((1, n), F32) for n in (48, 24, 96, 24)]
    return pl.pallas_call(
        o_kernel,
        out_shape=small + [s(a.shape, a.dtype) for a in big],
        in_specs=[VMEM] * 4 + [ANY] * 7,
        out_specs=[VMEM] * 6 + [ANY] * 7,
        scratch_shapes=[pltpu.VMEM(a.shape, a.dtype) for a in big] + [pltpu.SemaphoreType.DMA((2, 7))],
        compiler_params=pltpu.CompilerParams(vmem_limit_bytes=VMEM_LIMIT),
        name="place_outputs",
    )(bias, gmb, cg, slope, *big)


def time_embed(noise_steps, model_width):
    half_width = model_width // 2
    frequency = jnp.exp(-math.log(10000.0) * jnp.arange(half_width, dtype=jnp.float32) / half_width)
    angles = noise_steps.astype(jnp.float32)[:, None] * frequency[None, :]
    return jnp.concatenate([jnp.cos(angles), jnp.sin(angles)], axis=-1)


def fast_local(
    tokens, condition, timesteps, loss_codes, out_grad, mod_weight, mod_bias, qkv_weight, qv_bias,
    proj_weight, proj_bias, up_weight, up_bias, down_weight, down_bias,
):
    cond = condition + time_embed(timesteps, tokens.shape[3])
    gate = jax.nn.sigmoid(cond)
    gated = (cond * gate).astype(BF)
    slope = gate * (1.0 + cond * (1.0 - gate))
    row = lambda a: a[None]
    bo, xt, ogt, n1, qkv, att, br, mid, n2, dg, gp, gb, wq, wp, wu, wd, mod, gmy, mwp = forward(
        tokens, out_grad, loss_codes, gated, row(qv_bias), row(proj_bias), row(up_bias), row(down_bias), row(mod_bias),
        mod_weight, qkv_weight, proj_weight, up_weight, down_weight,
    )
    tg, g_qkv, g_proj, g_up, g_down, bias, g_mod, gb_mod, cg = backward(
        tokens.shape, xt, ogt, loss_codes, mod, gmy, mwp, n1, qkv, att, br, mid, n2, dg, gp, gb, wq, wp, wu, wd
    )
    big = (bo, tg, g_mod, g_qkv, g_proj, g_up, g_down)
    cond_grad, modb, qvb, projb, upb, downb, *big = outputs(big, bias, gb_mod, cg, slope, mod_bias.shape[0])
    bo, tg, g_mod, g_qkv, g_proj, g_up, g_down = big
    return (
        bo, tg, cond_grad, g_mod, modb[0], g_qkv, qvb[0], g_proj, projb[0], g_up, upb[0], g_down, downb[0],
    )


def layernorm(inputs):
    center = inputs - jnp.mean(inputs, axis=-1, keepdims=True)
    spread = jnp.mean(center * center, axis=-1, keepdims=True)
    return center * lax.rsqrt(spread + 1e-06)


def modulate(inputs, shift_part, scale_part):
    return layernorm(inputs) * (1.0 + scale_part) + shift_part


def softmax_last(scores):
    return jax.nn.softmax(scores, axis=-1)


def gelu_tanh(inputs):
    return jax.nn.gelu(inputs, approximate=True)


def product(left_side, right_side):
    return jnp.dot(left_side, right_side, preferred_element_type=jnp.float32)


def column_sum(inputs):
    return jnp.sum(inputs.astype(jnp.float32), axis=0)


def local(
    tokens,
    condition,
    timesteps,
    loss_codes,
    out_grad,
    mod_weight,
    mod_bias,
    qkv_weight,
    qv_bias,
    proj_weight,
    proj_bias,
    up_weight,
    up_bias,
    down_weight,
    down_bias,
):
    gathered = (
        lax.all_gather(mod_weight, ("wide", "narrow"), axis=0, tiled=True),
        lax.all_gather(mod_bias, ("wide", "narrow"), axis=0, tiled=True),
        lax.all_gather(qkv_weight, ("wide", "narrow"), axis=0, tiled=True),
        lax.all_gather(qv_bias, ("wide", "narrow"), axis=0, tiled=True),
        lax.all_gather(proj_weight, ("wide", "narrow"), axis=0, tiled=True),
        lax.all_gather(proj_bias, ("wide", "narrow"), axis=0, tiled=True),
        lax.all_gather(up_weight, ("wide", "narrow"), axis=0, tiled=True),
        lax.all_gather(up_bias, ("wide", "narrow"), axis=0, tiled=True),
        lax.all_gather(down_weight, ("wide", "narrow"), axis=0, tiled=True),
        lax.all_gather(down_bias, ("wide", "narrow"), axis=0, tiled=True),
    )
    (
        mod_full,
        modb_full,
        qkv_full,
        qvb_full,
        proj_full,
        projb_full,
        up_full,
        upb_full,
        down_full,
        downb_full,
    ) = gathered
    frames = tokens.shape[1]
    patches = tokens.shape[2]
    model_width = tokens.shape[3]
    head_count = model_width // HEAD_DIM
    scale_factor = HEAD_DIM ** (-0.5)
    shape_four = (frames, patches, head_count, HEAD_DIM)
    conditioning = condition[0] + time_embed(timesteps, model_width)[0]
    silu_value, silu_back = jax.vjp(jax.nn.silu, conditioning)
    gated = silu_value.astype(jnp.bfloat16)
    modulation = product(gated[None, :], mod_full)[0] + modb_full.astype(jnp.float32)
    shift_first, scale_first, gate_first, shift_second, scale_second, gate_second = jnp.split(
        modulation, 6
    )
    token_rows = tokens[0].reshape(frames * patches, model_width).astype(jnp.float32)
    normed_value, first_norm_back = jax.vjp(modulate, token_rows, shift_first, scale_first)
    normed = normed_value.astype(jnp.bfloat16)
    projected = product(normed, qkv_full)
    queries = (
        (projected[:, :model_width] + qvb_full[:model_width].astype(jnp.float32))
        .astype(jnp.bfloat16)
        .reshape(shape_four)
    )
    keys_all = projected[:, model_width : 2 * model_width].astype(jnp.bfloat16).reshape(shape_four)
    values_all = (
        (projected[:, 2 * model_width :] + qvb_full[model_width:].astype(jnp.float32))
        .astype(jnp.bfloat16)
        .reshape(shape_four)
    )
    scores = (
        jnp.einsum("fphd,gphd->phfg", queries, keys_all, preferred_element_type=jnp.float32)
        * scale_factor
    )
    soft_value, softmax_back = jax.vjp(softmax_last, scores)
    softened = soft_value.astype(jnp.bfloat16)
    attended_four = jnp.einsum(
        "phfg,gphd->fphd", softened, values_all, preferred_element_type=jnp.float32
    )
    attended = attended_four.reshape(frames * patches, model_width).astype(jnp.bfloat16)
    branch_first = product(attended, proj_full) + projb_full.astype(jnp.float32)
    middle = token_rows + gate_first * branch_first
    second_value, second_norm_back = jax.vjp(modulate, middle, shift_second, scale_second)
    normed_second = second_value.astype(jnp.bfloat16)
    hidden = product(normed_second, up_full) + upb_full.astype(jnp.float32)
    gelu_value, gelu_back = jax.vjp(gelu_tanh, hidden)
    activated = gelu_value.astype(jnp.bfloat16)
    branch_second = product(activated, down_full) + downb_full.astype(jnp.float32)
    result = middle + gate_second * branch_second
    block_output = result.astype(jnp.bfloat16).reshape(tokens.shape)
    mod_back, qkv_back, proj_back, up_back, down_back = (
        lax.all_gather(mod_weight, ("wide", "narrow"), axis=0, tiled=True),
        lax.all_gather(qkv_weight, ("wide", "narrow"), axis=0, tiled=True),
        lax.all_gather(proj_weight, ("wide", "narrow"), axis=0, tiled=True),
        lax.all_gather(up_weight, ("wide", "narrow"), axis=0, tiled=True),
        lax.all_gather(down_weight, ("wide", "narrow"), axis=0, tiled=True),
    )
    clip_weight = (loss_codes[0].astype(jnp.float32) + 1.0) * 0.25
    cotangent = out_grad[0].reshape(frames * patches, model_width).astype(jnp.float32) * clip_weight
    grad_gate_second = jnp.sum(cotangent * branch_second, axis=0)
    grad_branch_second = (cotangent * gate_second).astype(jnp.bfloat16)
    grad_down = jnp.einsum(
        "rk,rd->kd", activated, grad_branch_second, preferred_element_type=jnp.float32
    )
    grad_down_bias = column_sum(grad_branch_second)
    grad_activated = jnp.einsum(
        "rd,kd->rk", grad_branch_second, down_back, preferred_element_type=jnp.float32
    )
    grad_hidden = gelu_back(grad_activated)[0].astype(jnp.bfloat16)
    grad_up = jnp.einsum(
        "rd,rk->dk", normed_second, grad_hidden, preferred_element_type=jnp.float32
    )
    grad_up_bias = column_sum(grad_hidden)
    grad_normed_second = jnp.einsum(
        "rk,dk->rd", grad_hidden, up_back, preferred_element_type=jnp.float32
    )
    middle_part, grad_shift_second, grad_scale_second = second_norm_back(grad_normed_second)
    grad_middle = cotangent + middle_part
    grad_gate_first = jnp.sum(grad_middle * branch_first, axis=0)
    grad_branch_first = (grad_middle * gate_first).astype(jnp.bfloat16)
    grad_proj = jnp.einsum(
        "re,rd->ed", attended, grad_branch_first, preferred_element_type=jnp.float32
    )
    grad_proj_bias = column_sum(grad_branch_first)
    grad_attended = (
        jnp.einsum("rd,ed->re", grad_branch_first, proj_back, preferred_element_type=jnp.float32)
        .astype(jnp.bfloat16)
        .reshape(shape_four)
    )
    grad_softened = jnp.einsum(
        "fphd,gphd->phfg", grad_attended, values_all, preferred_element_type=jnp.float32
    )
    grad_values = jnp.einsum(
        "phfg,fphd->gphd", softened, grad_attended, preferred_element_type=jnp.float32
    ).astype(jnp.bfloat16)
    grad_scores = softmax_back(grad_softened)[0].astype(jnp.bfloat16)
    grad_queries = (
        jnp.einsum("phfg,gphd->fphd", grad_scores, keys_all, preferred_element_type=jnp.float32)
        * scale_factor
    ).astype(jnp.bfloat16)
    grad_keys = (
        jnp.einsum("phfg,fphd->gphd", grad_scores, queries, preferred_element_type=jnp.float32)
        * scale_factor
    ).astype(jnp.bfloat16)
    flat_shape = (frames * patches, model_width)
    grad_projected = jnp.concatenate(
        [
            grad_queries.reshape(flat_shape),
            grad_keys.reshape(flat_shape),
            grad_values.reshape(flat_shape),
        ],
        axis=1,
    )
    grad_qkv = jnp.einsum("rd,rk->dk", normed, grad_projected, preferred_element_type=jnp.float32)
    grad_qv_bias = jnp.concatenate(
        [column_sum(grad_queries.reshape(flat_shape)), column_sum(grad_values.reshape(flat_shape))]
    )
    grad_normed = jnp.einsum(
        "rk,dk->rd", grad_projected, qkv_back, preferred_element_type=jnp.float32
    )
    token_part, grad_shift_first, grad_scale_first = first_norm_back(grad_normed)
    tokens_grad = (grad_middle + token_part).astype(jnp.bfloat16).reshape(tokens.shape)
    grad_modulation = jnp.concatenate(
        [
            grad_shift_first,
            grad_scale_first,
            grad_gate_first,
            grad_shift_second,
            grad_scale_second,
            grad_gate_second,
        ]
    ).astype(jnp.bfloat16)
    grad_gated = jnp.einsum(
        "ij,j->i", mod_back, grad_modulation, preferred_element_type=jnp.float32
    )
    condition_grad = silu_back(grad_gated)[0][None, :]
    remaining = (
        grad_qkv,
        grad_qv_bias,
        grad_proj,
        grad_proj_bias,
        grad_up,
        grad_up_bias,
        grad_down,
        grad_down_bias,
    )
    grad_mod = jnp.einsum("i,j->ij", gated, grad_modulation, preferred_element_type=jnp.float32)
    grad_mod_bias = grad_modulation.astype(jnp.float32)
    gradients = (grad_mod, grad_mod_bias) + remaining
    owned = lax.psum_scatter(gradients, ("wide", "narrow"), scatter_dimension=0, tiled=True)
    owned_mod = owned[0]
    owned_mod_bias = owned[1]
    rest_owned = owned[2:]
    return (
        block_output,
        tokens_grad,
        condition_grad,
        owned_mod,
        owned_mod_bias,
        rest_owned[0],
        rest_owned[1],
        rest_owned[2],
        rest_owned[3],
        rest_owned[4],
        rest_owned[5],
        rest_owned[6],
        rest_owned[7],
    )


def solution(mesh):
    axes = ("wide", "narrow")
    four, two, one = P(axes, None, None, None), P(axes, None), P(axes)
    in_specs = (four, two, one, one, four, two, one, two, one, two, one, two, one, two, one)
    out_specs = (four, four, two, two, one, two, one, two, one, two, one, two, one)
    body = fast_local if (mesh.shape["wide"], mesh.shape["narrow"]) == (8, 4) else local
    return jax.shard_map(body, mesh=mesh, in_specs=in_specs, out_specs=out_specs, check_vma=False)
```
